32 devices in a mesh: dp: 4 (over x, core), seq: 8 (over z, y).
Axes of the slice: x: 2, y: 2, z: 4, core: 2. Of those that a mesh axis runs over, the one named last changes fastest.
Arguments:
- decoder_in: bfloat16 [2, 32, 512, 768], P(None, ('dp', 'seq')), may hold values from -6 to 6
- memory: bfloat16 [2, 32, 1024, 768], P(None, ('dp', 'seq')), may hold values from -6 to 6
- doc_offsets: int32 [2, 4, 8], P(None, 'dp'), may hold values from 256 to 511, as said below
- self_query: bfloat16 [768, 768], P(('dp', 'seq')), may hold values from -0.0546875 to 0.0546875
- self_key: bfloat16 [768, 768], P(('dp', 'seq')), may hold values from -0.21875 to 0.21875
- self_value: bfloat16 [768, 768], P(('dp', 'seq')), may hold values from -0.21875 to 0.21875
- self_out: bfloat16 [768, 768], P(('dp', 'seq')), may hold values from -0.625 to 0.625
- cross_query: bfloat16 [768, 768], P(('dp', 'seq')), may hold values from -0.0546875 to 0.0546875
- cross_key: bfloat16 [768, 768], P(('dp', 'seq')), may hold values from -0.21875 to 0.21875
- cross_value: bfloat16 [768, 768], P(('dp', 'seq')), may hold values from -0.21875 to 0.21875
- cross_out: bfloat16 [768, 768], P(('dp', 'seq')), may hold values from -0.625 to 0.625
- ffn_gate: bfloat16 [768, 2048], P(('dp', 'seq')), may hold values from -0.21875 to 0.21875
- ffn_up: bfloat16 [768, 2048], P(('dp', 'seq')), may hold values from -0.21875 to 0.21875
- ffn_down: bfloat16 [2048, 768], P(('dp', 'seq')), may hold values from -0.125 to 0.125
- norm_self: bfloat16 [768], P(('dp', 'seq')), may hold values from 0.5 to 1.5
- norm_cross: bfloat16 [768], P(('dp', 'seq')), may hold values from 0.5 to 1.5
- norm_ffn: bfloat16 [768], P(('dp', 'seq')), may hold values from 0.5 to 1.5
- bias_table: bfloat16 [12, 32], replicated, may hold values from -4 to 4
- cotangent: bfloat16 [2, 32, 512, 768], P(None, ('dp', 'seq')), may hold values from -6 to 6
Outputs:
- out_layer: bfloat16 [2, 32, 512, 768], P(None, ('dp', 'seq'))
- grad_decoder: bfloat16 [2, 32, 512, 768], P(None, ('dp', 'seq'))
- grad_memory: bfloat16 [2, 32, 1024, 768], P(None, ('dp', 'seq'))
- grad_self_query: float32 [768, 768], P(('dp', 'seq'))
- grad_self_key: float32 [768, 768], P(('dp', 'seq'))
- grad_self_value: float32 [768, 768], P(('dp', 'seq'))
- grad_self_out: float32 [768, 768], P(('dp', 'seq'))
- grad_cross_query: float32 [768, 768], P(('dp', 'seq'))
- grad_cross_key: float32 [768, 768], P(('dp', 'seq'))
- grad_cross_value: float32 [768, 768], P(('dp', 'seq'))
- grad_cross_out: float32 [768, 768], P(('dp', 'seq'))
- grad_ffn_gate: float32 [768, 2048], P(('dp', 'seq'))
- grad_ffn_up: float32 [768, 2048], P(('dp', 'seq'))
- grad_ffn_down: float32 [2048, 768], P(('dp', 'seq'))
- grad_norm_self: float32 [768], P(('dp', 'seq'))
- grad_norm_cross: float32 [768], P(('dp', 'seq'))
- grad_norm_ffn: float32 [768], P(('dp', 'seq'))
- grad_bias_table: float32 [12, 32], replicated
The draws below stay inside these ranges and needn't reach their ends.
Inputs may be any that keep to these rules, and one draw needn't show every extreme that they name: Within a group the memory row blocks form one stream; the slots of row block s before doc_offsets[m, g, s] belong to the document of target s - 1 (padding for s = 0), the rest to the document of target s.
All inputs are finite; a program needn't handle non-finite values.
Results may differ from the reference program's by a relative error of at most 0.029.
The reference program's roundings to bfloat16 on the way count: a program that leaves them out, or rounds other values in their place, can miss the bound.
Values may be sent and summed in bfloat16 or wider, within the bound.
No kernel may reach another device: no remote copies, remote signals or barrier semaphores. Data moves between devices by JAX's collectives and lax.ppermute only.
A program may use at most 256 MiB of HBM per device.

```python
import math
import jax
import jax.numpy as jnp
from jax import lax

D = 768
HEADS = 12
HEAD_DIM = 64
FF = 2048
BUCKETS = 32
REACH = 128
TGT_LEN = 512
MEM_DEV = 1024
MICRO = 2
GROUPS = 4
SHARDS = 8
TARGETS = 32


def draw_doc_offsets(key, part):
    key = jax.random.fold_in(key, 11)
    total_slots = MICRO * GROUPS * SHARDS
    first_key, second_key, third_key = jax.random.split(key, 3)
    values = jax.random.randint(first_key, (total_slots,), MEM_DEV // 4, MEM_DEV // 2)
    high_at = jax.random.randint(second_key, (), 0, total_slots)
    low_at = (high_at + 1 + jax.random.randint(third_key, (), 0, total_slots - 1)) % total_slots
    values = values.at[high_at].set(MEM_DEV // 2 - 1).at[low_at].set(MEM_DEV // 4)
    return values.reshape(MICRO, GROUPS, SHARDS).astype(jnp.int32)


def raised(entries, rng, source, target, shards_of, factor):
    owner, partner = [(jnp.arange(entries.shape[dim]) // (entries.shape[dim] // shards_of)).reshape([-1 if axis == dim else 1 for axis in range(entries.ndim)]) for dim in (source, target)]
    chosen = jax.random.permutation(rng, shards_of)[partner]
    strong = (owner == chosen) | (owner == (partner + shards_of // 2) % shards_of)
    return jnp.where(strong, factor * entries, entries)


def block_scale(rng, dims, cuts, least, top_value):
    def one(position, shards_of):
        steps = jax.random.uniform(jax.random.fold_in(jax.random.fold_in(rng, 6), position), (shards_of,), jnp.float32, least / len(cuts), top_value / len(cuts))
        return jnp.repeat(jnp.exp(steps), dims[position] // shards_of).reshape((-1,) + (1,) * (len(dims) - position - 1))

    loudness = one(*cuts[0])
    for cut in cuts[1:]:
        loudness = loudness * one(*cut)
    return loudness


def scatter_about(rng, extent, scale, most, shards=(), kind=jnp.bfloat16):
    values = scale * jax.random.normal(rng, extent, jnp.float32)
    if shards:
        values = values * block_scale(rng, extent, shards, -0.22, 0.18)
    return jnp.clip(values, -most, most).astype(kind)


def noise_with(own_key, shape, deviation, bound, cuts, heavy, held_as=jnp.bfloat16):
    drawn = deviation * jax.random.normal(own_key, shape, jnp.float32)
    if cuts:
        drawn = drawn * block_scale(own_key, shape, cuts, -0.22, 0.18)
    return jnp.clip(raised(drawn, jax.random.fold_in(own_key, 3), *heavy), -bound, bound).astype(held_as)


def setup_inputs(seed: int = 0) -> dict:
    splits = jax.random.split(jax.random.key(seed), 20)
    return {
        "decoder_in": noise_with(splits[0], (MICRO, TARGETS, TGT_LEN, D), 1.0, 6.0, ((1, 32),), (1, 3, 32, 2.75)),
        "memory": noise_with(splits[1], (MICRO, TARGETS, MEM_DEV, D), 1.0, 6.0, ((1, 32),), (1, 3, 32, 2.75)),
        "doc_offsets": draw_doc_offsets(jax.random.fold_in(splits[19], 71), 0),
        "self_query": scatter_about(splits[3], (D, D), (16 * D) ** -0.5, 0.0546875, ((0, 32),)),
        "self_key": scatter_about(splits[4], (D, D), D ** -0.5, 0.21875, ((0, 32),)),
        "self_value": scatter_about(splits[5], (D, D), D ** -0.5, 0.21875, ((0, 32),)),
        "self_out": scatter_about(splits[6], (D, D), (D // 8) ** -0.5, 0.625, ((0, 32),)),
        "cross_query": scatter_about(splits[7], (D, D), (16 * D) ** -0.5, 0.0546875, ((0, 32),)),
        "cross_key": scatter_about(splits[8], (D, D), D ** -0.5, 0.21875, ((0, 32),)),
        "cross_value": scatter_about(splits[9], (D, D), D ** -0.5, 0.21875, ((0, 32),)),
        "cross_out": scatter_about(splits[10], (D, D), (D // 8) ** -0.5, 0.625, ((0, 32),)),
        "ffn_gate": scatter_about(splits[11], (D, FF), D ** -0.5, 0.21875, ((0, 32),)),
        "ffn_up": scatter_about(splits[12], (D, FF), D ** -0.5, 0.21875, ((0, 32),)),
        "ffn_down": scatter_about(splits[13], (FF, D), FF ** -0.5, 0.125, ((0, 32),)),
        "norm_self": jnp.clip(1.0 + 0.1 * jax.random.normal(splits[14], (D,), jnp.float32), 0.5, 1.5).astype(jnp.bfloat16),
        "norm_cross": jnp.clip(1.0 + 0.1 * jax.random.normal(splits[15], (D,), jnp.float32), 0.5, 1.5).astype(jnp.bfloat16),
        "norm_ffn": jnp.clip(1.0 + 0.1 * jax.random.normal(splits[16], (D,), jnp.float32), 0.5, 1.5).astype(jnp.bfloat16),
        "bias_table": scatter_about(splits[17], (HEADS, BUCKETS), 1.0, 4.0),
        "cotangent": scatter_about(splits[18], (MICRO, TARGETS, TGT_LEN, D), 1.0, 6.0, ((1, 32),)),
    }


NORM_EPS = 1e-06
MASKED = -1e+30

@jax.custom_vjp
def low(v):
    return lax.optimization_barrier(v.astype(jnp.bfloat16)).astype(jnp.float32)

@jax.custom_vjp
def low_back(v):
    return v

def low_keep(v):
    return (low(v), None)

def low_pass(kept, grad):
    return (grad,)

def back_keep(v):
    return (v, None)

def back_low(kept, grad):
    return (low(grad),)
low.defvjp(low_keep, low_pass)
low_back.defvjp(back_keep, back_low)

def bucket_limits(buckets, reach):
    exact_count = buckets // 2
    limits = []
    for target in range(exact_count + 1, buckets):
        distance = exact_count
        while exact_count + int(math.log(distance / exact_count) / math.log(reach / exact_count) * (buckets - exact_count)) < target:
            distance += 1
        limits.append(distance)
    return limits

def bucket_grid(length, buckets, reach):
    row_ids = lax.broadcasted_iota(jnp.int32, (length, length), 0)
    col_ids = lax.broadcasted_iota(jnp.int32, (length, length), 1)
    distance = jnp.maximum(row_ids - col_ids, 0)
    exact_count = buckets // 2
    far_bucket = jnp.full((length, length), exact_count, jnp.int32)
    for threshold in bucket_limits(buckets, reach):
        far_bucket = far_bucket + (distance >= threshold).astype(jnp.int32)
    return jnp.where(distance < exact_count, distance, far_bucket)

def norm_rows(values, gain):
    inverse = lax.rsqrt(lax.optimization_barrier(jnp.mean(values * values, axis=-1, keepdims=True)) + NORM_EPS)
    return values * inverse * gain

def highest(left, right):
    return jnp.dot(left, right, precision=lax.Precision.HIGHEST, preferred_element_type=jnp.float32)

def rounded_both(values):
    return low_back(low(values))

def attention(queries, keys_in, values_in, bias, valid):
    raw_scores = low_back(jnp.einsum('qhe,khe->hqk', queries, keys_in, precision=lax.Precision.HIGHEST))
    scores = jnp.where(valid, raw_scores + bias, MASKED)
    top_score = lax.optimization_barrier(jnp.max(scores, axis=-1, keepdims=True))
    weights = jnp.exp(scores - top_score)
    probs = weights / lax.optimization_barrier(jnp.sum(weights, axis=-1, keepdims=True))
    mixed = jnp.einsum('hqk,khe->qhe', low(probs), values_in, precision=lax.Precision.HIGHEST)
    return rounded_both(mixed.reshape(mixed.shape[0], D))

def reference(decoder_in, memory, doc_offsets, self_query, self_key, self_value, self_out, cross_query, cross_key, cross_value, cross_out, ffn_gate, ffn_up, ffn_down, norm_self, norm_cross, norm_ffn, bias_table, cotangent):
    quarter_rows = MEM_DEV // 4
    half_rows = MEM_DEV // 2
    key_count = MEM_DEV - quarter_rows + half_rows
    offsets = doc_offsets.astype(jnp.int32)
    next_offsets = jnp.concatenate([offsets[:, :, 1:], jnp.zeros((MICRO, GROUPS, 1), jnp.int32)], axis=2)
    slot_ids = jnp.arange(MEM_DEV, dtype=jnp.int32)
    own_valid = slot_ids[quarter_rows:][None, None, None, :] >= offsets[:, :, :, None]
    next_valid = slot_ids[:half_rows][None, None, None, :] < next_offsets[:, :, :, None]
    key_valid = jnp.concatenate([own_valid, next_valid], axis=3).reshape(MICRO * TARGETS, 1, 1, key_count)
    buckets = bucket_grid(TGT_LEN, BUCKETS, REACH)
    positions = jnp.arange(TGT_LEN, dtype=jnp.int32)
    causal = (positions[:, None] >= positions[None, :])[None]

    def forward(rows_all, memory_all, params):
        w_sq, w_sk, w_sv, w_so, w_cq, w_ck, w_cv, w_co, w_gate, w_up, w_down, gain_self, gain_cross, gain_ffn, table = params
        flat_memory = memory_all.reshape(MICRO * TARGETS * MEM_DEV, D)

        def assemble(projection):
            full = rounded_both(highest(flat_memory, projection)).reshape(MICRO, GROUPS, SHARDS, MEM_DEV, D)
            after = jnp.concatenate([full[:, :, 1:, :half_rows], jnp.zeros((MICRO, GROUPS, 1, half_rows, D), jnp.float32)], axis=2)
            joined = jnp.concatenate([full[:, :, :, quarter_rows:], after], axis=3)
            return joined.reshape(MICRO * TARGETS, key_count, HEADS, HEAD_DIM)
        cross_keys = assemble(w_ck)
        cross_values = assemble(w_cv)
        self_bias = table[:, buckets]

        def one_target(packed):
            rows_in, keys_in, values_in, valid = packed
            input_one = low(norm_rows(rows_in, gain_self))
            query_one = rounded_both(highest(input_one, w_sq)).reshape(TGT_LEN, HEADS, HEAD_DIM)
            key_one = rounded_both(highest(input_one, w_sk)).reshape(TGT_LEN, HEADS, HEAD_DIM)
            value_one = rounded_both(highest(input_one, w_sv)).reshape(TGT_LEN, HEADS, HEAD_DIM)
            attn_one = attention(query_one, key_one, value_one, self_bias, causal)
            after_self = rows_in + low_back(highest(attn_one, w_so))
            input_two = low(norm_rows(after_self, gain_cross))
            query_two = rounded_both(highest(input_two, w_cq)).reshape(TGT_LEN, HEADS, HEAD_DIM)
            attn_two = attention(query_two, keys_in, values_in, 0.0, valid)
            after_cross = after_self + low_back(highest(attn_two, w_co))
            input_three = low(norm_rows(after_cross, gain_ffn))
            gate_pre = low_back(highest(input_three, w_gate))
            up_pre = low_back(highest(input_three, w_up))
            hidden = low(jax.nn.gelu(gate_pre, approximate=True) * up_pre)
            return after_cross + low_back(highest(hidden, w_down))
        outputs = lax.map(jax.checkpoint(one_target), (rows_all.reshape(MICRO * TARGETS, TGT_LEN, D), cross_keys, cross_values, key_valid))
        return outputs.reshape(MICRO, TARGETS, TGT_LEN, D)
    params = tuple((weight.astype(jnp.float32) for weight in (self_query, self_key, self_value, self_out, cross_query, cross_key, cross_value, cross_out, ffn_gate, ffn_up, ffn_down, norm_self, norm_cross, norm_ffn, bias_table)))
    result, pullback = jax.vjp(forward, decoder_in.astype(jnp.float32), memory.astype(jnp.float32), params)
    grad_rows, grad_mem, grad_params = pullback(cotangent.astype(jnp.float32))
    g_self_query, g_self_key, g_self_value, g_self_out, g_cross_query, g_cross_key, g_cross_value, g_cross_out, g_ffn_gate, g_ffn_up, g_ffn_down, g_norm_self, g_norm_cross, g_norm_ffn, g_table = grad_params
    return (result.astype(jnp.bfloat16), grad_rows.astype(jnp.bfloat16), grad_mem.astype(jnp.bfloat16), g_self_query, g_self_key, g_self_value, g_self_out, g_cross_query, g_cross_key, g_cross_value, g_cross_out, g_ffn_gate, g_ffn_up, g_ffn_down, g_norm_self, g_norm_cross, g_norm_ffn, g_table)
```

```python
import math

import jax
import jax.numpy as jnp
from jax import lax
from jax.experimental import pallas as pl
from jax.experimental.pallas import tpu as pltpu
from jax.sharding import PartitionSpec as P

D = 768
HEADS = 12
HEAD_DIM = 64
BUCKETS = 32
REACH = 128
TGT_LEN = 512
MEM_DEV = 1024
MICRO = 2
PAIRS = HEADS // 2
LANES = 2 * HEAD_DIM
OWN = MEM_DEV - MEM_DEV // 4
NEXT = MEM_DEV // 2
KEYS = OWN + NEXT
HALF = 256
MASKED = -1e30
NORM_EPS = 1e-06
AXES = ("dp", "seq")
BF = jnp.bfloat16
F32 = jnp.float32


def nn(a, b):
    return lax.dot_general(a, b, (((1,), (0,)), ((), ())), preferred_element_type=F32)


def bucket_limits(buckets, reach):
    exact_count = buckets // 2
    limits = []
    for target in range(exact_count + 1, buckets):
        distance = exact_count
        while (
            exact_count
            + int(
                math.log(distance / exact_count)
                / math.log(reach / exact_count)
                * (buckets - exact_count)
            )
            < target
        ):
            distance += 1
        limits.append(distance)
    return limits


def three_parts(row):
    high = row.astype(BF).astype(F32)
    rest = row - high
    middle = rest.astype(BF).astype(F32)
    return high, middle, rest - middle


def extra_rows(columns, first, parts):
    row_id = lax.broadcasted_iota(jnp.int32, (LANES, columns), 0)
    grid = jnp.where(row_id == 0, first, 0.0)
    for place, part in enumerate(parts):
        grid = jnp.where(row_id == place + 1, part, grid)
    return grid.astype(BF)


def head_rows(stacked, head):
    row_id = lax.broadcasted_iota(jnp.int32, stacked.shape, 0)
    return jnp.where((row_id // HEAD_DIM) == head, stacked, jnp.zeros_like(stacked))


def bias_tiles_kernel(table_ref, tiles_ref):
    head = pl.program_id(0)
    key_id = lax.broadcasted_iota(jnp.int32, (HALF, HALF), 0)
    query_id = lax.broadcasted_iota(jnp.int32, (HALF, HALF), 1)
    limits = bucket_limits(BUCKETS, REACH)
    exact_count = BUCKETS // 2
    for tile in range(2):
        distance = query_id - key_id + tile * HALF
        grid = jnp.full((HALF, HALF), table_ref[head, 0], F32)
        for bucket in range(1, BUCKETS):
            start = bucket if bucket <= exact_count else limits[bucket - exact_count - 1]
            grid = jnp.where(distance >= start, table_ref[head, bucket], grid)
        if tile == 0:
            grid = jnp.where(distance >= 0, grid, MASKED)
        tiles_ref[0, tile] = grid


def bias_tiles(table):
    return pl.pallas_call(
        bias_tiles_kernel,
        grid=(HEADS,),
        in_specs=[pl.BlockSpec(memory_space=pltpu.SMEM)],
        out_specs=pl.BlockSpec((1, 2, HALF, HALF), lambda h: (h, 0, 0, 0)),
        out_shape=jax.ShapeDtypeStruct((HEADS, 2, HALF, HALF), F32),
        name="bias_tiles",
    )(table)


def softmax_columns(scores):
    top = jnp.max(scores, axis=0, keepdims=True)
    weights = jnp.exp(scores - top)
    total = jnp.sum(weights, axis=0, keepdims=True)
    return weights.astype(BF), 1.0 / total, top + jnp.log(total)


def put_lse(lse_ref, rows):
    row_id = lax.broadcasted_iota(jnp.int32, (8, TGT_LEN), 0)
    lse_ref[0] = jnp.where(row_id == 0, rows[0], rows[1])


def cross_forward_kernel(q_ref, ko_ref, kn_ref, vo_ref, vn_ref, mask_ref, o_ref, lse_ref, k_ext):
    k_ext[:OWN, :LANES] = ko_ref[MEM_DEV - OWN :, :]
    k_ext[OWN:, :LANES] = kn_ref[...]
    k_ext[:, LANES:] = mask_ref[0]
    q_t = q_ref[...].T
    v_t = jnp.concatenate([vo_ref[MEM_DEV - OWN :, :], vn_ref[...]], axis=0).T
    ones = extra_rows(TGT_LEN, 1.0, ())
    mixed, lses = [], []
    for head in range(2):
        query = jnp.concatenate([head_rows(q_t, head), ones], axis=0)
        scores = nn(k_ext[...], query)
        weights, inverse, lse = softmax_columns(scores)
        mixed.append(nn(v_t[head * HEAD_DIM : (head + 1) * HEAD_DIM], weights) * inverse)
        lses.append(lse)
    o_ref[...] = jnp.concatenate(mixed, axis=0).T.astype(BF)
    put_lse(lse_ref, lses)


def cross_backward_kernel(
    q_ref, ko_ref, kn_ref, vo_ref, vn_ref, mask_ref, o_ref, do_ref, lse_ref,
    dq_ref, own_ref, next_ref, k_ext, v_ext,
):
    k_ext[:OWN, :LANES] = ko_ref[MEM_DEV - OWN :, :]
    k_ext[OWN:, :LANES] = kn_ref[...]
    k_ext[:, LANES:] = mask_ref[0]
    v_ext[:OWN, :LANES] = vo_ref[MEM_DEV - OWN :, :]
    v_ext[OWN:, :LANES] = vn_ref[...]
    v_ext[:, LANES:] = jnp.ones((KEYS, LANES), BF)
    k_t = k_ext[:, :LANES].T
    q = q_ref[...]
    d_o = do_ref[...]
    q_t = q.T
    do_t = d_o.T
    centre_t = (o_ref[...].astype(F32) * d_o.astype(F32)).T
    dq, dk, dv = [], [], []
    for head in range(2):
        rows = slice(head * HEAD_DIM, (head + 1) * HEAD_DIM)
        lse = lse_ref[0, head : head + 1, :]
        centre = jnp.sum(centre_t[rows], axis=0, keepdims=True)
        query = jnp.concatenate(
            [head_rows(q_t, head), extra_rows(TGT_LEN, 1.0, three_parts(-lse))], axis=0
        )
        grad = jnp.concatenate(
            [head_rows(do_t, head), extra_rows(TGT_LEN, 0.0, three_parts(-centre))], axis=0
        )
        probs = jnp.exp(nn(k_ext[...], query))
        grad_scores = (probs * nn(v_ext[...], grad)).astype(BF)
        dv.append(nn(probs.astype(BF), d_o))
        dk.append(nn(grad_scores, q))
        dq.append(nn(k_t[rows], grad_scores))
    dq_ref[...] = jnp.concatenate(dq, axis=0).T.astype(BF)
    lane = lax.broadcasted_iota(jnp.int32, (KEYS, LANES), 1)
    dk_pair = jnp.where(lane < HEAD_DIM, dk[0], dk[1]).astype(BF)
    dv_pair = jnp.where(lane < HEAD_DIM, dv[0], dv[1]).astype(BF)
    front = jnp.zeros((MEM_DEV - OWN, LANES), BF)
    for place, pair in enumerate((dk_pair, dv_pair)):
        own_ref[place, : MEM_DEV - OWN, :] = front
        own_ref[place, MEM_DEV - OWN :, :] = pair[:OWN]
        next_ref[place] = pair[OWN:]


def self_forward_kernel(q_ref, k_ref, v_ref, tiles_ref, o_ref, lse_ref):
    k = k_ref[...]
    q_t = q_ref[...].T
    v_t = v_ref[...].T
    mixed, lses = [], []
    for head in range(2):
        query = head_rows(q_t, head)
        value = v_t[head * HEAD_DIM : (head + 1) * HEAD_DIM]
        near, far = tiles_ref[head, 0], tiles_ref[head, 1]
        w0, i0, l0 = softmax_columns(nn(k[:HALF], query[:, :HALF]) + near)
        raw = nn(k, query[:, HALF:])
        w1, i1, l1 = softmax_columns(
            jnp.concatenate([raw[:HALF] + far, raw[HALF:] + near], axis=0)
        )
        out0 = nn(value[:, :HALF], w0) * i0
        out1 = nn(value, w1) * i1
        mixed.append(jnp.concatenate([out0, out1], axis=1))
        lses.append(jnp.concatenate([l0, l1], axis=1))
    o_ref[...] = jnp.concatenate(mixed, axis=0).T.astype(BF)
    put_lse(lse_ref, lses)


def self_backward_kernel(
    q_ref, k_ref, v_ref, tiles_ref, o_ref, do_ref, lse_ref,
    dq_ref, dk_ref, dv_ref, near_ref, far_ref, k_ext, v_ext,
):
    row_ext = jnp.ones((TGT_LEN, LANES), BF)
    k_ext[:, :LANES] = k_ref[...]
    k_ext[:, LANES:] = row_ext
    v_ext[:, :LANES] = v_ref[...]
    v_ext[:, LANES:] = row_ext
    k_t = k_ref[...].T
    q = q_ref[...]
    d_o = do_ref[...]
    q_t = q.T
    do_t = d_o.T
    centre_t = (o_ref[...].astype(F32) * d_o.astype(F32)).T
    first = pl.program_id(1) == 0
    dq, dk, dv = [], [], []
    for head in range(2):
        rows = slice(head * HEAD_DIM, (head + 1) * HEAD_DIM)
        lse = lse_ref[0, head : head + 1, :]
        centre = jnp.sum(centre_t[rows], axis=0, keepdims=True)
        query = jnp.concatenate(
            [head_rows(q_t, head), extra_rows(TGT_LEN, 0.0, three_parts(-lse))], axis=0
        )
        grad = jnp.concatenate(
            [head_rows(do_t, head), extra_rows(TGT_LEN, 0.0, three_parts(-centre))], axis=0
        )
        near, far = tiles_ref[head, 0], tiles_ref[head, 1]
        raw0 = nn(k_ext[:HALF, :], query[:, :HALF])
        raw1 = nn(k_ext[...], query[:, HALF:])
        p00 = jnp.exp(raw0 + near)
        p10 = jnp.exp(raw1[:HALF] + far)
        p11 = jnp.exp(raw1[HALF:] + near)
        g0 = nn(v_ext[:HALF, :], grad[:, :HALF])
        g1 = nn(v_ext[...], grad[:, HALF:])
        s00 = p00 * g0
        s10 = p10 * g1[:HALF]
        s11 = p11 * g1[HALF:]
        near_sum, far_sum = s00 + s11, s10

        @pl.when(first)
        def _():
            near_ref[head] = near_sum
            far_ref[head] = far_sum

        @pl.when(jnp.logical_not(first))
        def _():
            near_ref[head] += near_sum
            far_ref[head] += far_sum

        b00, b10, b11 = s00.astype(BF), s10.astype(BF), s11.astype(BF)
        w00, w10, w11 = p00.astype(BF), p10.astype(BF), p11.astype(BF)
        top = jnp.concatenate([w00, w10], axis=1)
        dv.append(jnp.concatenate([nn(top, d_o), nn(w11, d_o[HALF:])], axis=0))
        top = jnp.concatenate([b00, b10], axis=1)
        dk.append(jnp.concatenate([nn(top, q), nn(b11, q[HALF:])], axis=0))
        dq.append(
            jnp.concatenate(
                [
                    nn(k_t[rows, :HALF], b00),
                    nn(k_t[rows], jnp.concatenate([b10, b11], axis=0)),
                ],
                axis=1,
            )
        )
    dq_ref[...] = jnp.concatenate(dq, axis=0).T.astype(BF)
    lane = lax.broadcasted_iota(jnp.int32, (TGT_LEN, LANES), 1)
    dk_ref[...] = jnp.where(lane < HEAD_DIM, dk[0], dk[1]).astype(BF)
    dv_ref[...] = jnp.where(lane < HEAD_DIM, dv[0], dv[1]).astype(BF)


PAIR_GRID = (MICRO, PAIRS)
VMEM_LIMIT = 56 * 1024 * 1024


def params():
    return pltpu.CompilerParams(vmem_limit_bytes=VMEM_LIMIT)


def pair_block(rows, offset=0):
    return pl.BlockSpec((rows, LANES), lambda m, p: (m, p + offset))


LSE_BLOCK = pl.BlockSpec((1, 8, TGT_LEN), lambda m, p: (m * PAIRS + p, 0, 0))
LSE_SHAPE = jax.ShapeDtypeStruct((MICRO * PAIRS, 8, TGT_LEN), F32)
MASK_BLOCK = pl.BlockSpec((1, KEYS, LANES), lambda m, p: (m, 0, 0))
ROWS = MICRO * TGT_LEN


def cross_forward(q, kv_own, kv_next, mask):
    return pl.pallas_call(
        cross_forward_kernel,
        grid=PAIR_GRID,
        in_specs=[
            pair_block(TGT_LEN),
            pair_block(MEM_DEV),
            pair_block(NEXT),
            pair_block(MEM_DEV, PAIRS),
            pair_block(NEXT, PAIRS),
            MASK_BLOCK,
        ],
        out_specs=[pair_block(TGT_LEN), LSE_BLOCK],
        out_shape=[jax.ShapeDtypeStruct((ROWS, D), BF), LSE_SHAPE],
        scratch_shapes=[pltpu.VMEM((KEYS, 2 * LANES), BF)],
        compiler_params=params(),
        name="cross_forward",
    )(q, kv_own, kv_next, kv_own, kv_next, mask)


def cross_backward(q, kv_own, kv_next, mask, o, d_o, lse):
    return pl.pallas_call(
        cross_backward_kernel,
        grid=PAIR_GRID,
        in_specs=[
            pair_block(TGT_LEN),
            pair_block(MEM_DEV),
            pair_block(NEXT),
            pair_block(MEM_DEV, PAIRS),
            pair_block(NEXT, PAIRS),
            MASK_BLOCK,
            pair_block(TGT_LEN),
            pair_block(TGT_LEN),
            LSE_BLOCK,
        ],
        out_specs=[
            pair_block(TGT_LEN),
            pl.BlockSpec((2, MEM_DEV, LANES), lambda m, p: (0, m, p)),
            pl.BlockSpec((2, NEXT, LANES), lambda m, p: (0, m, p)),
        ],
        out_shape=[
            jax.ShapeDtypeStruct((ROWS, D), BF),
            jax.ShapeDtypeStruct((2, MICRO * MEM_DEV, D), BF),
            jax.ShapeDtypeStruct((2, MICRO * NEXT, D), BF),
        ],
        scratch_shapes=[pltpu.VMEM((KEYS, 2 * LANES), BF)] * 2,
        compiler_params=params(),
        name="cross_backward",
    )(q, kv_own, kv_next, kv_own, kv_next, mask, o, d_o, lse)


def swapped(spec):
    index = spec.index_map
    return pl.BlockSpec(spec.block_shape, lambda p, m: index(m, p))


TILE_BLOCK = pl.BlockSpec((2, 2, HALF, HALF), lambda p, m: (p, 0, 0, 0))


def self_forward(qkv, tiles):
    return pl.pallas_call(
        self_forward_kernel,
        grid=(PAIRS, MICRO),
        in_specs=[
            swapped(pair_block(TGT_LEN)),
            swapped(pair_block(TGT_LEN, PAIRS)),
            swapped(pair_block(TGT_LEN, 2 * PAIRS)),
            TILE_BLOCK,
        ],
        out_specs=[swapped(pair_block(TGT_LEN)), swapped(LSE_BLOCK)],
        out_shape=[jax.ShapeDtypeStruct((ROWS, D), BF), LSE_SHAPE],
        compiler_params=params(),
        name="self_forward",
    )(qkv, qkv, qkv, tiles)


def self_backward(qkv, tiles, o, d_o, lse):
    rows = jax.ShapeDtypeStruct((ROWS, D), BF)
    sums = jax.ShapeDtypeStruct((HEADS, HALF, HALF), F32)
    sum_block = pl.BlockSpec((2, HALF, HALF), lambda p, m: (p, 0, 0))
    return pl.pallas_call(
        self_backward_kernel,
        grid=(PAIRS, MICRO),
        in_specs=[
            swapped(pair_block(TGT_LEN)),
            swapped(pair_block(TGT_LEN, PAIRS)),
            swapped(pair_block(TGT_LEN, 2 * PAIRS)),
            TILE_BLOCK,
            swapped(pair_block(TGT_LEN)),
            swapped(pair_block(TGT_LEN)),
            swapped(LSE_BLOCK),
        ],
        out_specs=[swapped(pair_block(TGT_LEN))] * 3 + [sum_block] * 2,
        out_shape=[rows, rows, rows, sums, sums],
        scratch_shapes=[pltpu.VMEM((TGT_LEN, 2 * LANES), BF)] * 2,
        compiler_params=params(),
        name="self_backward",
    )(qkv, qkv, qkv, tiles, o, d_o, lse)


def distance_sums_kernel(near_ref, far_ref, sums_ref):
    near, far = near_ref[0], far_ref[0]
    key_id = lax.broadcasted_iota(jnp.int32, (HALF, HALF), 0)
    query_id = lax.broadcasted_iota(jnp.int32, (HALF, HALF), 1)
    close = (query_id - key_id + HALF) < REACH
    both = near + jnp.where(close, far, 0.0)
    group = both[:8]
    for first in range(8, HALF, 8):
        group = group + pltpu.roll(both[first : first + 8], HALF - first, 1)
    row_id = lax.broadcasted_iota(jnp.int32, (8, HALF), 0)
    turned = group
    for row in range(1, 8):
        turned = jnp.where(row_id == row, pltpu.roll(group, HALF - row, 1), turned)
    by_distance = jnp.sum(turned, axis=0, keepdims=True)
    rest = jnp.sum(jnp.where(close, 0.0, far), axis=0, keepdims=True)
    sums_ref[0] = jnp.where(row_id == 0, by_distance, jnp.where(row_id == 1, rest, 0.0))


def distance_sums(near, far):
    block = pl.BlockSpec((1, HALF, HALF), lambda h: (h, 0, 0))
    return pl.pallas_call(
        distance_sums_kernel,
        grid=(HEADS,),
        in_specs=[block, block],
        out_specs=pl.BlockSpec((1, 8, HALF), lambda h: (h, 0, 0)),
        out_shape=jax.ShapeDtypeStruct((HEADS, 8, HALF), F32),
        name="distance_sums",
    )(near, far)


def table_grad(near, far):
    sums = distance_sums(near, far)
    limits = bucket_limits(BUCKETS, REACH)
    starts = list(range(BUCKETS // 2 + 1)) + limits + [HALF]
    columns = [
        jnp.sum(sums[:, 0, starts[b] : starts[b + 1]], axis=1) for b in range(BUCKETS - 1)
    ]
    columns.append(jnp.sum(sums[:, 0, starts[BUCKETS - 1] :], axis=1) + jnp.sum(sums[:, 1], axis=1))
    return jnp.stack(columns, axis=1)


def key_masks(offsets_row, position):
    shard_ids = jnp.arange(offsets_row.shape[0], dtype=jnp.int32)
    own_start = jnp.sum(jnp.where(shard_ids == position, offsets_row, 0))
    next_start = jnp.sum(jnp.where(shard_ids == position + 1, offsets_row, 0))
    own_valid = jnp.arange(MEM_DEV - OWN, MEM_DEV, dtype=jnp.int32) >= own_start
    next_valid = jnp.arange(NEXT, dtype=jnp.int32) < next_start
    valid = jnp.concatenate([own_valid, next_valid])[:, None]
    lane = jnp.arange(LANES, dtype=jnp.int32)[None, :]
    return jnp.where((lane == 0), jnp.where(valid, 0.0, MASKED), 1.0).astype(BF)


def passed_along(block, distance):
    devices = range(lax.axis_size("seq"))
    route = [(i - distance, i) for i in devices if i - distance in devices]
    return lax.ppermute(block, "seq", route)


def device_bits():
    bits = []
    for axis in AXES:
        count = lax.axis_size(axis).bit_length() - 1
        bits += [(axis, place) for place in reversed(range(count))]
    return bits


def exchange(block, axis, place):
    route = [(i, i ^ (1 << place)) for i in range(lax.axis_size(axis))]
    return lax.ppermute(block, axis, route)


def reduce_rows(partial, order):
    bits = device_bits()
    share = partial.shape[0] >> len(bits)
    held = partial.reshape((2,) * len(bits) + (share, partial.shape[1]))
    left = list(bits)
    for step, bit in enumerate(order):
        axis, place = bit
        dim = left.index(bit)
        left.remove(bit)
        mine = (lax.axis_index(axis) >> place) & 1
        given = lax.dynamic_index_in_dim(held, 1 - mine, dim, keepdims=False)
        kept = lax.dynamic_index_in_dim(held, mine, dim, keepdims=False)
        total = kept.astype(F32) + exchange(given, axis, place).astype(F32)
        held = total if step == len(order) - 1 else total.astype(BF)
    return held


def reduce_orders():
    bits = device_bits()
    core = ("dp", 0)
    across = [bit for bit in bits if bit[0] == "dp" and bit != core]
    along = [bit for bit in bits if bit[0] == "seq" and bit[1] == 0]
    rest = [bit for bit in bits if bit[0] == "seq" and bit[1] > 0]
    return [core] + across + along + rest, [core] + along + across + rest


def reduced(partial):
    first, second = reduce_orders()
    cut = partial.shape[1] // 256 * 128
    return jnp.concatenate(
        [reduce_rows(partial[:, :cut], first), reduce_rows(partial[:, cut:], second)], axis=1
    )


def all_sum(values):
    for axis, place in device_bits():
        values = values + exchange(values, axis, place)
    return values


def project(rows, weight):
    return jnp.dot(rows, weight, preferred_element_type=F32)


def project_back(grads, weight):
    return jnp.einsum("lo,io->li", grads, weight, preferred_element_type=F32)


def weight_grad(rows, grads):
    return jnp.einsum("li,lo->io", rows, grads, preferred_element_type=F32).astype(BF)


def norm_rows(values, gain):
    inverse = lax.rsqrt(jnp.mean(values * values, axis=-1, keepdims=True) + NORM_EPS)
    return (values * inverse * gain).astype(BF), inverse


def norm_back(values, inverse, gain, grads):
    scaled = values * inverse
    gain_grad = jnp.sum(scaled * grads, axis=0)
    weighted = grads * gain
    centre = jnp.mean(scaled * weighted, axis=-1, keepdims=True)
    return inverse * (weighted - scaled * centre), gain_grad


def local(
    decoder_in,
    memory,
    doc_offsets,
    self_query,
    self_key,
    self_value,
    self_out,
    cross_query,
    cross_key,
    cross_value,
    cross_out,
    ffn_gate,
    ffn_up,
    ffn_down,
    norm_self,
    norm_cross,
    norm_ffn,
    bias_table,
    cotangent,
):
    position = lax.axis_index("seq")
    gains = jnp.stack([norm_self, norm_cross, norm_ffn], axis=1)
    gains = jnp.pad(gains, ((0, 0), (0, LANES - 3)))
    early = jnp.concatenate(
        [self_query, self_key, self_value, cross_key, cross_value, gains], axis=1
    )
    late = jnp.concatenate([self_out, cross_query, cross_out, ffn_gate, ffn_up], axis=1)
    early = lax.all_gather(early, AXES, axis=0, tiled=True)
    late = lax.all_gather(late, AXES, axis=0, tiled=True)
    w_down = lax.all_gather(ffn_down, AXES, axis=0, tiled=True)
    w_qkv, w_kv = early[:, : 3 * D], early[:, 3 * D : 5 * D]
    gain_self, gain_cross, gain_ffn = early[:, 5 * D : 5 * D + 3].T.astype(F32)
    w_so, w_cq, w_co = (late[:, i * D : (i + 1) * D] for i in range(3))
    ff = ffn_gate.shape[1]
    w_gate, w_up = late[:, 3 * D : 3 * D + ff], late[:, 3 * D + ff :]

    tiles = bias_tiles(bias_table.astype(F32))
    mask = jnp.stack([key_masks(doc_offsets[m, 0], position) for m in range(MICRO)])
    x = decoder_in.reshape(ROWS, D).astype(F32)
    mem = memory.reshape(MICRO * MEM_DEV, D)
    kv_own = project(mem, w_kv).astype(BF)
    kv_next = passed_along(kv_own.reshape(MICRO, MEM_DEV, 2 * D)[:, :NEXT], -1)
    kv_next = kv_next.reshape(MICRO * NEXT, 2 * D)
    h1, r1 = norm_rows(x, gain_self)
    qkv = project(h1, w_qkv).astype(BF)
    o1, lse1 = self_forward(qkv, tiles)
    x1 = x + project(o1, w_so)
    h2, r2 = norm_rows(x1, gain_cross)
    q2 = project(h2, w_cq).astype(BF)
    o2, lse2 = cross_forward(q2, kv_own, kv_next, mask)
    x2 = x1 + project(o2, w_co)
    h3, r3 = norm_rows(x2, gain_ffn)
    gate = project(h3, w_gate)
    up = project(h3, w_up)
    hidden, gated_back = jax.vjp(
        lambda g, u: jax.nn.gelu(g, approximate=True) * u, gate, up
    )
    hidden = hidden.astype(BF)
    out = (x2 + project(hidden, w_down)).astype(BF)

    dy_low = cotangent.reshape(ROWS, D)
    dy = dy_low.astype(F32)
    d_gate, d_up = gated_back(project_back(dy_low, w_down))
    d_gate, d_up = d_gate.astype(BF), d_up.astype(BF)
    g_down = reduced(weight_grad(hidden, dy_low))
    g_gate_up = reduced(
        jnp.concatenate([weight_grad(h3, d_gate), weight_grad(h3, d_up)], axis=1)
    )
    dh3 = project_back(d_gate, w_gate) + project_back(d_up, w_up)
    dx2, g_norm_ffn = norm_back(x2, r3, gain_ffn, dh3)
    dx2 = dy + dx2
    db2 = dx2.astype(BF)
    do2 = project_back(db2, w_co).astype(BF)
    dq2, dkv_own, dkv_next = cross_backward(q2, kv_own, kv_next, mask, o2, do2, lse2)
    dkv_prev = passed_along(dkv_next, 1).reshape(2, MICRO, NEXT, D)
    dkv = dkv_own.reshape(2, MICRO, MEM_DEV, D)
    dkv = jnp.concatenate(
        [
            (dkv[:, :, :NEXT].astype(F32) + dkv_prev.astype(F32)).astype(BF),
            dkv[:, :, NEXT:],
        ],
        axis=2,
    ).reshape(2, MICRO * MEM_DEV, D)
    grad_memory = project_back(dkv[0], w_kv[:, :D]) + project_back(dkv[1], w_kv[:, D:])
    dx1, g_norm_cross = norm_back(x1, r2, gain_cross, project_back(dq2, w_cq))
    dx1 = dx2 + dx1
    db1 = dx1.astype(BF)
    do1 = project_back(db1, w_so).astype(BF)
    g_cross = reduced(
        jnp.concatenate(
            [
                weight_grad(h2, dq2),
                weight_grad(mem, dkv[0]),
                weight_grad(mem, dkv[1]),
                weight_grad(o2, db2),
            ],
            axis=1,
        )
    )
    dq1, dk1, dv1, near, far = self_backward(qkv, tiles, o1, do1, lse1)
    dh1 = (
        project_back(dq1, w_qkv[:, :D])
        + project_back(dk1, w_qkv[:, D : 2 * D])
        + project_back(dv1, w_qkv[:, 2 * D :])
    )
    dx0, g_norm_self = norm_back(x, r1, gain_self, dh1)
    grad_decoder = (dx1 + dx0).astype(BF)
    g_norms = jnp.stack([g_norm_self, g_norm_cross, g_norm_ffn], axis=1).astype(BF)
    g_self = reduced(
        jnp.concatenate(
            [
                weight_grad(h1, dq1),
                weight_grad(h1, dk1),
                weight_grad(h1, dv1),
                weight_grad(o1, db1),
                jnp.pad(g_norms, ((0, 0), (0, LANES - 3))),
            ],
            axis=1,
        )
    )
    g_table = all_sum(table_grad(near, far))

    def cut(stack, index, width=D):
        return stack[:, index * width : (index + 1) * width]

    return (
        out.reshape(decoder_in.shape),
        grad_decoder.reshape(decoder_in.shape),
        grad_memory.astype(BF).reshape(memory.shape),
        cut(g_self, 0),
        cut(g_self, 1),
        cut(g_self, 2),
        cut(g_self, 3),
        cut(g_cross, 0),
        cut(g_cross, 1),
        cut(g_cross, 2),
        cut(g_cross, 3),
        cut(g_gate_up, 0, ff),
        cut(g_gate_up, 1, ff),
        g_down,
        g_self[:, 4 * D],
        g_self[:, 4 * D + 1],
        g_self[:, 4 * D + 2],
        g_table,
    )


def solution(mesh):
    in_specs = (
        P(None, ("dp", "seq"), None, None),
        P(None, ("dp", "seq"), None, None),
        P(None, "dp", None),
        P(("dp", "seq"), None),
        P(("dp", "seq"), None),
        P(("dp", "seq"), None),
        P(("dp", "seq"), None),
        P(("dp", "seq"), None),
        P(("dp", "seq"), None),
        P(("dp", "seq"), None),
        P(("dp", "seq"), None),
        P(("dp", "seq"), None),
        P(("dp", "seq"), None),
        P(("dp", "seq"), None),
        P(("dp", "seq")),
        P(("dp", "seq")),
        P(("dp", "seq")),
        P(),
        P(None, ("dp", "seq"), None, None),
    )
    out_specs = (
        P(None, ("dp", "seq"), None, None),
        P(None, ("dp", "seq"), None, None),
        P(None, ("dp", "seq"), None, None),
        P(("dp", "seq"), None),
        P(("dp", "seq"), None),
        P(("dp", "seq"), None),
        P(("dp", "seq"), None),
        P(("dp", "seq"), None),
        P(("dp", "seq"), None),
        P(("dp", "seq"), None),
        P(("dp", "seq"), None),
        P(("dp", "seq"), None),
        P(("dp", "seq"), None),
        P(("dp", "seq"), None),
        P(("dp", "seq")),
        P(("dp", "seq")),
        P(("dp", "seq")),
        P(),
    )
    return jax.shard_map(local, mesh=mesh, in_specs=in_specs, out_specs=out_specs, check_vma=False)
```

```python
import functools
import math

import jax
import jax.numpy as jnp
from jax import lax
from jax.experimental import pallas as pl
from jax.experimental.pallas import tpu as pltpu
from jax.sharding import PartitionSpec as P

D = 768
HEADS = 12
HEAD_DIM = 64
BUCKETS = 32
REACH = 128
TGT_LEN = 512
MEM_DEV = 1024
MICRO = 2
PAIRS = HEADS // 2
LANES = 2 * HEAD_DIM
OWN = MEM_DEV - MEM_DEV // 4
NEXT = MEM_DEV // 2
KEYS = OWN + NEXT
HALF = 256
MASKED = -1e30
NORM_EPS = 1e-06
AXES = ("dp", "seq")
ROWS = MICRO * TGT_LEN
BLOCK = 256
WIDE = 256
HALF_COLUMNS = 2048
VMEM_LIMIT = 60 * 1024 * 1024
BF = jnp.bfloat16
F32 = jnp.float32


def nn(a, b):
    return lax.dot_general(a, b, (((1,), (0,)), ((), ())), preferred_element_type=F32)


def bucket_limits(buckets, reach):
    exact_count = buckets // 2
    limits = []
    for target in range(exact_count + 1, buckets):
        distance = exact_count
        while (
            exact_count
            + int(
                math.log(distance / exact_count)
                / math.log(reach / exact_count)
                * (buckets - exact_count)
            )
            < target
        ):
            distance += 1
        limits.append(distance)
    return limits


def three_parts(row):
    high = row.astype(BF).astype(F32)
    rest = row - high
    middle = rest.astype(BF).astype(F32)
    return high, middle, rest - middle


def extra_rows(columns, first, parts):
    row_id = lax.broadcasted_iota(jnp.int32, (LANES, columns), 0)
    grid = jnp.where(row_id == 0, first, 0.0)
    for place, part in enumerate(parts):
        grid = jnp.where(row_id == place + 1, part, grid)
    return grid.astype(BF)


def head_rows(stacked, head):
    row_id = lax.broadcasted_iota(jnp.int32, stacked.shape, 0)
    return jnp.where((row_id // HEAD_DIM) == head, stacked, jnp.zeros_like(stacked))


def nt(a, b):
    return lax.dot_general(a, b, (((1,), (1,)), ((), ())), preferred_element_type=F32)


def params(**options):
    return pltpu.CompilerParams(vmem_limit_bytes=VMEM_LIMIT, **options)


def cost(us):
    return pl.CostEstimate(flops=int(us), bytes_accessed=0, transcendentals=0)


def shape(rows, columns, kind=BF):
    return jax.ShapeDtypeStruct((rows, columns), kind)


def row_block(columns, rows=BLOCK):
    return pl.BlockSpec((rows, columns), lambda i: (i, 0))


def fixed_block(rows, columns):
    return pl.BlockSpec((rows, columns), lambda i: (0, 0))


ANY = pl.BlockSpec(memory_space=pl.ANY)
SMEM = pl.BlockSpec(memory_space=pltpu.SMEM)


def halves_loaded(core_ref, own_ref, other_ref, pieces, sems):
    @pl.when(pl.program_id(0) == 0)
    def _():
        for side in range(2):

            @pl.when(core_ref[0] == side)
            def _():
                halves = (own_ref, other_ref) if side == 0 else (other_ref, own_ref)
                copies = [
                    pltpu.make_async_copy(halves[half].at[:, source], target, sems.at[place])
                    for place, (half, source, target) in enumerate(pieces)
                ]
                for copy in copies:
                    copy.start()
                for copy in copies:
                    copy.wait()


def key_value_pieces(w_kv):
    return [(0, slice(0, 2 * D), w_kv)]


def out_query_pieces(weights):
    return [(side, slice(0, D), weights.at[:, side * D : (side + 1) * D]) for side in range(2)]


def query_pieces(w_qkv):
    cut = HALF_COLUMNS - 2 * D
    return [
        (0, slice(2 * D, HALF_COLUMNS), w_qkv.at[:, :cut]),
        (1, slice(0, 3 * D - cut), w_qkv.at[:, cut:]),
    ]


def normed(values, gain):
    inverse = lax.rsqrt(jnp.mean(values * values, axis=-1, keepdims=True) + NORM_EPS)
    scaled = values * inverse
    return scaled, inverse, (scaled * gain).astype(BF)


def norm_back(values, gain, grads, gain_grad_ref):
    inverse = lax.rsqrt(jnp.mean(values * values, axis=-1, keepdims=True) + NORM_EPS)
    scaled = values * inverse
    add_rows(gain_grad_ref, jnp.sum(scaled * grads, axis=0, keepdims=True))
    weighted = grads * gain
    centre = jnp.mean(scaled * weighted, axis=-1, keepdims=True)
    return inverse * (weighted - scaled * centre)


def add_rows(total_ref, row):
    row_id = lax.broadcasted_iota(jnp.int32, (8, D), 0)
    addend = jnp.where(row_id == 0, row, 0.0)

    @pl.when(pl.program_id(0) == 0)
    def _():
        total_ref[...] = addend

    @pl.when(pl.program_id(0) > 0)
    def _():
        total_ref[...] += addend


def key_value_kernel(core_ref, own_ref, other_ref, rows_ref, kv_ref, w_kv, sems):
    halves_loaded(core_ref, own_ref, other_ref, key_value_pieces(w_kv), sems)
    kv_ref[...] = nn(rows_ref[...], w_kv[...]).astype(BF)


def key_value(core, own, other, rows, steps, index, us):
    return pl.pallas_call(
        key_value_kernel,
        grid=(steps,),
        in_specs=[SMEM, ANY, ANY, pl.BlockSpec((BLOCK, D), index)],
        out_specs=row_block(2 * D),
        out_shape=shape(steps * BLOCK, 2 * D),
        scratch_shapes=[pltpu.VMEM((D, 2 * D), BF), pltpu.SemaphoreType.DMA((1,))],
        compiler_params=params(),
        cost_estimate=cost(us),
        name="key_value",
    )(core, own, other, rows)


def self_inputs_kernel(
    core_ref, own_ref, other_ref, x_ref, h_ref, qkv_ref, gains_ref, w_qkv, gain_columns, sems
):
    first_gain = 5 * D - HALF_COLUMNS
    pieces = query_pieces(w_qkv)
    pieces.append((1, slice(first_gain, first_gain + LANES), gain_columns))
    halves_loaded(core_ref, own_ref, other_ref, pieces, sems)

    @pl.when(pl.program_id(0) == 0)
    def _():
        gains_ref[...] = gain_columns[...].astype(F32).T[:8]

    h_ref[...] = normed(x_ref[...].astype(F32), gains_ref[:1, :])[2]
    qkv_ref[...] = nn(h_ref[...], w_qkv[...]).astype(BF)


def self_inputs(core, own, other, x):
    return pl.pallas_call(
        self_inputs_kernel,
        grid=(ROWS // BLOCK,),
        in_specs=[SMEM, ANY, ANY, row_block(D)],
        out_specs=[row_block(D), row_block(3 * D), fixed_block(8, D)],
        out_shape=[shape(ROWS, D), shape(ROWS, 3 * D), shape(8, D, F32)],
        scratch_shapes=[
            pltpu.VMEM((D, 3 * D), BF),
            pltpu.VMEM((D, LANES), BF),
            pltpu.SemaphoreType.DMA((3,)),
        ],
        compiler_params=params(),
        cost_estimate=cost(6),
        name="self_inputs",
    )(core, own, other, x)


def cross_inputs_kernel(
    core_ref, own_ref, other_ref, gain_ref, x_ref, o_ref, x1_ref, h_ref, q_ref, weights, sems
):
    halves_loaded(core_ref, own_ref, other_ref, out_query_pieces(weights), sems)
    x1 = x_ref[...].astype(F32) + nn(o_ref[...], weights[:, :D])
    x1_ref[...] = x1
    h_ref[...] = normed(x1, gain_ref[1:2, :])[2]
    q_ref[...] = nn(h_ref[...], weights[:, D:]).astype(BF)


def cross_inputs(core, own, other, gain, x, o1):
    return pl.pallas_call(
        cross_inputs_kernel,
        grid=(ROWS // BLOCK,),
        in_specs=[SMEM, ANY, ANY, fixed_block(8, D), row_block(D), row_block(D)],
        out_specs=[row_block(D)] * 3,
        out_shape=[shape(ROWS, D, F32), shape(ROWS, D), shape(ROWS, D)],
        scratch_shapes=[pltpu.VMEM((D, 2 * D), BF), pltpu.SemaphoreType.DMA((2,))],
        compiler_params=params(),
        cost_estimate=cost(5),
        name="cross_inputs",
    )(core, own, other, gain, x, o1)


def ffn_kernel(
    core_ref, late_ref, own_ref, other_ref, gain_ref, x1_ref, o_ref, dy_ref,
    out_ref, h_ref, hidden_ref, dgate_ref, dup_ref, db_ref, dx_ref, do_ref, gain_grad_ref,
    w_out, w_gate, w_up, w_down, sems, down_sems,
):
    width = w_gate.shape[1]
    copies = [
        pltpu.make_async_copy(late_ref.at[:, :D], w_out, sems.at[0]),
        pltpu.make_async_copy(late_ref.at[:, D : D + width], w_gate, sems.at[1]),
        pltpu.make_async_copy(late_ref.at[:, D + width :], w_up, sems.at[2]),
    ]
    first = pl.program_id(0) == 0

    @pl.when(first)
    def _():
        for copy in copies:
            copy.start()

    pieces = [(side, slice(None), w_down.at[:, side * D // 2 : (side + 1) * D // 2]) for side in range(2)]
    halves_loaded(core_ref, own_ref, other_ref, pieces, down_sems)

    def arrived(place):
        @pl.when(first)
        def _():
            copies[place].wait()

    arrived(0)
    x2 = x1_ref[...] + nn(o_ref[...], w_out[...])
    h_ref[...] = normed(x2, gain_ref[2:3, :])[2]
    dy_low = dy_ref[...]
    arrived(1)
    gate = nn(h_ref[...], w_gate[...])
    arrived(2)
    up = nn(h_ref[...], w_up[...])
    d_hidden = nt(dy_low, w_down[...])
    scale = math.sqrt(2.0 / math.pi)
    square = gate * gate
    turn = jnp.tanh(scale * gate * (1.0 + 0.044715 * square))
    half = 0.5 * (1.0 + turn)
    gelu = gate * half
    slope = half + 0.5 * gate * (1.0 - turn * turn) * (scale * (1.0 + 3 * 0.044715 * square))
    hidden_ref[...] = (gelu * up).astype(BF)
    dgate_ref[...] = (d_hidden * up * slope).astype(BF)
    dup_ref[...] = (d_hidden * gelu).astype(BF)
    out_ref[...] = (x2 + nn(hidden_ref[...], w_down[...])).astype(BF)
    dh = nt(dgate_ref[...], w_gate[...]) + nt(dup_ref[...], w_up[...])
    dx = dy_low.astype(F32) + norm_back(x2, gain_ref[2:3, :], dh, gain_grad_ref)
    dx_ref[...] = dx
    db_ref[...] = dx.astype(BF)
    do_ref[...] = nt(db_ref[...], w_out[...]).astype(BF)


def ffn(core, late, own, other, gain, x1, o2, dy):
    width = own.shape[0]
    return pl.pallas_call(
        ffn_kernel,
        grid=(ROWS // BLOCK,),
        in_specs=[SMEM, ANY, ANY, ANY, fixed_block(8, D), row_block(D), row_block(D), row_block(D)],
        out_specs=[
            row_block(D),
            row_block(D),
            row_block(width),
            row_block(width),
            row_block(width),
            row_block(D),
            row_block(D),
            row_block(D),
            fixed_block(8, D),
        ],
        out_shape=[
            shape(ROWS, D),
            shape(ROWS, D),
            shape(ROWS, width),
            shape(ROWS, width),
            shape(ROWS, width),
            shape(ROWS, D),
            shape(ROWS, D, F32),
            shape(ROWS, D),
            shape(8, D, F32),
        ],
        scratch_shapes=[
            pltpu.VMEM((D, D), BF),
            pltpu.VMEM((D, width), BF),
            pltpu.VMEM((D, width), BF),
            pltpu.VMEM((width, D), BF),
            pltpu.SemaphoreType.DMA((3,)),
            pltpu.SemaphoreType.DMA((2,)),
        ],
        compiler_params=params(),
        cost_estimate=cost(30),
        name="ffn",
    )(core, late, own, other, gain, x1, o2, dy)


def self_grads_kernel(
    core_ref, own_ref, other_ref, gain_ref, x1_ref, dx2_ref, dq0_ref, dq1_ref,
    dx1_ref, db_ref, do_ref, gain_grad_ref, weights, sems,
):
    halves_loaded(core_ref, own_ref, other_ref, out_query_pieces(weights), sems)
    low = pl.program_id(0) < TGT_LEN // BLOCK
    dh = nt(jnp.where(low, dq0_ref[...], dq1_ref[...]), weights[:, D:])
    dx1 = dx2_ref[...] + norm_back(x1_ref[...], gain_ref[1:2, :], dh, gain_grad_ref)
    dx1_ref[...] = dx1
    db_ref[...] = dx1.astype(BF)
    do_ref[...] = nt(db_ref[...], weights[:, :D]).astype(BF)


def self_grads(core, own, other, gain, x1, dx2, dq2):
    half = TGT_LEN // BLOCK
    return pl.pallas_call(
        self_grads_kernel,
        grid=(ROWS // BLOCK,),
        in_specs=[
            SMEM,
            ANY,
            ANY,
            fixed_block(8, D),
            row_block(D),
            row_block(D),
            pl.BlockSpec((BLOCK, D), lambda i: (jnp.minimum(i, half - 1), 0)),
            pl.BlockSpec((BLOCK, D), lambda i: (jnp.maximum(i - half, 0), 0)),
        ],
        out_specs=[row_block(D), row_block(D), row_block(D), fixed_block(8, D)],
        out_shape=[shape(ROWS, D, F32), shape(ROWS, D), shape(ROWS, D), shape(8, D, F32)],
        scratch_shapes=[pltpu.VMEM((D, 2 * D), BF), pltpu.SemaphoreType.DMA((2,))],
        compiler_params=params(),
        cost_estimate=cost(5),
        name="self_grads",
    )(core, own, other, gain, x1, dx2, *dq2)


def input_grads_kernel(
    core_ref, own_ref, other_ref, gain_ref, x_ref, dx1_ref, dqkv_ref,
    dx_ref, gain_grad_ref, w_qkv, sems,
):
    halves_loaded(core_ref, own_ref, other_ref, query_pieces(w_qkv), sems)
    dh = (
        nt(dqkv_ref[0], w_qkv[:, :D])
        + nt(dqkv_ref[1], w_qkv[:, D : 2 * D])
        + nt(dqkv_ref[2], w_qkv[:, 2 * D :])
    )
    x = x_ref[...].astype(F32)
    dx_ref[...] = (dx1_ref[...] + norm_back(x, gain_ref[:1, :], dh, gain_grad_ref)).astype(BF)


def input_grads(core, own, other, gain, x, dx1, dqkv):
    return pl.pallas_call(
        input_grads_kernel,
        grid=(ROWS // BLOCK,),
        in_specs=[
            SMEM, ANY, ANY, fixed_block(8, D), row_block(D), row_block(D),
            pl.BlockSpec((3, BLOCK, D), lambda i: (0, i, 0)),
        ],
        out_specs=[row_block(D), fixed_block(8, D)],
        out_shape=[shape(ROWS, D), shape(8, D, F32)],
        scratch_shapes=[pltpu.VMEM((D, 3 * D), BF), pltpu.SemaphoreType.DMA((2,))],
        compiler_params=params(),
        cost_estimate=cost(6),
        name="input_grads",
    )(core, own, other, gain, x, dx1, dqkv)


def memory_grads_kernel(core_ref, own_ref, other_ref, dkv_ref, dm_ref, w_kv, sems):
    halves_loaded(core_ref, own_ref, other_ref, key_value_pieces(w_kv), sems)
    dm_ref[...] = (nt(dkv_ref[0], w_kv[:, :D]) + nt(dkv_ref[1], w_kv[:, D:])).astype(BF)


def memory_grads(core, own, other, dkv):
    rows = dkv.shape[1]
    return pl.pallas_call(
        memory_grads_kernel,
        grid=(rows // BLOCK,),
        in_specs=[SMEM, ANY, ANY, pl.BlockSpec((2, BLOCK, D), lambda i: (0, i, 0))],
        out_specs=row_block(D),
        out_shape=shape(rows, D),
        scratch_shapes=[pltpu.VMEM((D, 2 * D), BF), pltpu.SemaphoreType.DMA((1,))],
        compiler_params=params(),
        cost_estimate=cost(rows / 400),
        name="memory_grads",
    )(core, own, other, dkv)


def stored_by_core(core_ref, grad, give_ref, keep_ref):
    across, _, count = give_ref.shape[0], 2, give_ref.shape[1]
    for side in range(2):

        @pl.when(core_ref[0] == side)
        def _():
            for place in range(across):
                first = place * 2 * count
                here, there = first + side * count, first + (1 - side) * count
                keep_ref[place] = grad[here : here + count].astype(BF)
                give_ref[place] = grad[there : there + count].astype(BF)


def row_grads_kernel(core_ref, rows_ref, grads_ref, give_ref, keep_ref, turned):
    @pl.when(pl.program_id(0) == 0)
    def _():
        turned[...] = rows_ref[...].T

    stored_by_core(core_ref, nn(turned[...], grads_ref[0]), give_ref, keep_ref)


def row_grads(core, rows, grads, across, us):
    units, length = grads.shape[0], grads.shape[1]
    count = D // (2 * across)
    block = pl.BlockSpec((across, count, D), lambda u: (0, 0, u))
    piece = jax.ShapeDtypeStruct((across, count, units * D), BF)
    return pl.pallas_call(
        row_grads_kernel,
        grid=(units,),
        in_specs=[SMEM, fixed_block(length, D), pl.BlockSpec((1, length, D), lambda u: (u, 0, 0))],
        out_specs=[block, block],
        out_shape=[piece, piece],
        scratch_shapes=[pltpu.VMEM((D, length), BF)],
        compiler_params=params(),
        cost_estimate=cost(us),
        name="row_grads",
    )(core, rows, grads)


def pair_grads_kernel(counts, core_ref, *refs):
    give_ref, keep_ref = refs[-2:]
    used = 0
    for place, count in enumerate(counts):
        turned = refs[used][...].T
        length = turned.shape[1] // count
        grad = sum(
            nn(turned[:, part * length : (part + 1) * length], refs[used + 1 + part][...])
            for part in range(count)
        )
        used += 1 + count
        columns = slice(place * D, (place + 1) * D)
        stored_by_core(core_ref, grad, give_ref.at[:, :, columns], keep_ref.at[:, :, columns])


def pair_grads(core, pairs, across):
    count = D // (2 * across)
    piece = jax.ShapeDtypeStruct((across, count, len(pairs) * D), BF)
    whole = pl.BlockSpec(memory_space=pltpu.VMEM)
    flat = [array for rows, grads in pairs for array in (rows,) + tuple(grads)]
    return pl.pallas_call(
        functools.partial(pair_grads_kernel, [len(grads) for _, grads in pairs]),
        in_specs=[SMEM] + [whole] * len(flat),
        out_specs=[whole, whole],
        out_shape=[piece, piece],
        compiler_params=params(),
        cost_estimate=cost(2.5 * len(pairs)),
        name="pair_grads",
    )(core, *flat)


def ffn_weight_grads_kernel(h_ref, hidden_ref, dgate_ref, dup_ref, dy_ref, out_ref):
    unit = pl.program_id(0)
    devices = out_ref.shape[0]
    width = dgate_ref.shape[1]

    def from_columns(grads_ref):
        turned = h_ref[...].T
        share = D // devices
        for first in range(0, width, 2 * WIDE):
            both = [
                nn(turned, grads_ref[:, place : place + WIDE]).reshape(devices, share, WIDE)
                for place in (first, first + WIDE)
            ]
            row = first // WIDE * share
            out_ref[:, row : row + 2 * share, :] = jnp.concatenate(both, axis=1).astype(BF)

    @pl.when(unit == 0)
    def _():
        from_columns(dgate_ref)

    @pl.when(unit == 1)
    def _():
        from_columns(dup_ref)

    @pl.when(unit == 2)
    def _():
        turned = hidden_ref[...].T
        share = width // devices
        for place in range(D // WIDE):
            grad = nn(turned, dy_ref[:, place * WIDE : (place + 1) * WIDE])
            out_ref[:, place * share : (place + 1) * share, :] = grad.reshape(
                devices, share, WIDE
            ).astype(BF)


def ffn_weight_grads(h3, hidden, d_gate, d_up, dy, devices):
    width = hidden.shape[1]
    rows = D * width // WIDE // devices
    return pl.pallas_call(
        ffn_weight_grads_kernel,
        grid=(3,),
        in_specs=[
            fixed_block(ROWS, D),
            fixed_block(ROWS, width),
            fixed_block(ROWS, width),
            fixed_block(ROWS, width),
            fixed_block(ROWS, D),
        ],
        out_specs=pl.BlockSpec((devices, rows, WIDE), lambda u: (0, u, 0)),
        out_shape=jax.ShapeDtypeStruct((devices, 3 * rows, WIDE), BF),
        compiler_params=params(),
        cost_estimate=cost(13),
        name="ffn_weight_grads",
    )(h3, hidden, d_gate, d_up, dy)


def memory_weight_grads_kernel(
    core_ref, mem_ref, next_ref, own0_ref, own1_ref, after0_ref, after1_ref,
    give_ref, keep_ref, turned,
):
    @pl.when(pl.program_id(0) == 0)
    def _():
        for m in range(MICRO):
            turned[:, m * OWN : (m + 1) * OWN] = mem_ref[m, 0, MEM_DEV - OWN :, :].T
        turned[:, MICRO * OWN :] = next_ref[...].T

    grad, used = 0.0, 0
    for part_ref in (own0_ref, own1_ref, after0_ref, after1_ref):
        length = part_ref.shape[1]
        grad = grad + nn(turned[:, used : used + length], part_ref[0])
        used += length
    stored_by_core(core_ref, grad, give_ref, keep_ref)


def memory_weight_grads(core, memory, next_rows, dkv_own, dkv_next, across):
    count = D // (2 * across)
    block = pl.BlockSpec((across, count, D), lambda u: (0, 0, u))
    piece = jax.ShapeDtypeStruct((across, count, 2 * D), BF)
    return pl.pallas_call(
        memory_weight_grads_kernel,
        grid=(2,),
        in_specs=[
            SMEM,
            pl.BlockSpec((MICRO, 1, MEM_DEV, D), lambda u: (0, 0, 0, 0)),
            fixed_block(MICRO * NEXT, D),
        ]
        + [pl.BlockSpec((1, OWN, D), lambda u: (u, 0, 0))] * MICRO
        + [pl.BlockSpec((1, NEXT, D), lambda u: (u, 0, 0))] * MICRO,
        out_specs=[block, block],
        out_shape=[piece, piece],
        scratch_shapes=[pltpu.VMEM((D, MICRO * (OWN + NEXT)), BF)],
        compiler_params=params(),
        cost_estimate=cost(8),
        name="memory_weight_grads",
    )(core, memory, next_rows, *dkv_own, *dkv_next)


def memory_total_kernel(
    core_ref, own_ref, other_ref, dkv0_ref, dkv1_ref, prev0_ref, prev1_ref, dm_ref, w_kv, sems
):
    halves_loaded(core_ref, own_ref, other_ref, key_value_pieces(w_kv), sems)
    low = pl.program_id(0) < 4
    block = pl.program_id(0) % 4
    prev = jnp.where(low, prev0_ref[...], prev1_ref[...])

    @pl.when(block == 0)
    def _():
        dm_ref[...] = prev

    @pl.when(block > 0)
    def _():
        dk, dv = (jnp.where(low, dkv0_ref[place], dkv1_ref[place]) for place in range(2))
        shared = jnp.where(block == 1, prev.astype(F32), 0.0)
        dm_ref[...] = (nt(dk, w_kv[:, :D]) + nt(dv, w_kv[:, D:]) + shared).astype(BF)


def memory_total(core, own, other, dkv, prev):
    def spot(i, m):
        return jnp.clip(i - 4 * m, 0, 3)

    def dkv_block(m):
        return pl.BlockSpec((2, BLOCK, D), lambda i: (0, jnp.maximum(spot(i, m) - 1, 0), 0))

    def prev_block(m):
        return pl.BlockSpec((BLOCK, D), lambda i: (jnp.minimum(spot(i, m), 1), 0))

    return pl.pallas_call(
        memory_total_kernel,
        grid=(MICRO * 4,),
        in_specs=[SMEM, ANY, ANY]
        + [dkv_block(m) for m in range(MICRO)]
        + [prev_block(m) for m in range(MICRO)],
        out_specs=row_block(D),
        out_shape=shape(MICRO * MEM_DEV, D),
        scratch_shapes=[pltpu.VMEM((D, 2 * D), BF), pltpu.SemaphoreType.DMA((1,))],
        compiler_params=params(),
        cost_estimate=cost(7),
        name="memory_total",
    )(core, own, other, *dkv, *prev)


def extras_kernel(share, core_ref, sums_ref, first_ref, second_ref, third_ref, give_ref, keep_ref):
    row_id = lax.broadcasted_iota(jnp.int32, (8, D), 0)
    norms = jnp.zeros((8, D), F32)
    for place, ref in enumerate((first_ref, second_ref, third_ref)):
        norms = jnp.where(row_id == place, ref[:1, :], norms)
    stacked = jnp.concatenate([norms, jnp.zeros((LANES - 8, D), F32)], axis=0).T
    distance = lax.broadcasted_iota(jnp.int32, (HALF, LANES), 0)
    bucket_id = lax.broadcasted_iota(jnp.int32, (HALF, LANES), 1)
    exact_count = BUCKETS // 2
    bucket = jnp.full((HALF, LANES), exact_count, jnp.int32)
    for threshold in bucket_limits(BUCKETS, REACH):
        bucket = bucket + (distance >= threshold).astype(jnp.int32)
    bucket = jnp.where(distance < exact_count, distance, bucket)
    sums = sums_ref[...]
    together = LANES // BUCKETS
    lines = [jnp.zeros((1, LANES), F32) for _ in range(HEADS // together)]
    for part in range(together):
        near_hot = (bucket == bucket_id - part * BUCKETS).astype(F32)
        far_hot = (bucket_id == (part + 1) * BUCKETS - 1).astype(F32)
        table = sum(
            lax.dot_general(
                sums[:, place, :], hot, (((1,), (0,)), ((), ())),
                precision=lax.Precision.HIGHEST, preferred_element_type=F32,
            )
            for place, hot in ((0, near_hot), (1, far_hot))
        )
        for line in range(len(lines)):
            head = line * together + part
            lines[line] = lines[line] + table[head : head + 1]
    row_in_share = lax.broadcasted_iota(jnp.int32, (D, LANES), 0) % share
    tall = jnp.zeros((D, LANES), F32)
    for line, row in enumerate(lines):
        tall = jnp.where(row_in_share == line, row, tall)
    both = jnp.concatenate([stacked, tall], axis=1)
    stored_by_core(core_ref, both, give_ref, keep_ref)


def extras(core, sums, norms, across, share):
    piece = jax.ShapeDtypeStruct((across, D // (2 * across), 2 * LANES), BF)
    whole = pl.BlockSpec(memory_space=pltpu.VMEM)
    return pl.pallas_call(
        functools.partial(extras_kernel, share),
        in_specs=[SMEM] + [whole] * 4,
        out_specs=[whole, whole],
        out_shape=[piece, piece],
        compiler_params=params(),
        cost_estimate=cost(2),
        name="extras",
    )(core, sums, *norms)


def bias_tiles_kernel(table_ref, tiles_ref):
    head = pl.program_id(0)
    key_id = lax.broadcasted_iota(jnp.int32, (HALF, HALF), 0)
    query_id = lax.broadcasted_iota(jnp.int32, (HALF, HALF), 1)
    limits = bucket_limits(BUCKETS, REACH)
    exact_count = BUCKETS // 2
    for tile in range(2):
        distance = query_id - key_id + tile * HALF
        grid = jnp.full((HALF, HALF), table_ref[head, 0], F32)
        for bucket in range(1, BUCKETS):
            start = bucket if bucket <= exact_count else limits[bucket - exact_count - 1]
            grid = jnp.where(distance >= start, table_ref[head, bucket], grid)
        if tile == 0:
            grid = jnp.where(distance >= 0, grid, MASKED)
        tiles_ref[0, tile] = grid


def bias_tiles(table):
    return pl.pallas_call(
        bias_tiles_kernel,
        grid=(HEADS,),
        in_specs=[pl.BlockSpec(memory_space=pltpu.SMEM)],
        out_specs=pl.BlockSpec((1, 2, HALF, HALF), lambda h: (h, 0, 0, 0)),
        out_shape=jax.ShapeDtypeStruct((HEADS, 2, HALF, HALF), F32),
        cost_estimate=cost(8),
        name="bias_tiles",
    )(table)


def softmax_columns(scores):
    top = jnp.max(scores, axis=0, keepdims=True)
    weights = jnp.exp(scores - top)
    total = jnp.sum(weights, axis=0, keepdims=True)
    return weights.astype(BF), 1.0 / total, top + jnp.log(total)


def put_lse(lse_ref, rows):
    row_id = lax.broadcasted_iota(jnp.int32, (8, TGT_LEN), 0)
    lse_ref[0] = jnp.where(row_id == 0, rows[0], rows[1])


def cross_forward_kernel(q_ref, ko_ref, kn_ref, vo_ref, vn_ref, mask_ref, o_ref, lse_ref, k_ext):
    k_ext[:OWN, :LANES] = ko_ref[...]
    k_ext[OWN:, :LANES] = kn_ref[...]
    k_ext[:, LANES:] = mask_ref[0]
    q_t = q_ref[...].T
    v_t = jnp.concatenate([vo_ref[...], vn_ref[...]], axis=0).T
    ones = extra_rows(TGT_LEN, 1.0, ())
    mixed, lses = [], []
    for head in range(2):
        query = jnp.concatenate([head_rows(q_t, head), ones], axis=0)
        scores = nn(k_ext[...], query)
        weights, inverse, lse = softmax_columns(scores)
        mixed.append(nn(v_t[head * HEAD_DIM : (head + 1) * HEAD_DIM], weights) * inverse)
        lses.append(lse)
    o_ref[...] = jnp.concatenate(mixed, axis=0).T.astype(BF)
    put_lse(lse_ref, lses)


def cross_backward_kernel(
    q_ref, ko_ref, kn_ref, vo_ref, vn_ref, mask_ref, o_ref, do_ref, lse_ref,
    dq_ref, own_ref, next_ref, k_ext, v_ext,
):
    k_ext[:OWN, :LANES] = ko_ref[...]
    k_ext[OWN:, :LANES] = kn_ref[...]
    k_ext[:, LANES:] = mask_ref[0]
    v_ext[:OWN, :LANES] = vo_ref[...]
    v_ext[OWN:, :LANES] = vn_ref[...]
    v_ext[:, LANES:] = jnp.ones((KEYS, LANES), BF)
    k_t = k_ext[:, :LANES].T
    q = q_ref[...]
    d_o = do_ref[...]
    q_t = q.T
    do_t = d_o.T
    centre_t = (o_ref[...].astype(F32) * d_o.astype(F32)).T
    dq, dk, dv = [], [], []
    for head in range(2):
        rows = slice(head * HEAD_DIM, (head + 1) * HEAD_DIM)
        lse = lse_ref[0, head : head + 1, :]
        centre = jnp.sum(centre_t[rows], axis=0, keepdims=True)
        query = jnp.concatenate(
            [head_rows(q_t, head), extra_rows(TGT_LEN, 1.0, three_parts(-lse))], axis=0
        )
        grad = jnp.concatenate(
            [head_rows(do_t, head), extra_rows(TGT_LEN, 0.0, three_parts(-centre))], axis=0
        )
        probs = jnp.exp(nn(k_ext[...], query))
        grad_scores = (probs * nn(v_ext[...], grad)).astype(BF)
        dv.append(nn(probs.astype(BF), d_o))
        dk.append(nn(grad_scores, q))
        dq.append(nn(k_t[rows], grad_scores))
    dq_ref[...] = jnp.concatenate(dq, axis=0).T.astype(BF)
    lane = lax.broadcasted_iota(jnp.int32, (KEYS, LANES), 1)
    dk_pair = jnp.where(lane < HEAD_DIM, dk[0], dk[1]).astype(BF)
    dv_pair = jnp.where(lane < HEAD_DIM, dv[0], dv[1]).astype(BF)
    for place, pair in enumerate((dk_pair, dv_pair)):
        own_ref[place] = pair[:OWN]
        next_ref[place] = pair[OWN:]


def self_forward_kernel(q_ref, k_ref, v_ref, tiles_ref, o_ref, lse_ref):
    k = k_ref[...]
    q_t = q_ref[...].T
    v_t = v_ref[...].T
    mixed, lses = [], []
    for head in range(2):
        query = head_rows(q_t, head)
        value = v_t[head * HEAD_DIM : (head + 1) * HEAD_DIM]
        near, far = tiles_ref[head, 0], tiles_ref[head, 1]
        w0, i0, l0 = softmax_columns(nn(k[:HALF], query[:, :HALF]) + near)
        raw = nn(k, query[:, HALF:])
        w1, i1, l1 = softmax_columns(
            jnp.concatenate([raw[:HALF] + far, raw[HALF:] + near], axis=0)
        )
        out0 = nn(value[:, :HALF], w0) * i0
        out1 = nn(value, w1) * i1
        mixed.append(jnp.concatenate([out0, out1], axis=1))
        lses.append(jnp.concatenate([l0, l1], axis=1))
    o_ref[...] = jnp.concatenate(mixed, axis=0).T.astype(BF)
    put_lse(lse_ref, lses)


def distance_sums(near, far):
    key_id = lax.broadcasted_iota(jnp.int32, (HALF, HALF), 0)
    query_id = lax.broadcasted_iota(jnp.int32, (HALF, HALF), 1)
    close = (query_id - key_id + HALF) < REACH
    both = near + jnp.where(close, far, 0.0)
    group = both[:8]
    for first in range(8, HALF, 8):
        group = group + pltpu.roll(both[first : first + 8], HALF - first, 1)
    row_id = lax.broadcasted_iota(jnp.int32, (8, HALF), 0)
    turned = group
    for row in range(1, 8):
        turned = jnp.where(row_id == row, pltpu.roll(group, HALF - row, 1), turned)
    by_distance = jnp.sum(turned, axis=0, keepdims=True)
    rest = jnp.sum(jnp.where(close, 0.0, far), axis=0, keepdims=True)
    return jnp.where(row_id == 0, by_distance, jnp.where(row_id == 1, rest, 0.0))


def self_backward_kernel(
    q_ref, k_ref, v_ref, tiles_ref, o_ref, do_ref, lse_ref,
    dqkv_ref, sums_ref, k_ext, v_ext, near_ref, far_ref,
):
    row_ext = jnp.ones((TGT_LEN, LANES), BF)
    k_ext[:, :LANES] = k_ref[...]
    k_ext[:, LANES:] = row_ext
    v_ext[:, :LANES] = v_ref[...]
    v_ext[:, LANES:] = row_ext
    k_t = k_ref[...].T
    q = q_ref[...]
    d_o = do_ref[...]
    q_t = q.T
    do_t = d_o.T
    centre_t = (o_ref[...].astype(F32) * d_o.astype(F32)).T
    first = pl.program_id(1) == 0
    dq, dk, dv = [], [], []
    for head in range(2):
        rows = slice(head * HEAD_DIM, (head + 1) * HEAD_DIM)
        lse = lse_ref[0, head : head + 1, :]
        centre = jnp.sum(centre_t[rows], axis=0, keepdims=True)
        query = jnp.concatenate(
            [head_rows(q_t, head), extra_rows(TGT_LEN, 0.0, three_parts(-lse))], axis=0
        )
        grad = jnp.concatenate(
            [head_rows(do_t, head), extra_rows(TGT_LEN, 0.0, three_parts(-centre))], axis=0
        )
        near, far = tiles_ref[head, 0], tiles_ref[head, 1]
        raw0 = nn(k_ext[:HALF, :], query[:, :HALF])
        raw1 = nn(k_ext[...], query[:, HALF:])
        p00 = jnp.exp(raw0 + near)
        p10 = jnp.exp(raw1[:HALF] + far)
        p11 = jnp.exp(raw1[HALF:] + near)
        g0 = nn(v_ext[:HALF, :], grad[:, :HALF])
        g1 = nn(v_ext[...], grad[:, HALF:])
        s00 = p00 * g0
        s10 = p10 * g1[:HALF]
        s11 = p11 * g1[HALF:]
        near_sum, far_sum = s00 + s11, s10

        @pl.when(first)
        def _():
            near_ref[head] = near_sum
            far_ref[head] = far_sum

        @pl.when(jnp.logical_not(first))
        def _():
            sums_ref[head] = distance_sums(near_ref[head] + near_sum, far_ref[head] + far_sum)

        b00, b10, b11 = s00.astype(BF), s10.astype(BF), s11.astype(BF)
        w00, w10, w11 = p00.astype(BF), p10.astype(BF), p11.astype(BF)
        top = jnp.concatenate([w00, w10], axis=1)
        dv.append(jnp.concatenate([nn(top, d_o), nn(w11, d_o[HALF:])], axis=0))
        top = jnp.concatenate([b00, b10], axis=1)
        dk.append(jnp.concatenate([nn(top, q), nn(b11, q[HALF:])], axis=0))
        dq.append(
            jnp.concatenate(
                [
                    nn(k_t[rows, :HALF], b00),
                    nn(k_t[rows], jnp.concatenate([b10, b11], axis=0)),
                ],
                axis=1,
            )
        )
    dqkv_ref[0] = jnp.concatenate(dq, axis=0).T.astype(BF)
    lane = lax.broadcasted_iota(jnp.int32, (TGT_LEN, LANES), 1)
    dqkv_ref[1] = jnp.where(lane < HEAD_DIM, dk[0], dk[1]).astype(BF)
    dqkv_ref[2] = jnp.where(lane < HEAD_DIM, dv[0], dv[1]).astype(BF)


PAIR_GRID = (MICRO, PAIRS)


def pair_block(rows, offset=0):
    return pl.BlockSpec((rows, LANES), lambda m, p: (m, p + offset))


LSE_BLOCK = pl.BlockSpec((1, 8, TGT_LEN), lambda m, p: (m * PAIRS + p, 0, 0))
LSE_SHAPE = jax.ShapeDtypeStruct((MICRO * PAIRS, 8, TGT_LEN), F32)
MASK_BLOCK = pl.BlockSpec((1, KEYS, LANES), lambda m, p: (m, 0, 0))


def cross_forward(q, kv_own, kv_next, mask):
    return pl.pallas_call(
        cross_forward_kernel,
        grid=PAIR_GRID,
        in_specs=[
            pair_block(TGT_LEN),
            pair_block(OWN),
            pair_block(NEXT),
            pair_block(OWN, PAIRS),
            pair_block(NEXT, PAIRS),
            MASK_BLOCK,
        ],
        out_specs=[pair_block(TGT_LEN), LSE_BLOCK],
        out_shape=[jax.ShapeDtypeStruct((ROWS, D), BF), LSE_SHAPE],
        scratch_shapes=[pltpu.VMEM((KEYS, 2 * LANES), BF)],
        compiler_params=params(),
        cost_estimate=cost(32),
        name="cross_forward",
    )(q, kv_own, kv_next, kv_own, kv_next, mask)


def cross_backward(m, q, kv_own, kv_next, mask, o, d_o, lse):
    def block(rows, offset=0):
        return pl.BlockSpec((rows, LANES), lambda p: (m, p + offset))

    return pl.pallas_call(
        cross_backward_kernel,
        grid=(PAIRS,),
        in_specs=[
            block(TGT_LEN),
            block(OWN),
            block(NEXT),
            block(OWN, PAIRS),
            block(NEXT, PAIRS),
            pl.BlockSpec((1, KEYS, LANES), lambda p: (m, 0, 0)),
            block(TGT_LEN),
            block(TGT_LEN),
            pl.BlockSpec((1, 8, TGT_LEN), lambda p: (m * PAIRS + p, 0, 0)),
        ],
        out_specs=[
            pl.BlockSpec((TGT_LEN, LANES), lambda p: (0, p)),
            pl.BlockSpec((2, OWN, LANES), lambda p: (0, 0, p)),
            pl.BlockSpec((2, NEXT, LANES), lambda p: (0, 0, p)),
        ],
        out_shape=[
            shape(TGT_LEN, D),
            jax.ShapeDtypeStruct((2, OWN, D), BF),
            jax.ShapeDtypeStruct((2, NEXT, D), BF),
        ],
        scratch_shapes=[pltpu.VMEM((KEYS, 2 * LANES), BF)] * 2,
        compiler_params=params(),
        cost_estimate=cost(22),
        name="cross_backward",
    )(q, kv_own, kv_next, kv_own, kv_next, mask, o, d_o, lse)


def swapped(spec):
    index = spec.index_map
    return pl.BlockSpec(spec.block_shape, lambda p, m: index(m, p))


TILE_BLOCK = pl.BlockSpec((2, 2, HALF, HALF), lambda p, m: (p, 0, 0, 0))


def self_forward(qkv, tiles):
    return pl.pallas_call(
        self_forward_kernel,
        grid=(PAIRS, MICRO),
        in_specs=[
            swapped(pair_block(TGT_LEN)),
            swapped(pair_block(TGT_LEN, PAIRS)),
            swapped(pair_block(TGT_LEN, 2 * PAIRS)),
            TILE_BLOCK,
        ],
        out_specs=[swapped(pair_block(TGT_LEN)), swapped(LSE_BLOCK)],
        out_shape=[jax.ShapeDtypeStruct((ROWS, D), BF), LSE_SHAPE],
        compiler_params=params(),
        cost_estimate=cost(17),
        name="self_forward",
    )(qkv, qkv, qkv, tiles)


def self_backward(qkv, tiles, o, d_o, lse):
    sums = jax.ShapeDtypeStruct((HEADS, 8, HALF), F32)
    return pl.pallas_call(
        self_backward_kernel,
        grid=(PAIRS, MICRO),
        in_specs=[
            swapped(pair_block(TGT_LEN)),
            swapped(pair_block(TGT_LEN, PAIRS)),
            swapped(pair_block(TGT_LEN, 2 * PAIRS)),
            TILE_BLOCK,
            swapped(pair_block(TGT_LEN)),
            swapped(pair_block(TGT_LEN)),
            swapped(LSE_BLOCK),
        ],
        out_specs=[
            pl.BlockSpec((3, TGT_LEN, LANES), lambda p, m: (0, m, p)),
            pl.BlockSpec((2, 8, HALF), lambda p, m: (p, 0, 0)),
        ],
        out_shape=[jax.ShapeDtypeStruct((3, ROWS, D), BF), sums],
        scratch_shapes=[pltpu.VMEM((TGT_LEN, 2 * LANES), BF)] * 2
        + [pltpu.VMEM((2, HALF, HALF), F32)] * 2,
        compiler_params=params(),
        cost_estimate=cost(24),
        name="self_backward",
    )(qkv, qkv, qkv, tiles, o, d_o, lse)


def key_masks(offsets_row, position):
    shard_ids = jnp.arange(offsets_row.shape[0], dtype=jnp.int32)
    own_start = jnp.sum(jnp.where(shard_ids == position, offsets_row, 0))
    next_start = jnp.sum(jnp.where(shard_ids == position + 1, offsets_row, 0))
    own_valid = jnp.arange(MEM_DEV - OWN, MEM_DEV, dtype=jnp.int32) >= own_start
    next_valid = jnp.arange(NEXT, dtype=jnp.int32) < next_start
    valid = jnp.concatenate([own_valid, next_valid])[:, None]
    lane = jnp.arange(LANES, dtype=jnp.int32)[None, :]
    return jnp.where((lane == 0), jnp.where(valid, 0.0, MASKED), 1.0).astype(BF)


def passed_along(block, distance):
    devices = range(lax.axis_size("seq"))
    route = [(i - distance, i) for i in devices if i - distance in devices]
    return lax.ppermute(block, "seq", route)


def device_bits():
    bits = []
    for axis in AXES:
        count = lax.axis_size(axis).bit_length() - 1
        bits += [(axis, place) for place in reversed(range(count))]
    return bits


def bit_groups():
    bits = device_bits()
    core = ("dp", 0)
    low = (lax.axis_size("seq").bit_length() - 1) // 2
    plane = [b for b in bits if b != core and (b[0] == "dp" or b[1] < low)]
    column = [b for b in bits if b[0] == "seq" and b[1] >= low]
    return [core], plane, column


def mine(bit):
    axis, place = bit
    return (lax.axis_index(axis) >> place) & 1


def flips(group):
    for mask in range(1, 1 << len(group)):
        yield [(mask >> place) & 1 for place in range(len(group))]


def exchange(block, group, flip):
    mask = 0
    for (axis, place), turned in zip(group, flip):
        stride = lax.axis_size("seq") if axis == "dp" else 1
        mask ^= turned * stride << place
    count = lax.axis_size("dp") * lax.axis_size("seq")
    return lax.ppermute(block, AXES, [(i, i ^ mask) for i in range(count)])


def gather_stage(held, dims, group, fillers=()):
    order = device_bits()
    joined = sorted(dims + group, key=order.index)
    tail = held.shape[len(dims) :]
    spot = tuple(1 if bit in group else 2 for bit in joined) + tail
    turns = [[0] * len(group)] + list(flips(group))
    pieces = [held] + [exchange(held, group, flip) for flip in turns[1:]]
    pieces, fillers = tied(pieces, fillers)
    result = jnp.zeros((2,) * len(joined) + tail, held.dtype)
    for flip, piece in zip(turns, pieces):
        start = [mine(bit) ^ flip[group.index(bit)] if bit in group else 0 for bit in joined]
        result = lax.dynamic_update_slice(result, piece.reshape(spot), start + [0] * len(tail))
    return result, joined, fillers


def paired_halves(shard, core):
    halves = shard.reshape(shard.shape[0], 2, -1)
    here = lax.dynamic_index_in_dim(halves, core, 1, keepdims=False)
    there = lax.dynamic_index_in_dim(halves, 1 - core, 1, keepdims=False)
    received = exchange(there, bit_groups()[0], [1])
    return jnp.stack([jnp.where(core == 0, here, received), jnp.where(core == 0, received, here)])


def both_halves(held):
    own = held.reshape(-1, held.shape[-1])
    return own, exchange(own, bit_groups()[0], [1])


def gather_bits(held, dims, group):
    for bit in reversed(group):
        held, dims, _ = gather_stage(held, dims, [bit])
    return held, dims, ()


def tree_sum(terms):
    terms = [term.astype(F32) for term in terms]
    while len(terms) > 1:
        terms = [
            terms[place] + terms[place + 1] if place + 1 < len(terms) else terms[place]
            for place in range(0, len(terms), 2)
        ]
    return terms[0]


def picked(array, dims, group, flip):
    left = list(dims)
    for bit, turned in zip(group, flip):
        place = left.index(bit)
        left.remove(bit)
        array = lax.dynamic_index_in_dim(array, mine(bit) ^ turned, place, keepdims=False)
    return array


def scatter_parts(bundles, dims, group):
    def part(flip):
        sums = [
            tree_sum([picked(term, dims, group, flip) for term in terms]).astype(BF)
            for terms in bundles
        ]
        return jnp.concatenate(sums, axis=-1) if len(sums) > 1 else sums[0]

    return [part([0] * len(group))] + [part(flip) for flip in flips(group)]


def scattered(parts, group):
    sent = [exchange(part, group, flip) for part, flip in zip(parts[1:], flips(group))]
    return parts[:1] + sent


def core_stage(give, keep):
    core, _, _ = bit_groups()
    dims = [bit for bit in device_bits() if bit not in core]
    received = exchange(give, core, [1])
    split = (2,) * len(dims) + (give.shape[0] * give.shape[1] >> len(dims), give.shape[2])
    return [keep.reshape(split), received.reshape(split)]


def without(dims, group):
    return [bit for bit in dims if bit not in group]


def passed_along(block, distance):
    devices = range(lax.axis_size("seq"))
    route = [(i - distance, i) for i in devices if i - distance in devices]
    return lax.ppermute(block, "seq", route)


def ffn_grads(h3, hidden, d_gate, d_up, dy, later):
    devices = lax.axis_size("dp") * lax.axis_size("seq")
    width = hidden.shape[1]
    if D // devices % 8 or width // devices % 16:
        total = [
            lax.psum_scatter(
                lax.dot_general(
                    rows, grads, (((0,), (0,)), ((), ())), preferred_element_type=F32
                ),
                AXES,
                scatter_dimension=0,
                tiled=True,
            )
            for rows, grads in ((h3, d_gate), (h3, d_up), (hidden, dy))
        ]
        return total, later
    partial = ffn_weight_grads(h3, hidden, d_gate, d_up, dy, devices)
    later, partial = tied(later, partial)
    return lax.psum_scatter(partial, AXES, scatter_dimension=0, tiled=True), later


def ffn_columns(total, share, width):
    if isinstance(total, (list, tuple)):
        return total
    total = total[0].astype(F32)
    rows = share * width // WIDE

    def columns(first, height):
        block = total[first : first + rows].reshape(-1, height, WIDE)
        return block.transpose(1, 0, 2).reshape(height, -1)

    return columns(0, share), columns(rows, share), columns(2 * rows, rows * WIDE // D)


def tied(values, parts):
    values, parts = lax.optimization_barrier((values, parts))
    return values, parts


def local(
    decoder_in,
    memory,
    doc_offsets,
    self_query,
    self_key,
    self_value,
    self_out,
    cross_query,
    cross_key,
    cross_value,
    cross_out,
    ffn_gate,
    ffn_up,
    ffn_down,
    norm_self,
    norm_cross,
    norm_ffn,
    bias_table,
    cotangent,
):
    position = lax.axis_index("seq")
    core = lax.axis_index("dp") & 1
    core_id = core.reshape(1).astype(jnp.int32)
    across = lax.axis_size("dp") // 2
    share = self_query.shape[0]
    core_bits, plane, column = bit_groups()

    gains = jnp.stack([norm_self, norm_cross, norm_ffn], axis=1)
    gains = jnp.pad(gains, ((0, 0), (0, 2 * LANES - 3)))
    first = jnp.concatenate(
        [cross_key, cross_value, self_query, self_key, self_value, gains], axis=1
    )
    second = jnp.concatenate([self_out, cross_query], axis=1)
    late = jnp.concatenate([cross_out, ffn_gate, ffn_up], axis=1)
    first = paired_halves(first, core)
    first, dims, _ = gather_stage(first, core_bits, column)
    first, second, ffn_down, doc_offsets, memory, bias_table = lax.optimization_barrier(
        (first, second, ffn_down, doc_offsets, memory, bias_table)
    )
    second = paired_halves(second, core)
    third = paired_halves(ffn_down, core)
    tiles = bias_tiles(bias_table.astype(F32))
    mask = jnp.stack([key_masks(doc_offsets[m, 0], position) for m in range(MICRO)])
    next_rows = memory[:, 0, :NEXT]
    second, _, _ = gather_bits(second, core_bits, column)
    first, _, (second, third, tiles, mask, next_rows) = gather_stage(
        first, dims, plane, (second, third, tiles, mask, next_rows)
    )
    own, other = both_halves(first)
    late = lax.all_gather(late, AXES, axis=0, tiled=True)
    x = decoder_in.reshape(ROWS, D)
    dy = cotangent.reshape(ROWS, D)
    mem = memory.reshape(MICRO * MEM_DEV, D)
    next_rows = passed_along(next_rows, -1).reshape(MICRO * NEXT, D)

    x, second = tied(x, second)
    h1, qkv, gains = self_inputs(core_id, own, other, x)
    o1, lse1 = self_forward(qkv, tiles)
    mem, o1 = tied(mem, o1)
    kv_own = key_value(
        core_id, own, other, mem, MICRO * OWN // BLOCK, lambda i: (i + i // 3 + 1, 0), 6
    )
    second, _, (o1, kv_own, next_rows) = gather_stage(
        second, dims, plane, (o1, kv_own, next_rows)
    )
    own_b, other_b = both_halves(second)
    next_rows, third, own_b = lax.optimization_barrier((next_rows, third, own_b))
    kv_next = key_value(
        core_id, own, other, next_rows, MICRO * NEXT // BLOCK, lambda i: (i, 0), 4
    )
    o1, kv_next = tied(o1, kv_next)
    x1, h2, q2 = cross_inputs(core_id, own_b, other_b, gains, x, o1)
    third, _, q2 = gather_stage(third, core_bits, column, q2)
    o2, lse2 = cross_forward(q2, kv_own, kv_next, mask)
    third, _, o2 = gather_stage(third, dims, plane, o2)
    own_c, other_c = both_halves(third)
    out, h3, hidden, d_gate, d_up, db2, dx2, do2, g_norm_ffn = ffn(
        core_id, late, own_c, other_c, gains, x1, o2, dy
    )
    ffn_total, do2 = ffn_grads(h3, hidden, d_gate, d_up, dy, do2)
    dims = without(device_bits(), core_bits)
    arguments = (q2, kv_own, kv_next, mask, o2, do2, lse2)
    results, arrived = [], []
    for m in range(MICRO):
        dq_m, own_m, next_m = cross_backward(m, *arguments)
        dm_m = memory_grads(core_id, own, other, next_m)
        if m + 1 < MICRO:
            arguments, dm_m = tied(arguments, dm_m)
        results.append((dq_m, own_m, next_m))
        if arrived:
            dm_m, arrived[-1] = tied(dm_m, arrived[-1])
        arrived.append(passed_along(dm_m, 1))
    dq2, dkv_own, dkv_next = zip(*results)
    dkv_own, dkv_next, dm_m = lax.optimization_barrier((dkv_own, dkv_next, dm_m))
    pair_terms = core_stage(*pair_grads(core_id, [(o2, (db2,)), (h2, dq2)], across))
    give, keep = memory_weight_grads(core_id, memory, next_rows, dkv_own, dkv_next, across)
    dq2, give = tied(dq2, give)
    memory_terms = core_stage(give, keep)
    dx1, db1, do1, g_norm_cross = self_grads(core_id, own_b, other_b, gains, x1, dx2, dq2)
    (db1, do1), arrived[-1], pair_terms, memory_terms = lax.optimization_barrier(
        ((db1, do1), arrived[-1], pair_terms, memory_terms)
    )
    out_terms = core_stage(*pair_grads(core_id, [(o1, (db1,))], across))
    cross_parts = scatter_parts([pair_terms, memory_terms, out_terms], dims, plane)
    do1, cross_parts = tied(do1, cross_parts)
    cross_terms = scattered(cross_parts, plane)
    dqkv, sums = self_backward(qkv, tiles, o1, do1, lse1)
    give, keep = row_grads(core_id, h1, dqkv, across, 5)
    (dqkv, cross_terms, ffn_total), give = tied((dqkv, cross_terms, ffn_total), give)
    self_terms = core_stage(give, keep)
    cross_parts = scatter_parts([cross_terms], without(dims, plane), column)
    dqkv, cross_parts = tied(dqkv, cross_parts)
    cross_terms = scattered(cross_parts, column)
    grad_decoder, g_norm_self = input_grads(core_id, own, other, gains, x, dx1, dqkv)
    extra_terms = core_stage(
        *extras(core_id, sums, [g_norm_self, g_norm_cross, g_norm_ffn], across, share)
    )
    self_terms, extra_terms, cross_terms = lax.optimization_barrier(
        (self_terms, extra_terms, cross_terms)
    )
    self_parts = scatter_parts([self_terms, extra_terms], dims, plane)
    dkv_own, self_parts = tied(dkv_own, self_parts)
    self_terms = scattered(self_parts, plane)
    grad_memory = memory_total(core_id, own, other, dkv_own, arrived)
    grad_memory, self_terms = tied(grad_memory, self_terms)
    self_parts = scatter_parts([self_terms], without(dims, plane), column)
    g_self = tree_sum(scattered(self_parts, column))
    g_cross = tree_sum(cross_terms)
    g_gate, g_up, g_down = ffn_columns(ffn_total, share, ffn_gate.shape[1])

    table = g_self[: HEADS * BUCKETS // LANES, 3 * D + LANES :].reshape(HEADS, BUCKETS)

    def cut(stack, index):
        return stack[:, index * D : (index + 1) * D]

    return (
        out.reshape(decoder_in.shape),
        grad_decoder.reshape(decoder_in.shape),
        grad_memory.reshape(memory.shape),
        cut(g_self, 0),
        cut(g_self, 1),
        cut(g_self, 2),
        cut(g_cross, 4),
        cut(g_cross, 1),
        cut(g_cross, 2),
        cut(g_cross, 3),
        cut(g_cross, 0),
        g_gate,
        g_up,
        g_down,
        g_self[:, 3 * D],
        g_self[:, 3 * D + 1],
        g_self[:, 3 * D + 2],
        table,
    )


def solution(mesh):
    in_specs = (
        P(None, ("dp", "seq"), None, None),
        P(None, ("dp", "seq"), None, None),
        P(None, "dp", None),
        P(("dp", "seq"), None),
        P(("dp", "seq"), None),
        P(("dp", "seq"), None),
        P(("dp", "seq"), None),
        P(("dp", "seq"), None),
        P(("dp", "seq"), None),
        P(("dp", "seq"), None),
        P(("dp", "seq"), None),
        P(("dp", "seq"), None),
        P(("dp", "seq"), None),
        P(("dp", "seq"), None),
        P(("dp", "seq")),
        P(("dp", "seq")),
        P(("dp", "seq")),
        P(),
        P(None, ("dp", "seq"), None, None),
    )
    out_specs = (
        P(None, ("dp", "seq"), None, None),
        P(None, ("dp", "seq"), None, None),
        P(None, ("dp", "seq"), None, None),
        P(("dp", "seq"), None),
        P(("dp", "seq"), None),
        P(("dp", "seq"), None),
        P(("dp", "seq"), None),
        P(("dp", "seq"), None),
        P(("dp", "seq"), None),
        P(("dp", "seq"), None),
        P(("dp", "seq"), None),
        P(("dp", "seq"), None),
        P(("dp", "seq"), None),
        P(("dp", "seq"), None),
        P(("dp", "seq")),
        P(("dp", "seq")),
        P(("dp", "seq")),
        P(),
    )
    return jax.shard_map(local, mesh=mesh, in_specs=in_specs, out_specs=out_specs, check_vma=False)
```

```python
import functools
import math

import jax
import jax.numpy as jnp
from jax import lax
from jax.experimental import pallas as pl
from jax.experimental.pallas import tpu as pltpu
from jax.sharding import PartitionSpec as P

D = 768
HEADS = 12
HEAD_DIM = 64
BUCKETS = 32
REACH = 128
TGT_LEN = 512
MEM_DEV = 1024
MICRO = 2
PAIRS = HEADS // 2
LANES = 2 * HEAD_DIM
OWN = MEM_DEV - MEM_DEV // 4
NEXT = MEM_DEV // 2
KEYS = OWN + NEXT
HALF = 256
MASKED = -1e30
NORM_EPS = 1e-06
AXES = ("dp", "seq")
ROWS = MICRO * TGT_LEN
BLOCK = 256
WIDE = 256
SMALL_SCORE = 59.0
FFN_CHUNK = 1024
HALF_COLUMNS = 2048
VMEM_LIMIT = 52 * 1024 * 1024
BF = jnp.bfloat16
F32 = jnp.float32


def nn(a, b):
    return lax.dot_general(a, b, (((1,), (0,)), ((), ())), preferred_element_type=F32)


def bucket_limits(buckets, reach):
    exact_count = buckets // 2
    limits = []
    for target in range(exact_count + 1, buckets):
        distance = exact_count
        while (
            exact_count
            + int(
                math.log(distance / exact_count)
                / math.log(reach / exact_count)
                * (buckets - exact_count)
            )
            < target
        ):
            distance += 1
        limits.append(distance)
    return limits


def three_parts(row):
    high = row.astype(BF).astype(F32)
    rest = row - high
    middle = rest.astype(BF).astype(F32)
    return high, middle, rest - middle


def extra_rows(columns, first, parts):
    row_id = lax.broadcasted_iota(jnp.int32, (LANES, columns), 0)
    grid = jnp.where(row_id == 0, first, 0.0)
    for place, part in enumerate(parts):
        grid = jnp.where(row_id == place + 1, part, grid)
    return grid.astype(BF)


def head_rows(stacked, head):
    row_id = lax.broadcasted_iota(jnp.int32, stacked.shape, 0)
    return jnp.where((row_id // HEAD_DIM) == head, stacked, jnp.zeros_like(stacked))


def far(array):
    return pltpu.with_memory_space_constraint(array, pltpu.HBM)


def nt(a, b):
    return lax.dot_general(a, b, (((1,), (1,)), ((), ())), preferred_element_type=F32)


def params(**options):
    return pltpu.CompilerParams(vmem_limit_bytes=VMEM_LIMIT, **options)


def cost(us):
    return pl.CostEstimate(flops=int(us), bytes_accessed=0, transcendentals=0)


def shape(rows, columns, kind=BF):
    return jax.ShapeDtypeStruct((rows, columns), kind)


def row_block(columns, rows=BLOCK):
    return pl.BlockSpec((rows, columns), lambda i: (i, 0))


def fixed_block(rows, columns):
    return pl.BlockSpec((rows, columns), lambda i: (0, 0))


ANY = pl.BlockSpec(memory_space=pl.ANY)
SMEM = pl.BlockSpec(memory_space=pltpu.SMEM)


def halves_loaded(core_ref, own_ref, other_ref, pieces, sems):
    @pl.when(pl.program_id(0) == 0)
    def _():
        for side in range(2):

            @pl.when(core_ref[0] == side)
            def _():
                halves = (own_ref, other_ref) if side == 0 else (other_ref, own_ref)
                copies = [
                    pltpu.make_async_copy(halves[half].at[:, source], target, sems.at[place])
                    for place, (half, source, target) in enumerate(pieces)
                ]
                for copy in copies:
                    copy.start()
                for copy in copies:
                    copy.wait()


def key_value_pieces(w_kv):
    return [(0, slice(0, 2 * D), w_kv)]


def out_query_pieces(weights):
    return [(side, slice(0, D), weights.at[:, side * D : (side + 1) * D]) for side in range(2)]


def query_pieces(w_qkv):
    cut = HALF_COLUMNS - 2 * D
    return [
        (0, slice(2 * D, HALF_COLUMNS), w_qkv.at[:, :cut]),
        (1, slice(0, 3 * D - cut), w_qkv.at[:, cut:]),
    ]


def normed(values, gain):
    inverse = lax.rsqrt(jnp.mean(values * values, axis=-1, keepdims=True) + NORM_EPS)
    scaled = values * inverse
    return scaled, inverse, (scaled * gain).astype(BF)


def norm_back(values, gain, grads, gain_grad_ref):
    inverse = lax.rsqrt(jnp.mean(values * values, axis=-1, keepdims=True) + NORM_EPS)
    scaled = values * inverse
    add_rows(gain_grad_ref, jnp.sum(scaled * grads, axis=0, keepdims=True))
    weighted = grads * gain
    centre = jnp.mean(scaled * weighted, axis=-1, keepdims=True)
    return inverse * (weighted - scaled * centre)


def add_rows(total_ref, row):
    row_id = lax.broadcasted_iota(jnp.int32, (8, D), 0)
    addend = jnp.where(row_id == 0, row, 0.0)

    @pl.when(pl.program_id(0) == 0)
    def _():
        total_ref[...] = addend

    @pl.when(pl.program_id(0) > 0)
    def _():
        total_ref[...] += addend


def keep_largest(total_ref, values):
    head = lax.broadcasted_iota(jnp.int32, (D, LANES), 0) // HEAD_DIM
    lane = lax.broadcasted_iota(jnp.int32, (D, LANES), 1)
    hot = jnp.where(head == lane, 1.0, 0.0).astype(BF)
    values = values.astype(F32)
    squares = nn((values * values).astype(BF), hot)
    row = jnp.broadcast_to(jnp.max(squares, axis=0, keepdims=True), (8, LANES))

    @pl.when(pl.program_id(0) == 0)
    def _():
        total_ref[...] = row

    @pl.when(pl.program_id(0) > 0)
    def _():
        total_ref[...] = jnp.maximum(total_ref[...], row)


def key_value_kernel(core_ref, own_ref, other_ref, rows_ref, kv_ref, size_ref, w_kv, sems):
    halves_loaded(core_ref, own_ref, other_ref, key_value_pieces(w_kv), sems)
    kv_ref[...] = nn(rows_ref[...], w_kv[...]).astype(BF)
    keep_largest(size_ref, kv_ref[:, :D])


def key_value(core, own, other, rows, steps, index, us):
    return pl.pallas_call(
        key_value_kernel,
        grid=(steps,),
        in_specs=[SMEM, ANY, ANY, pl.BlockSpec((BLOCK, D), index)],
        out_specs=[row_block(2 * D), fixed_block(8, LANES)],
        out_shape=[shape(steps * BLOCK, 2 * D), shape(8, LANES, F32)],
        scratch_shapes=[pltpu.VMEM((D, 2 * D), BF), pltpu.SemaphoreType.DMA((1,))],
        compiler_params=params(),
        cost_estimate=cost(us),
        name="key_value",
    )(core, own, other, rows)


def self_inputs_kernel(
    core_ref, own_ref, other_ref, x_ref, h_ref, qkv_ref, gains_ref, w_qkv, gain_columns, sems
):
    first_gain = 5 * D - HALF_COLUMNS
    pieces = query_pieces(w_qkv)
    pieces.append((1, slice(first_gain, first_gain + LANES), gain_columns))
    halves_loaded(core_ref, own_ref, other_ref, pieces, sems)

    @pl.when(pl.program_id(0) == 0)
    def _():
        gains_ref[...] = gain_columns[...].astype(F32).T[:8]

    h_ref[...] = normed(x_ref[...].astype(F32), gains_ref[:1, :])[2]
    qkv_ref[...] = nn(h_ref[...], w_qkv[...]).astype(BF)


def self_inputs(core, own, other, x):
    return pl.pallas_call(
        self_inputs_kernel,
        grid=(ROWS // BLOCK,),
        in_specs=[SMEM, ANY, ANY, row_block(D)],
        out_specs=[row_block(D), row_block(3 * D), fixed_block(8, D)],
        out_shape=[shape(ROWS, D), shape(ROWS, 3 * D), shape(8, D, F32)],
        scratch_shapes=[
            pltpu.VMEM((D, 3 * D), BF),
            pltpu.VMEM((D, LANES), BF),
            pltpu.SemaphoreType.DMA((3,)),
        ],
        compiler_params=params(),
        cost_estimate=cost(6),
        name="self_inputs",
    )(core, own, other, x)


def cross_inputs_kernel(
    core_ref, own_ref, other_ref, gain_ref, x_ref, o_ref,
    x1_ref, h_ref, q_ref, size_ref, weights, sems,
):
    halves_loaded(core_ref, own_ref, other_ref, out_query_pieces(weights), sems)
    x1 = x_ref[...].astype(F32) + nn(o_ref[...], weights[:, :D])
    x1_ref[...] = x1
    h_ref[...] = normed(x1, gain_ref[1:2, :])[2]
    q_ref[...] = nn(h_ref[...], weights[:, D:]).astype(BF)
    keep_largest(size_ref, q_ref[...])


def cross_inputs(core, own, other, gain, x, o1):
    return pl.pallas_call(
        cross_inputs_kernel,
        grid=(ROWS // BLOCK,),
        in_specs=[SMEM, ANY, ANY, fixed_block(8, D), row_block(D), row_block(D)],
        out_specs=[row_block(D)] * 3 + [fixed_block(8, LANES)],
        out_shape=[shape(ROWS, D, F32), shape(ROWS, D), shape(ROWS, D), shape(8, LANES, F32)],
        scratch_shapes=[pltpu.VMEM((D, 2 * D), BF), pltpu.SemaphoreType.DMA((2,))],
        compiler_params=params(),
        cost_estimate=cost(5),
        name="cross_inputs",
    )(core, own, other, gain, x, o1)


def ffn_kernel(
    core_ref, late_ref, own_ref, other_ref, gain_ref, x1_ref, o_ref, dy_ref,
    out_ref, h_ref, acts_ref, db_ref, dx_ref, do_ref, gain_grad_ref,
    w_out, w_gate, w_up, w_down, sems,
):
    width = w_gate.shape[1]
    first = pl.program_id(0) == 0
    copies = [
        pltpu.make_async_copy(late_ref.at[:, :D], w_out, sems.at[0]),
        pltpu.make_async_copy(late_ref.at[:, D : D + width], w_gate, sems.at[1]),
        pltpu.make_async_copy(late_ref.at[:, D + width :], w_up, sems.at[2]),
    ]

    def down_copies(side):
        halves = (own_ref, other_ref) if side == 0 else (other_ref, own_ref)
        columns = [slice(half * D // 2, (half + 1) * D // 2) for half in range(2)]
        return [
            pltpu.make_async_copy(halves[half], w_down.at[:, columns[half]], sems.at[3 + half])
            for half in range(2)
        ]

    @pl.when(first)
    def _():
        for copy in copies:
            copy.start()
        for side in range(2):

            @pl.when(core_ref[0] == side)
            def _():
                for copy in down_copies(side):
                    copy.start()

    def arrived(place):
        @pl.when(first)
        def _():
            copies[place].wait()

    arrived(0)
    x2 = x1_ref[...] + nn(o_ref[...], w_out[...])
    h_ref[...] = normed(x2, gain_ref[2:3, :])[2]
    dy_low = dy_ref[...]
    arrived(1)
    arrived(2)

    @pl.when(first)
    def _():
        for side in range(2):

            @pl.when(core_ref[0] == side)
            def _():
                for copy in down_copies(side):
                    copy.wait()

    scale = math.sqrt(2.0 / math.pi)
    out, dh = x2, 0.0
    h = h_ref[...]
    for start in range(0, width, FFN_CHUNK):
        part = slice(start, start + FFN_CHUNK)
        gate = nn(h, w_gate[:, part])
        up = nn(h, w_up[:, part])
        d_hidden = nt(dy_low, w_down[part, :])
        square = gate * gate
        turn = jnp.tanh(gate * (scale + (scale * 0.044715) * square))
        half = 0.5 + 0.5 * turn
        gelu = gate * half
        bend = gate * (0.5 * scale + (0.5 * scale * 3 * 0.044715) * square)
        slope = half + (1.0 - turn * turn) * bend
        hidden = (gelu * up).astype(BF)
        d_gate = (d_hidden * up * slope).astype(BF)
        d_up = (d_hidden * gelu).astype(BF)
        acts_ref[0, :, part] = d_gate
        acts_ref[1, :, part] = d_up
        acts_ref[2, :, part] = hidden
        out = out + nn(hidden, w_down[part, :])
        dh = dh + nt(d_gate, w_gate[:, part]) + nt(d_up, w_up[:, part])
    out_ref[...] = out.astype(BF)
    dx = dy_low.astype(F32) + norm_back(x2, gain_ref[2:3, :], dh, gain_grad_ref)
    dx_ref[...] = dx
    db_ref[...] = dx.astype(BF)
    do_ref[...] = nt(db_ref[...], w_out[...]).astype(BF)


def ffn(core, late, own, other, gain, x1, o2, dy):
    width = own.shape[0]
    return pl.pallas_call(
        ffn_kernel,
        grid=(ROWS // BLOCK,),
        in_specs=[SMEM, ANY, ANY, ANY, fixed_block(8, D), row_block(D), row_block(D), row_block(D)],
        out_specs=[
            row_block(D),
            row_block(D),
            pl.BlockSpec((3, BLOCK, width), lambda i: (0, i, 0)),
            row_block(D),
            row_block(D),
            row_block(D),
            fixed_block(8, D),
        ],
        out_shape=[
            shape(ROWS, D),
            shape(ROWS, D),
            jax.ShapeDtypeStruct((3, ROWS, width), BF),
            shape(ROWS, D),
            shape(ROWS, D, F32),
            shape(ROWS, D),
            shape(8, D, F32),
        ],
        scratch_shapes=[
            pltpu.VMEM((D, D), BF),
            pltpu.VMEM((D, width), BF),
            pltpu.VMEM((D, width), BF),
            pltpu.VMEM((width, D), BF),
            pltpu.SemaphoreType.DMA((5,)),
        ],
        compiler_params=params(),
        cost_estimate=cost(30),
        name="ffn",
    )(core, far(late), far(own), far(other), gain, far(x1), o2, far(dy))


def self_grads_kernel(
    core_ref, own_ref, other_ref, gain_ref, x1_ref, dx2_ref, dq0_ref, dq1_ref,
    dx1_ref, db_ref, do_ref, gain_grad_ref, weights, sems,
):
    halves_loaded(core_ref, own_ref, other_ref, out_query_pieces(weights), sems)
    low = pl.program_id(0) < TGT_LEN // BLOCK
    dh = nt(jnp.where(low, dq0_ref[...], dq1_ref[...]), weights[:, D:])
    dx1 = dx2_ref[...] + norm_back(x1_ref[...], gain_ref[1:2, :], dh, gain_grad_ref)
    dx1_ref[...] = dx1
    db_ref[...] = dx1.astype(BF)
    do_ref[...] = nt(db_ref[...], weights[:, :D]).astype(BF)


def self_grads(core, own, other, gain, x1, dx2, dq2):
    half = TGT_LEN // BLOCK
    return pl.pallas_call(
        self_grads_kernel,
        grid=(ROWS // BLOCK,),
        in_specs=[
            SMEM,
            ANY,
            ANY,
            fixed_block(8, D),
            row_block(D),
            row_block(D),
            pl.BlockSpec((BLOCK, D), lambda i: (jnp.minimum(i, half - 1), 0)),
            pl.BlockSpec((BLOCK, D), lambda i: (jnp.maximum(i - half, 0), 0)),
        ],
        out_specs=[row_block(D), row_block(D), row_block(D), fixed_block(8, D)],
        out_shape=[shape(ROWS, D, F32), shape(ROWS, D), shape(ROWS, D), shape(8, D, F32)],
        scratch_shapes=[pltpu.VMEM((D, 2 * D), BF), pltpu.SemaphoreType.DMA((2,))],
        compiler_params=params(),
        cost_estimate=cost(5),
        name="self_grads",
    )(core, far(own), far(other), gain, far(x1), far(dx2), *dq2)


def input_grads_kernel(
    core_ref, own_ref, other_ref, gain_ref, x_ref, dx1_ref, dqkv_ref,
    dx_ref, gain_grad_ref, w_qkv, sems,
):
    halves_loaded(core_ref, own_ref, other_ref, query_pieces(w_qkv), sems)
    dh = (
        nt(dqkv_ref[0], w_qkv[:, :D])
        + nt(dqkv_ref[1], w_qkv[:, D : 2 * D])
        + nt(dqkv_ref[2], w_qkv[:, 2 * D :])
    )
    x = x_ref[...].astype(F32)
    dx_ref[...] = (dx1_ref[...] + norm_back(x, gain_ref[:1, :], dh, gain_grad_ref)).astype(BF)


def input_grads(core, own, other, gain, x, dx1, dqkv):
    return pl.pallas_call(
        input_grads_kernel,
        grid=(ROWS // BLOCK,),
        in_specs=[
            SMEM, ANY, ANY, fixed_block(8, D), row_block(D), row_block(D),
            pl.BlockSpec((3, BLOCK, D), lambda i: (0, i, 0)),
        ],
        out_specs=[row_block(D), fixed_block(8, D)],
        out_shape=[shape(ROWS, D), shape(8, D, F32)],
        scratch_shapes=[pltpu.VMEM((D, 3 * D), BF), pltpu.SemaphoreType.DMA((2,))],
        compiler_params=params(),
        cost_estimate=cost(6),
        name="input_grads",
    )(core, far(own), far(other), gain, far(x), dx1, dqkv)


def memory_grads_kernel(core_ref, own_ref, other_ref, dkv_ref, dm_ref, w_kv, sems):
    halves_loaded(core_ref, own_ref, other_ref, key_value_pieces(w_kv), sems)
    dm_ref[...] = (nt(dkv_ref[0], w_kv[:, :D]) + nt(dkv_ref[1], w_kv[:, D:])).astype(BF)


def memory_grads(core, own, other, dkv):
    rows = dkv.shape[1]
    return pl.pallas_call(
        memory_grads_kernel,
        grid=(rows // BLOCK,),
        in_specs=[SMEM, ANY, ANY, pl.BlockSpec((2, BLOCK, D), lambda i: (0, i, 0))],
        out_specs=row_block(D),
        out_shape=shape(rows, D),
        scratch_shapes=[pltpu.VMEM((D, 2 * D), BF), pltpu.SemaphoreType.DMA((1,))],
        compiler_params=params(),
        cost_estimate=cost(rows / 400),
        name="memory_grads",
    )(core, own, other, dkv)


def stored_by_core(core_ref, grad, give_ref, keep_ref):
    across, _, count = give_ref.shape[0], 2, give_ref.shape[1]
    for side in range(2):

        @pl.when(core_ref[0] == side)
        def _():
            for place in range(across):
                first = place * 2 * count
                here, there = first + side * count, first + (1 - side) * count
                keep_ref[place] = grad[here : here + count].astype(BF)
                give_ref[place] = grad[there : there + count].astype(BF)


def row_grads_kernel(core_ref, rows_ref, grads_ref, give_ref, keep_ref, turned):
    @pl.when(pl.program_id(0) == 0)
    def _():
        turned[...] = rows_ref[...].T

    stored_by_core(core_ref, nn(turned[...], grads_ref[0]), give_ref, keep_ref)


def row_grads(core, rows, grads, across, us):
    units, length = grads.shape[0], grads.shape[1]
    count = D // (2 * across)
    block = pl.BlockSpec((across, count, D), lambda u: (0, 0, u))
    piece = jax.ShapeDtypeStruct((across, count, units * D), BF)
    return pl.pallas_call(
        row_grads_kernel,
        grid=(units,),
        in_specs=[SMEM, fixed_block(length, D), pl.BlockSpec((1, length, D), lambda u: (u, 0, 0))],
        out_specs=[block, block],
        out_shape=[piece, piece],
        scratch_shapes=[pltpu.VMEM((D, length), BF)],
        compiler_params=params(),
        cost_estimate=cost(us),
        name="row_grads",
    )(core, rows, grads)


def pair_grads_kernel(counts, core_ref, *refs):
    give_ref, keep_ref = refs[-2:]
    used = 0
    for place, count in enumerate(counts):
        turned = refs[used][...].T
        length = turned.shape[1] // count
        grad = sum(
            nn(turned[:, part * length : (part + 1) * length], refs[used + 1 + part][...])
            for part in range(count)
        )
        used += 1 + count
        columns = slice(place * D, (place + 1) * D)
        stored_by_core(core_ref, grad, give_ref.at[:, :, columns], keep_ref.at[:, :, columns])


def pair_grads(core, pairs, across):
    count = D // (2 * across)
    piece = jax.ShapeDtypeStruct((across, count, len(pairs) * D), BF)
    whole = pl.BlockSpec(memory_space=pltpu.VMEM)
    flat = [array for rows, grads in pairs for array in (rows,) + tuple(grads)]
    return pl.pallas_call(
        functools.partial(pair_grads_kernel, [len(grads) for _, grads in pairs]),
        in_specs=[SMEM] + [whole] * len(flat),
        out_specs=[whole, whole],
        out_shape=[piece, piece],
        compiler_params=params(),
        cost_estimate=cost(2.5 * len(pairs)),
        name="pair_grads",
    )(core, *flat)


def ffn_weight_grads_kernel(h_ref, acts_ref, dy_ref, out_ref):
    devices = out_ref.shape[0]
    width = acts_ref.shape[2]

    @pl.when(pl.program_id(0) < 2)
    def _():
        turned = h_ref[...].T
        share = D // devices
        for first in range(0, width, 2 * WIDE):
            both = [
                nn(turned, acts_ref[0, :, place : place + WIDE]).reshape(devices, share, WIDE)
                for place in (first, first + WIDE)
            ]
            row = first // WIDE * share
            out_ref[:, row : row + 2 * share, :] = jnp.concatenate(both, axis=1).astype(BF)

    @pl.when(pl.program_id(0) == 2)
    def _():
        turned = acts_ref[0].T
        share = width // devices
        for place in range(D // WIDE):
            grad = nn(turned, dy_ref[:, place * WIDE : (place + 1) * WIDE])
            out_ref[:, place * share : (place + 1) * share, :] = grad.reshape(
                devices, share, WIDE
            ).astype(BF)


def ffn_weight_grads(h3, acts, dy, devices):
    width = acts.shape[2]
    rows = D * width // WIDE // devices
    return pl.pallas_call(
        ffn_weight_grads_kernel,
        grid=(3,),
        in_specs=[
            fixed_block(ROWS, D),
            pl.BlockSpec((1, ROWS, width), lambda u: (u, 0, 0)),
            fixed_block(ROWS, D),
        ],
        out_specs=pl.BlockSpec((devices, rows, WIDE), lambda u: (0, u, 0)),
        out_shape=jax.ShapeDtypeStruct((devices, 3 * rows, WIDE), BF),
        compiler_params=params(),
        cost_estimate=cost(13),
        name="ffn_weight_grads",
    )(h3, far(acts), far(dy))


def memory_weight_grads_kernel(
    core_ref, mem_ref, next_ref, own0_ref, own1_ref, after0_ref, after1_ref,
    give_ref, keep_ref, turned,
):
    @pl.when(pl.program_id(0) == 0)
    def _():
        for m in range(MICRO):
            turned[:, m * OWN : (m + 1) * OWN] = mem_ref[m, 0, MEM_DEV - OWN :, :].T
        turned[:, MICRO * OWN :] = next_ref[...].T

    grad, used = 0.0, 0
    for part_ref in (own0_ref, own1_ref, after0_ref, after1_ref):
        length = part_ref.shape[1]
        grad = grad + nn(turned[:, used : used + length], part_ref[0])
        used += length
    stored_by_core(core_ref, grad, give_ref, keep_ref)


def memory_weight_grads(core, memory, next_rows, dkv_own, dkv_next, across):
    count = D // (2 * across)
    block = pl.BlockSpec((across, count, D), lambda u: (0, 0, u))
    piece = jax.ShapeDtypeStruct((across, count, 2 * D), BF)
    return pl.pallas_call(
        memory_weight_grads_kernel,
        grid=(2,),
        in_specs=[
            SMEM,
            pl.BlockSpec((MICRO, 1, MEM_DEV, D), lambda u: (0, 0, 0, 0)),
            fixed_block(MICRO * NEXT, D),
        ]
        + [pl.BlockSpec((1, OWN, D), lambda u: (u, 0, 0))] * MICRO
        + [pl.BlockSpec((1, NEXT, D), lambda u: (u, 0, 0))] * MICRO,
        out_specs=[block, block],
        out_shape=[piece, piece],
        scratch_shapes=[pltpu.VMEM((D, MICRO * (OWN + NEXT)), BF)],
        compiler_params=params(),
        cost_estimate=cost(8),
        name="memory_weight_grads",
    )(core, memory, next_rows, *dkv_own, *dkv_next)


def memory_total_kernel(core_ref, own_ref, other_ref, dkv_ref, prev_ref, dm_ref, w_kv, sems):
    halves_loaded(core_ref, own_ref, other_ref, key_value_pieces(w_kv), sems)
    block = pl.program_id(0)

    @pl.when(block == 0)
    def _():
        dm_ref[...] = prev_ref[...]

    @pl.when(block > 0)
    def _():
        grads = nt(dkv_ref[0], w_kv[:, :D]) + nt(dkv_ref[1], w_kv[:, D:])
        shared = jnp.where(block == 1, prev_ref[...].astype(F32), 0.0)
        dm_ref[...] = (grads + shared).astype(BF)


def memory_total(core, own, other, dkv, prev):
    return pl.pallas_call(
        memory_total_kernel,
        grid=(MEM_DEV // BLOCK,),
        in_specs=[
            SMEM,
            ANY,
            ANY,
            pl.BlockSpec((2, BLOCK, D), lambda i: (0, jnp.maximum(i - 1, 0), 0)),
            pl.BlockSpec((BLOCK, D), lambda i: (jnp.minimum(i, 1), 0)),
        ],
        out_specs=row_block(D),
        out_shape=shape(MEM_DEV, D),
        scratch_shapes=[pltpu.VMEM((D, 2 * D), BF), pltpu.SemaphoreType.DMA((1,))],
        compiler_params=params(),
        cost_estimate=cost(4),
        name="memory_total",
    )(core, own, other, dkv, prev)


def extras_kernel(share, core_ref, sums_ref, first_ref, second_ref, third_ref, give_ref, keep_ref):
    row_id = lax.broadcasted_iota(jnp.int32, (8, D), 0)
    norms = jnp.zeros((8, D), F32)
    for place, ref in enumerate((first_ref, second_ref, third_ref)):
        norms = jnp.where(row_id == place, ref[:1, :], norms)
    stacked = jnp.concatenate([norms, jnp.zeros((LANES - 8, D), F32)], axis=0).T
    distance = lax.broadcasted_iota(jnp.int32, (HALF, LANES), 0)
    bucket_id = lax.broadcasted_iota(jnp.int32, (HALF, LANES), 1)
    exact_count = BUCKETS // 2
    bucket = jnp.full((HALF, LANES), exact_count, jnp.int32)
    for threshold in bucket_limits(BUCKETS, REACH):
        bucket = bucket + (distance >= threshold).astype(jnp.int32)
    bucket = jnp.where(distance < exact_count, distance, bucket)
    sums = sums_ref[...]
    together = LANES // BUCKETS
    lines = [jnp.zeros((1, LANES), F32) for _ in range(HEADS // together)]
    for part in range(together):
        near_hot = (bucket == bucket_id - part * BUCKETS).astype(F32)
        far_hot = (bucket_id == (part + 1) * BUCKETS - 1).astype(F32)
        table = sum(
            lax.dot_general(
                sums[:, place, :], hot, (((1,), (0,)), ((), ())),
                precision=lax.Precision.HIGHEST, preferred_element_type=F32,
            )
            for place, hot in ((0, near_hot), (1, far_hot))
        )
        for line in range(len(lines)):
            head = line * together + part
            lines[line] = lines[line] + table[head : head + 1]
    row_in_share = lax.broadcasted_iota(jnp.int32, (D, LANES), 0) % share
    tall = jnp.zeros((D, LANES), F32)
    for line, row in enumerate(lines):
        tall = jnp.where(row_in_share == line, row, tall)
    both = jnp.concatenate([stacked, tall], axis=1)
    stored_by_core(core_ref, both, give_ref, keep_ref)


def extras(core, sums, norms, across, share):
    piece = jax.ShapeDtypeStruct((across, D // (2 * across), 2 * LANES), BF)
    whole = pl.BlockSpec(memory_space=pltpu.VMEM)
    return pl.pallas_call(
        functools.partial(extras_kernel, share),
        in_specs=[SMEM] + [whole] * 4,
        out_specs=[whole, whole],
        out_shape=[piece, piece],
        compiler_params=params(),
        cost_estimate=cost(2),
        name="extras",
    )(core, sums, *norms)


def bias_tiles_kernel(table_ref, tiles_ref):
    head = pl.program_id(0)
    key_id = lax.broadcasted_iota(jnp.int32, (HALF, HALF), 0)
    query_id = lax.broadcasted_iota(jnp.int32, (HALF, HALF), 1)
    limits = bucket_limits(BUCKETS, REACH)
    exact_count = BUCKETS // 2
    for tile in range(2):
        distance = query_id - key_id + tile * HALF
        grid = jnp.full((HALF, HALF), table_ref[head, 0], F32)
        for bucket in range(1, BUCKETS):
            start = bucket if bucket <= exact_count else limits[bucket - exact_count - 1]
            grid = jnp.where(distance >= start, table_ref[head, bucket], grid)
        if tile == 0:
            grid = jnp.where(distance >= 0, grid, MASKED)
        tiles_ref[0, tile] = grid


def bias_tiles(table):
    return pl.pallas_call(
        bias_tiles_kernel,
        grid=(HEADS,),
        in_specs=[pl.BlockSpec(memory_space=pltpu.SMEM)],
        out_specs=pl.BlockSpec((1, 2, HALF, HALF), lambda h: (h, 0, 0, 0)),
        out_shape=jax.ShapeDtypeStruct((HEADS, 2, HALF, HALF), F32),
        cost_estimate=cost(8),
        name="bias_tiles",
    )(table)


def softmax_columns(scores):
    top = jnp.max(scores, axis=0, keepdims=True)
    weights = jnp.exp(scores - top)
    total = jnp.sum(weights, axis=0, keepdims=True)
    return weights.astype(BF), 1.0 / total, top + jnp.log(total)


def put_lse(lse_ref, rows):
    row_id = lax.broadcasted_iota(jnp.int32, (8, TGT_LEN), 0)
    lse_ref[0] = jnp.where(row_id == 0, rows[0], rows[1])


def attended(scores, value, small):
    top = 0.0 if small else jnp.max(scores, axis=0, keepdims=True)
    weights = jnp.exp(scores if small else scores - top).astype(BF)
    both = nn(value, weights)
    total = both[HEAD_DIM : HEAD_DIM + 1]
    return both[:HEAD_DIM] * (1.0 / total), top + jnp.log(total)


def cross_forward_kernel(
    small_ref, q_ref, ko_ref, kn_ref, vo_ref, vn_ref, mask_ref, o_ref, lse_ref, k_ext
):
    def run(small):
        k_ext[:OWN, :LANES] = ko_ref[...]
        k_ext[OWN:, :LANES] = kn_ref[...]
        k_ext[:, LANES:] = mask_ref[0]
        q_t = q_ref[...].T
        v_t = jnp.concatenate([vo_ref[...], vn_ref[...]], axis=0).T
        ones = extra_rows(TGT_LEN, 1.0, ())
        rows_of_ones = jnp.ones((16, KEYS), BF)
        scores = [
            nn(k_ext[...], jnp.concatenate([head_rows(q_t, head), ones], axis=0))
            for head in range(2)
        ]
        values = [
            jnp.concatenate([v_t[head * HEAD_DIM : (head + 1) * HEAD_DIM], rows_of_ones], axis=0)
            for head in range(2)
        ]
        mixed, lses = zip(*[attended(scores[head], values[head], small) for head in range(2)])
        o_ref[...] = jnp.concatenate(mixed, axis=0).T.astype(BF)
        put_lse(lse_ref, lses)

    @pl.when(small_ref[0] == 1)
    def _():
        run(True)

    @pl.when(small_ref[0] != 1)
    def _():
        run(False)


def cross_backward_kernel(
    q_ref, ko_ref, kn_ref, vo_ref, vn_ref, mask_ref, o_ref, do_ref, lse_ref,
    dq_ref, own_ref, next_ref, k_ext, v_ext,
):
    k_ext[:OWN, :LANES] = ko_ref[...]
    k_ext[OWN:, :LANES] = kn_ref[...]
    k_ext[:, LANES:] = mask_ref[0]
    v_ext[:OWN, :LANES] = vo_ref[...]
    v_ext[OWN:, :LANES] = vn_ref[...]
    v_ext[:, LANES:] = jnp.ones((KEYS, LANES), BF)
    k_t = k_ext[:, :LANES].T
    q = q_ref[...]
    d_o = do_ref[...]
    q_t = q.T
    do_t = d_o.T
    centre_t = (o_ref[...].astype(F32) * d_o.astype(F32)).T
    dq, dk, dv = [], [], []
    for head in range(2):
        rows = slice(head * HEAD_DIM, (head + 1) * HEAD_DIM)
        lse = lse_ref[0, head : head + 1, :]
        centre = jnp.sum(centre_t[rows], axis=0, keepdims=True)
        query = jnp.concatenate(
            [head_rows(q_t, head), extra_rows(TGT_LEN, 1.0, three_parts(-lse))], axis=0
        )
        grad = jnp.concatenate(
            [head_rows(do_t, head), extra_rows(TGT_LEN, 0.0, three_parts(-centre))], axis=0
        )
        probs = jnp.exp(nn(k_ext[...], query))
        grad_scores = (probs * nn(v_ext[...], grad)).astype(BF)
        dv.append(nn(probs.astype(BF), d_o))
        dk.append(nn(grad_scores, q))
        dq.append(nn(k_t[rows], grad_scores))
    dq_ref[...] = jnp.concatenate(dq, axis=0).T.astype(BF)
    lane = lax.broadcasted_iota(jnp.int32, (KEYS, LANES), 1)
    dk_pair = jnp.where(lane < HEAD_DIM, dk[0], dk[1]).astype(BF)
    dv_pair = jnp.where(lane < HEAD_DIM, dv[0], dv[1]).astype(BF)
    for place, pair in enumerate((dk_pair, dv_pair)):
        own_ref[place] = pair[:OWN]
        next_ref[place] = pair[OWN:]


def self_forward_kernel(q_ref, k_ref, v_ref, tiles_ref, o_ref, lse_ref):
    k = k_ref[...]
    q_t = q_ref[...].T
    v_t = v_ref[...].T
    mixed, lses = [], []
    for head in range(2):
        query = head_rows(q_t, head)
        value = v_t[head * HEAD_DIM : (head + 1) * HEAD_DIM]
        near, far = tiles_ref[head, 0], tiles_ref[head, 1]
        w0, i0, l0 = softmax_columns(nn(k[:HALF], query[:, :HALF]) + near)
        raw = nn(k, query[:, HALF:])
        w1, i1, l1 = softmax_columns(
            jnp.concatenate([raw[:HALF] + far, raw[HALF:] + near], axis=0)
        )
        out0 = nn(value[:, :HALF], w0) * i0
        out1 = nn(value, w1) * i1
        mixed.append(jnp.concatenate([out0, out1], axis=1))
        lses.append(jnp.concatenate([l0, l1], axis=1))
    o_ref[...] = jnp.concatenate(mixed, axis=0).T.astype(BF)
    put_lse(lse_ref, lses)


def distance_sums(near, far):
    key_id = lax.broadcasted_iota(jnp.int32, (HALF, HALF), 0)
    query_id = lax.broadcasted_iota(jnp.int32, (HALF, HALF), 1)
    close = (query_id - key_id + HALF) < REACH
    both = near + jnp.where(close, far, 0.0)
    group = both[:8]
    for first in range(8, HALF, 8):
        group = group + pltpu.roll(both[first : first + 8], HALF - first, 1)
    row_id = lax.broadcasted_iota(jnp.int32, (8, HALF), 0)
    turned = group
    for row in range(1, 8):
        turned = jnp.where(row_id == row, pltpu.roll(group, HALF - row, 1), turned)
    by_distance = jnp.sum(turned, axis=0, keepdims=True)
    rest = jnp.sum(jnp.where(close, 0.0, far), axis=0, keepdims=True)
    return jnp.where(row_id == 0, by_distance, jnp.where(row_id == 1, rest, 0.0))


def self_backward_kernel(
    q_ref, k_ref, v_ref, tiles_ref, o_ref, do_ref, lse_ref,
    dqkv_ref, sums_ref, k_ext, v_ext, near_ref, far_ref,
):
    row_ext = jnp.ones((TGT_LEN, LANES), BF)
    k_ext[:, :LANES] = k_ref[...]
    k_ext[:, LANES:] = row_ext
    v_ext[:, :LANES] = v_ref[...]
    v_ext[:, LANES:] = row_ext
    k_t = k_ref[...].T
    q = q_ref[...]
    d_o = do_ref[...]
    q_t = q.T
    do_t = d_o.T
    centre_t = (o_ref[...].astype(F32) * d_o.astype(F32)).T
    first = pl.program_id(1) == 0
    dq, dk, dv = [], [], []
    for head in range(2):
        rows = slice(head * HEAD_DIM, (head + 1) * HEAD_DIM)
        lse = lse_ref[0, head : head + 1, :]
        centre = jnp.sum(centre_t[rows], axis=0, keepdims=True)
        query = jnp.concatenate(
            [head_rows(q_t, head), extra_rows(TGT_LEN, 0.0, three_parts(-lse))], axis=0
        )
        grad = jnp.concatenate(
            [head_rows(do_t, head), extra_rows(TGT_LEN, 0.0, three_parts(-centre))], axis=0
        )
        near, far = tiles_ref[head, 0], tiles_ref[head, 1]
        raw0 = nn(k_ext[:HALF, :], query[:, :HALF])
        raw1 = nn(k_ext[...], query[:, HALF:])
        p00 = jnp.exp(raw0 + near)
        p10 = jnp.exp(raw1[:HALF] + far)
        p11 = jnp.exp(raw1[HALF:] + near)
        g0 = nn(v_ext[:HALF, :], grad[:, :HALF])
        g1 = nn(v_ext[...], grad[:, HALF:])
        s00 = p00 * g0
        s10 = p10 * g1[:HALF]
        s11 = p11 * g1[HALF:]
        near_sum, far_sum = s00 + s11, s10

        @pl.when(first)
        def _():
            near_ref[head] = near_sum
            far_ref[head] = far_sum

        @pl.when(jnp.logical_not(first))
        def _():
            sums_ref[head] = distance_sums(near_ref[head] + near_sum, far_ref[head] + far_sum)

        b00, b10, b11 = s00.astype(BF), s10.astype(BF), s11.astype(BF)
        w00, w10, w11 = p00.astype(BF), p10.astype(BF), p11.astype(BF)
        top = jnp.concatenate([w00, w10], axis=1)
        dv.append(jnp.concatenate([nn(top, d_o), nn(w11, d_o[HALF:])], axis=0))
        top = jnp.concatenate([b00, b10], axis=1)
        dk.append(jnp.concatenate([nn(top, q), nn(b11, q[HALF:])], axis=0))
        dq.append(
            jnp.concatenate(
                [
                    nn(k_t[rows, :HALF], b00),
                    nn(k_t[rows], jnp.concatenate([b10, b11], axis=0)),
                ],
                axis=1,
            )
        )
    dqkv_ref[0] = jnp.concatenate(dq, axis=0).T.astype(BF)
    lane = lax.broadcasted_iota(jnp.int32, (TGT_LEN, LANES), 1)
    dqkv_ref[1] = jnp.where(lane < HEAD_DIM, dk[0], dk[1]).astype(BF)
    dqkv_ref[2] = jnp.where(lane < HEAD_DIM, dv[0], dv[1]).astype(BF)


PAIR_GRID = (MICRO, PAIRS)


def pair_block(rows, offset=0):
    return pl.BlockSpec((rows, LANES), lambda m, p: (m, p + offset))


LSE_BLOCK = pl.BlockSpec((1, 8, TGT_LEN), lambda m, p: (m * PAIRS + p, 0, 0))
LSE_SHAPE = jax.ShapeDtypeStruct((MICRO * PAIRS, 8, TGT_LEN), F32)
MASK_BLOCK = pl.BlockSpec((1, KEYS, LANES), lambda m, p: (m, 0, 0))


def cross_forward(small, q, kv_own, kv_next, mask):
    return pl.pallas_call(
        cross_forward_kernel,
        grid=PAIR_GRID,
        in_specs=[
            SMEM,
            pair_block(TGT_LEN),
            pair_block(OWN),
            pair_block(NEXT),
            pair_block(OWN, PAIRS),
            pair_block(NEXT, PAIRS),
            MASK_BLOCK,
        ],
        out_specs=[pair_block(TGT_LEN), LSE_BLOCK],
        out_shape=[jax.ShapeDtypeStruct((ROWS, D), BF), LSE_SHAPE],
        scratch_shapes=[pltpu.VMEM((KEYS, 2 * LANES), BF)],
        compiler_params=params(),
        cost_estimate=cost(32),
        name="cross_forward",
    )(small, q, kv_own, kv_next, kv_own, kv_next, mask)


def cross_backward(m, q, kv_own, kv_next, mask, o, d_o, lse):
    def block(rows, offset=0):
        return pl.BlockSpec((rows, LANES), lambda p: (m, p + offset))

    return pl.pallas_call(
        cross_backward_kernel,
        grid=(PAIRS,),
        in_specs=[
            block(TGT_LEN),
            block(OWN),
            block(NEXT),
            block(OWN, PAIRS),
            block(NEXT, PAIRS),
            pl.BlockSpec((1, KEYS, LANES), lambda p: (m, 0, 0)),
            block(TGT_LEN),
            block(TGT_LEN),
            pl.BlockSpec((1, 8, TGT_LEN), lambda p: (m * PAIRS + p, 0, 0)),
        ],
        out_specs=[
            pl.BlockSpec((TGT_LEN, LANES), lambda p: (0, p)),
            pl.BlockSpec((2, OWN, LANES), lambda p: (0, 0, p)),
            pl.BlockSpec((2, NEXT, LANES), lambda p: (0, 0, p)),
        ],
        out_shape=[
            shape(TGT_LEN, D),
            jax.ShapeDtypeStruct((2, OWN, D), BF),
            jax.ShapeDtypeStruct((2, NEXT, D), BF),
        ],
        scratch_shapes=[pltpu.VMEM((KEYS, 2 * LANES), BF)] * 2,
        compiler_params=params(),
        cost_estimate=cost(22),
        name="cross_backward",
    )(*map(far, (q, kv_own, kv_next, kv_own, kv_next, mask, o, d_o, lse)))


def swapped(spec):
    index = spec.index_map
    return pl.BlockSpec(spec.block_shape, lambda p, m: index(m, p))


TILE_BLOCK = pl.BlockSpec((2, 2, HALF, HALF), lambda p, m: (p, 0, 0, 0))


def self_forward(qkv, tiles):
    return pl.pallas_call(
        self_forward_kernel,
        grid=(PAIRS, MICRO),
        in_specs=[
            swapped(pair_block(TGT_LEN)),
            swapped(pair_block(TGT_LEN, PAIRS)),
            swapped(pair_block(TGT_LEN, 2 * PAIRS)),
            TILE_BLOCK,
        ],
        out_specs=[swapped(pair_block(TGT_LEN)), swapped(LSE_BLOCK)],
        out_shape=[jax.ShapeDtypeStruct((ROWS, D), BF), LSE_SHAPE],
        compiler_params=params(),
        cost_estimate=cost(17),
        name="self_forward",
    )(qkv, qkv, qkv, tiles)


def self_backward(qkv, tiles, o, d_o, lse):
    sums = jax.ShapeDtypeStruct((HEADS, 8, HALF), F32)
    return pl.pallas_call(
        self_backward_kernel,
        grid=(PAIRS, MICRO),
        in_specs=[
            swapped(pair_block(TGT_LEN)),
            swapped(pair_block(TGT_LEN, PAIRS)),
            swapped(pair_block(TGT_LEN, 2 * PAIRS)),
            TILE_BLOCK,
            swapped(pair_block(TGT_LEN)),
            swapped(pair_block(TGT_LEN)),
            swapped(LSE_BLOCK),
        ],
        out_specs=[
            pl.BlockSpec((3, TGT_LEN, LANES), lambda p, m: (0, m, p)),
            pl.BlockSpec((2, 8, HALF), lambda p, m: (p, 0, 0)),
        ],
        out_shape=[jax.ShapeDtypeStruct((3, ROWS, D), BF), sums],
        scratch_shapes=[pltpu.VMEM((TGT_LEN, 2 * LANES), BF)] * 2
        + [pltpu.VMEM((2, HALF, HALF), F32)] * 2,
        compiler_params=params(),
        cost_estimate=cost(24),
        name="self_backward",
    )(qkv, qkv, qkv, tiles, o, d_o, lse)


def key_masks(offsets_row, position):
    shard_ids = jnp.arange(offsets_row.shape[0], dtype=jnp.int32)
    own_start = jnp.sum(jnp.where(shard_ids == position, offsets_row, 0))
    next_start = jnp.sum(jnp.where(shard_ids == position + 1, offsets_row, 0))
    own_valid = jnp.arange(MEM_DEV - OWN, MEM_DEV, dtype=jnp.int32) >= own_start
    next_valid = jnp.arange(NEXT, dtype=jnp.int32) < next_start
    valid = jnp.concatenate([own_valid, next_valid])[:, None]
    lane = jnp.arange(LANES, dtype=jnp.int32)[None, :]
    return jnp.where((lane == 0), jnp.where(valid, 0.0, MASKED), 1.0).astype(BF)


def passed_along(block, distance):
    devices = range(lax.axis_size("seq"))
    route = [(i - distance, i) for i in devices if i - distance in devices]
    return lax.ppermute(block, "seq", route)


def device_bits():
    bits = []
    for axis in AXES:
        count = lax.axis_size(axis).bit_length() - 1
        bits += [(axis, place) for place in reversed(range(count))]
    return bits


def bit_groups():
    bits = device_bits()
    core = ("dp", 0)
    low = (lax.axis_size("seq").bit_length() - 1) // 2
    plane = [b for b in bits if b != core and (b[0] == "dp" or b[1] < low)]
    column = [b for b in bits if b[0] == "seq" and b[1] >= low]
    return [core], plane, column


def mine(bit):
    axis, place = bit
    return (lax.axis_index(axis) >> place) & 1


def flips(group):
    for mask in range(1, 1 << len(group)):
        yield [(mask >> place) & 1 for place in range(len(group))]


def exchange(block, group, flip):
    mask = 0
    for (axis, place), turned in zip(group, flip):
        stride = lax.axis_size("seq") if axis == "dp" else 1
        mask ^= turned * stride << place
    count = lax.axis_size("dp") * lax.axis_size("seq")
    return lax.ppermute(block, AXES, [(i, i ^ mask) for i in range(count)])


def gather_stage(held, dims, group, fillers=()):
    order = device_bits()
    joined = sorted(dims + group, key=order.index)
    tail = held.shape[len(dims) :]
    spot = tuple(1 if bit in group else 2 for bit in joined) + tail
    turns = [[0] * len(group)] + list(flips(group))
    pieces = [held] + [exchange(held, group, flip) for flip in turns[1:]]
    pieces, fillers = tied(pieces, fillers)
    result = jnp.zeros((2,) * len(joined) + tail, held.dtype)
    for flip, piece in zip(turns, pieces):
        start = [mine(bit) ^ flip[group.index(bit)] if bit in group else 0 for bit in joined]
        result = lax.dynamic_update_slice(result, piece.reshape(spot), start + [0] * len(tail))
    return result, joined, fillers


def paired_halves(shard, core):
    halves = shard.reshape(shard.shape[0], 2, -1)
    here = lax.dynamic_index_in_dim(halves, core, 1, keepdims=False)
    there = lax.dynamic_index_in_dim(halves, 1 - core, 1, keepdims=False)
    received = exchange(there, bit_groups()[0], [1])
    return jnp.stack([jnp.where(core == 0, here, received), jnp.where(core == 0, received, here)])


def both_halves(held):
    own = held.reshape(-1, held.shape[-1])
    return own, exchange(own, bit_groups()[0], [1])


def gather_bits(held, dims, group):
    for bit in reversed(group):
        held, dims, _ = gather_stage(held, dims, [bit])
    return held, dims, ()


def tree_sum(terms):
    terms = [term.astype(F32) for term in terms]
    while len(terms) > 1:
        terms = [
            terms[place] + terms[place + 1] if place + 1 < len(terms) else terms[place]
            for place in range(0, len(terms), 2)
        ]
    return terms[0]


def picked(array, dims, group, flip):
    left = list(dims)
    for bit, turned in zip(group, flip):
        place = left.index(bit)
        left.remove(bit)
        array = lax.dynamic_index_in_dim(array, mine(bit) ^ turned, place, keepdims=False)
    return array


def scatter_parts(bundles, dims, group):
    def part(flip):
        sums = [
            tree_sum([picked(term, dims, group, flip) for term in terms]).astype(BF)
            for terms in bundles
        ]
        return jnp.concatenate(sums, axis=-1) if len(sums) > 1 else sums[0]

    return [part([0] * len(group))] + [part(flip) for flip in flips(group)]


def scattered(parts, group):
    sent = [exchange(part, group, flip) for part, flip in zip(parts[1:], flips(group))]
    return parts[:1] + sent


def core_stage(give, keep):
    core, _, _ = bit_groups()
    dims = [bit for bit in device_bits() if bit not in core]
    received = exchange(give, core, [1])
    split = (2,) * len(dims) + (give.shape[0] * give.shape[1] >> len(dims), give.shape[2])
    return [keep.reshape(split), received.reshape(split)]


def without(dims, group):
    return [bit for bit in dims if bit not in group]


def passed_along(block, distance):
    devices = range(lax.axis_size("seq"))
    route = [(i - distance, i) for i in devices if i - distance in devices]
    return lax.ppermute(block, "seq", route)


def ffn_grads(h3, acts, dy, later):
    devices = lax.axis_size("dp") * lax.axis_size("seq")
    width = acts.shape[2]
    if D // devices % 8 or width // devices % 16:
        total = [
            lax.psum_scatter(
                lax.dot_general(
                    rows, grads, (((0,), (0,)), ((), ())), preferred_element_type=F32
                ),
                AXES,
                scatter_dimension=0,
                tiled=True,
            )
            for rows, grads in ((h3, acts[0]), (h3, acts[1]), (acts[2], dy))
        ]
        return total, later
    partial = ffn_weight_grads(h3, acts, dy, devices)
    later, partial = tied(later, partial)
    return lax.psum_scatter(partial, AXES, scatter_dimension=0, tiled=True), later


def ffn_columns(total, share, width):
    if isinstance(total, (list, tuple)):
        return total
    total = total[0].astype(F32)
    rows = share * width // WIDE

    def columns(first, height):
        block = total[first : first + rows].reshape(-1, height, WIDE)
        return block.transpose(1, 0, 2).reshape(height, -1)

    return columns(0, share), columns(rows, share), columns(2 * rows, rows * WIDE // D)


def tied(values, parts):
    values, parts = lax.optimization_barrier((values, parts))
    return values, parts


def local(
    decoder_in,
    memory,
    doc_offsets,
    self_query,
    self_key,
    self_value,
    self_out,
    cross_query,
    cross_key,
    cross_value,
    cross_out,
    ffn_gate,
    ffn_up,
    ffn_down,
    norm_self,
    norm_cross,
    norm_ffn,
    bias_table,
    cotangent,
):
    position = lax.axis_index("seq")
    core = lax.axis_index("dp") & 1
    core_id = core.reshape(1).astype(jnp.int32)
    across = lax.axis_size("dp") // 2
    share = self_query.shape[0]
    core_bits, plane, column = bit_groups()

    gains = jnp.stack([norm_self, norm_cross, norm_ffn], axis=1)
    gains = jnp.pad(gains, ((0, 0), (0, 2 * LANES - 3)))
    first = jnp.concatenate(
        [cross_key, cross_value, self_query, self_key, self_value, gains], axis=1
    )
    second = jnp.concatenate([self_out, cross_query], axis=1)
    late = jnp.concatenate([cross_out, ffn_gate, ffn_up], axis=1)
    first = paired_halves(first, core)
    first, dims, _ = gather_stage(first, core_bits, column)
    first, second, ffn_down, doc_offsets, memory, bias_table = lax.optimization_barrier(
        (first, second, ffn_down, doc_offsets, memory, bias_table)
    )
    second = paired_halves(second, core)
    third = paired_halves(ffn_down, core)
    tiles = bias_tiles(bias_table.astype(F32))
    mask = jnp.stack([key_masks(doc_offsets[m, 0], position) for m in range(MICRO)])
    next_rows = memory[:, 0, :NEXT]
    narrow = second.reshape(2, 2 * share, -1)
    second, _, _ = gather_bits(jnp.concatenate([narrow, third], axis=1), core_bits, column)
    first, _, (second, tiles, mask, next_rows, late) = gather_stage(
        first, dims, plane, (second, tiles, mask, next_rows, late)
    )
    third = second[..., 2 * share :, :]
    second = second[..., : 2 * share, :].reshape(third.shape[:-2] + (share, D))
    own, other = both_halves(first)
    late = lax.all_gather(late, AXES, axis=0, tiled=True)
    x = decoder_in.reshape(ROWS, D)
    dy = cotangent.reshape(ROWS, D)
    mem = memory.reshape(MICRO * MEM_DEV, D)
    next_rows = passed_along(next_rows, -1).reshape(MICRO * NEXT, D)

    x, second = tied(x, second)
    h1, qkv, gains = self_inputs(core_id, own, other, x)
    o1, lse1 = self_forward(qkv, tiles)
    mem, o1 = tied(mem, o1)
    kv_own, own_size = key_value(
        core_id, own, other, mem, MICRO * OWN // BLOCK, lambda i: (i + i // 3 + 1, 0), 6
    )
    second, _, (o1, kv_own, next_rows) = gather_stage(
        second, dims, plane, (o1, kv_own, next_rows)
    )
    own_b, other_b = both_halves(second)
    next_rows, third, own_b = lax.optimization_barrier((next_rows, third, own_b))
    kv_next, next_size = key_value(
        core_id, own, other, next_rows, MICRO * NEXT // BLOCK, lambda i: (i, 0), 4
    )
    o1, kv_next = tied(o1, kv_next)
    x1, h2, q2, query_size = cross_inputs(core_id, own_b, other_b, gains, x, o1)
    largest = jnp.max(query_size[:1] * jnp.maximum(own_size[:1], next_size[:1]))
    small = (largest <= SMALL_SCORE**2).astype(jnp.int32).reshape(1)
    o2, lse2 = cross_forward(small, q2, kv_own, kv_next, mask)
    third, _, o2 = gather_stage(third, dims, plane, o2)
    own_c, other_c = both_halves(third)
    out, h3, acts, db2, dx2, do2, g_norm_ffn = ffn(
        core_id, late, own_c, other_c, gains, x1, o2, dy
    )
    ffn_total, do2 = ffn_grads(h3, acts, dy, do2)
    dims = without(device_bits(), core_bits)
    arguments = (q2, kv_own, kv_next, mask, o2, do2, lse2)
    results, arrived = [], []
    for m in range(MICRO):
        dq_m, own_m, next_m = cross_backward(m, *arguments)
        dm_m = memory_grads(core_id, own, other, next_m)
        if m + 1 < MICRO:
            arguments, dm_m = tied(arguments, dm_m)
        results.append((dq_m, own_m, next_m))
        if arrived:
            dm_m, arrived[-1] = tied(dm_m, arrived[-1])
        arrived.append(passed_along(dm_m, 1))
    dq2, dkv_own, dkv_next = zip(*results)
    dkv_own, dkv_next, dm_m = lax.optimization_barrier((dkv_own, dkv_next, dm_m))
    pair_terms = core_stage(*pair_grads(core_id, [(o2, (db2,)), (h2, dq2)], across))
    give, keep = memory_weight_grads(core_id, memory, next_rows, dkv_own, dkv_next, across)
    dq2, give = tied(dq2, give)
    memory_terms = core_stage(give, keep)
    dx1, db1, do1, g_norm_cross = self_grads(core_id, own_b, other_b, gains, x1, dx2, dq2)
    (db1, do1), pair_terms, memory_terms = lax.optimization_barrier(
        ((db1, do1), pair_terms, memory_terms)
    )
    out_terms = core_stage(*pair_grads(core_id, [(o1, (db1,))], across))
    cross_parts = scatter_parts([pair_terms, memory_terms, out_terms], dims, plane)
    do1, cross_parts = tied(do1, cross_parts)
    cross_terms = scattered(cross_parts, plane)
    dqkv, sums = self_backward(qkv, tiles, o1, do1, lse1)
    dqkv, arrived[-1] = tied(dqkv, arrived[-1])
    give, keep = row_grads(core_id, h1, dqkv, across, 5)
    dqkv, give, cross_terms = lax.optimization_barrier((dqkv, give, cross_terms))
    self_terms = core_stage(give, keep)
    left = without(dims, plane)
    high, low = column[:1], column[1:]
    cross_parts = scatter_parts([cross_terms], left, high)
    dqkv, cross_parts = tied(dqkv, cross_parts)
    cross_terms = scattered(cross_parts, high)
    grad_decoder, g_norm_self = input_grads(core_id, own, other, gains, x, dx1, dqkv)
    g_norm_self, cross_terms, self_terms = lax.optimization_barrier(
        (g_norm_self, cross_terms, self_terms)
    )
    self_parts = scatter_parts([self_terms], dims, plane)
    cross_parts = scatter_parts([cross_terms], low, low)
    give, keep = extras(core_id, sums, [g_norm_self, g_norm_cross, g_norm_ffn], across, share)
    dkv_own, cross_parts, self_parts, give = lax.optimization_barrier(
        (dkv_own, cross_parts, self_parts, give)
    )
    self_terms = scattered(self_parts, plane)
    extra_terms = core_stage(give, keep)
    cross_terms = scattered(cross_parts, low)
    totals = [memory_total(core_id, own, other, dkv_own[0], arrived[0])]
    totals[0], extra_terms = tied(totals[0], extra_terms)
    extra_left = list(dims)
    for bit in plane:
        extra_parts = scatter_parts([extra_terms], extra_left, [bit])
        extra_left.remove(bit)
        if len(totals) == 1:
            dkv_own, extra_parts = tied(dkv_own, extra_parts)
        extra_terms = scattered(extra_parts, [bit])
        if len(totals) == 1:
            totals.append(memory_total(core_id, own, other, dkv_own[1], arrived[1]))
            totals[1], extra_terms = tied(totals[1], extra_terms)
    totals, self_terms, extra_terms = lax.optimization_barrier((totals, self_terms, extra_terms))
    self_parts = scatter_parts([self_terms, extra_terms], left, column)
    self_parts, cross_terms, ffn_total = lax.optimization_barrier(
        (self_parts, cross_terms, ffn_total)
    )
    g_self = tree_sum(scattered(self_parts, column))
    g_cross = tree_sum(cross_terms)
    grad_memory = jnp.stack(totals)
    g_gate, g_up, g_down = ffn_columns(ffn_total, share, ffn_gate.shape[1])

    table = g_self[: HEADS * BUCKETS // LANES, 3 * D + LANES :].reshape(HEADS, BUCKETS)

    def cut(stack, index):
        return stack[:, index * D : (index + 1) * D]

    return (
        out.reshape(decoder_in.shape),
        grad_decoder.reshape(decoder_in.shape),
        grad_memory.reshape(memory.shape),
        cut(g_self, 0),
        cut(g_self, 1),
        cut(g_self, 2),
        cut(g_cross, 4),
        cut(g_cross, 1),
        cut(g_cross, 2),
        cut(g_cross, 3),
        cut(g_cross, 0),
        g_gate,
        g_up,
        g_down,
        g_self[:, 3 * D],
        g_self[:, 3 * D + 1],
        g_self[:, 3 * D + 2],
        table,
    )


def solution(mesh):
    in_specs = (
        P(None, ("dp", "seq"), None, None),
        P(None, ("dp", "seq"), None, None),
        P(None, "dp", None),
        P(("dp", "seq"), None),
        P(("dp", "seq"), None),
        P(("dp", "seq"), None),
        P(("dp", "seq"), None),
        P(("dp", "seq"), None),
        P(("dp", "seq"), None),
        P(("dp", "seq"), None),
        P(("dp", "seq"), None),
        P(("dp", "seq"), None),
        P(("dp", "seq"), None),
        P(("dp", "seq"), None),
        P(("dp", "seq")),
        P(("dp", "seq")),
        P(("dp", "seq")),
        P(),
        P(None, ("dp", "seq"), None, None),
    )
    out_specs = (
        P(None, ("dp", "seq"), None, None),
        P(None, ("dp", "seq"), None, None),
        P(None, ("dp", "seq"), None, None),
        P(("dp", "seq"), None),
        P(("dp", "seq"), None),
        P(("dp", "seq"), None),
        P(("dp", "seq"), None),
        P(("dp", "seq"), None),
        P(("dp", "seq"), None),
        P(("dp", "seq"), None),
        P(("dp", "seq"), None),
        P(("dp", "seq"), None),
        P(("dp", "seq"), None),
        P(("dp", "seq"), None),
        P(("dp", "seq")),
        P(("dp", "seq")),
        P(("dp", "seq")),
        P(),
    )
    return jax.shard_map(local, mesh=mesh, in_specs=in_specs, out_specs=out_specs, check_vma=False)
```

```python
import functools
import math

import jax
import jax.numpy as jnp
from jax import lax
from jax.experimental import pallas as pl
from jax.experimental.pallas import tpu as pltpu
from jax.sharding import PartitionSpec as P

D = 768
HEADS = 12
HEAD_DIM = 64
BUCKETS = 32
REACH = 128
TGT_LEN = 512
MEM_DEV = 1024
MICRO = 2
PAIRS = HEADS // 2
LANES = 2 * HEAD_DIM
OWN = MEM_DEV - MEM_DEV // 4
NEXT = MEM_DEV // 2
KEYS = OWN + NEXT
HALF = 256
MASKED = -1e30
NORM_EPS = 1e-06
AXES = ("dp", "seq")
ROWS = MICRO * TGT_LEN
BLOCK = 256
WIDE = 256
SMALL_SCORE = 59.0
FFN_CHUNK = 1024
HALF_COLUMNS = 2048
VMEM_LIMIT = 52 * 1024 * 1024
BF = jnp.bfloat16
F32 = jnp.float32


def nn(a, b):
    return lax.dot_general(a, b, (((1,), (0,)), ((), ())), preferred_element_type=F32)


def bucket_limits(buckets, reach):
    exact_count = buckets // 2
    limits = []
    for target in range(exact_count + 1, buckets):
        distance = exact_count
        while (
            exact_count
            + int(
                math.log(distance / exact_count)
                / math.log(reach / exact_count)
                * (buckets - exact_count)
            )
            < target
        ):
            distance += 1
        limits.append(distance)
    return limits


def three_parts(row):
    high = row.astype(BF).astype(F32)
    rest = row - high
    middle = rest.astype(BF).astype(F32)
    return high, middle, rest - middle


def extra_rows(columns, first, parts):
    row_id = lax.broadcasted_iota(jnp.int32, (LANES, columns), 0)
    grid = jnp.where(row_id == 0, first, 0.0)
    for place, part in enumerate(parts):
        grid = jnp.where(row_id == place + 1, part, grid)
    return grid.astype(BF)


def head_rows(stacked, head):
    row_id = lax.broadcasted_iota(jnp.int32, stacked.shape, 0)
    return jnp.where((row_id // HEAD_DIM) == head, stacked, jnp.zeros_like(stacked))


def far(array):
    return pltpu.with_memory_space_constraint(array, pltpu.HBM)


def nt(a, b):
    return lax.dot_general(a, b, (((1,), (1,)), ((), ())), preferred_element_type=F32)


def params(**options):
    return pltpu.CompilerParams(vmem_limit_bytes=VMEM_LIMIT, **options)


def cost(us):
    return pl.CostEstimate(flops=int(us), bytes_accessed=0, transcendentals=0)


def shape(rows, columns, kind=BF):
    return jax.ShapeDtypeStruct((rows, columns), kind)


def row_block(columns, rows=BLOCK):
    return pl.BlockSpec((rows, columns), lambda i: (i, 0))


def fixed_block(rows, columns):
    return pl.BlockSpec((rows, columns), lambda i: (0, 0))


ANY = pl.BlockSpec(memory_space=pl.ANY)
SMEM = pl.BlockSpec(memory_space=pltpu.SMEM)


def halves_loaded(core_ref, own_ref, other_ref, pieces, sems):
    @pl.when(pl.program_id(0) == 0)
    def _():
        for side in range(2):

            @pl.when(core_ref[0] == side)
            def _():
                halves = (own_ref, other_ref) if side == 0 else (other_ref, own_ref)
                copies = [
                    pltpu.make_async_copy(halves[half].at[:, source], target, sems.at[place])
                    for place, (half, source, target) in enumerate(pieces)
                ]
                for copy in copies:
                    copy.start()
                for copy in copies:
                    copy.wait()


def key_value_pieces(w_kv):
    return [(0, slice(0, 2 * D), w_kv)]


def out_query_pieces(weights):
    return [(side, slice(0, D), weights.at[:, side * D : (side + 1) * D]) for side in range(2)]


def query_pieces(w_qkv):
    cut = HALF_COLUMNS - 2 * D
    return [
        (0, slice(2 * D, HALF_COLUMNS), w_qkv.at[:, :cut]),
        (1, slice(0, 3 * D - cut), w_qkv.at[:, cut:]),
    ]


def normed(values, gain):
    inverse = lax.rsqrt(jnp.mean(values * values, axis=-1, keepdims=True) + NORM_EPS)
    scaled = values * inverse
    return scaled, inverse, (scaled * gain).astype(BF)


def norm_back(values, gain, grads, gain_grad_ref):
    inverse = lax.rsqrt(jnp.mean(values * values, axis=-1, keepdims=True) + NORM_EPS)
    scaled = values * inverse
    add_rows(gain_grad_ref, jnp.sum(scaled * grads, axis=0, keepdims=True))
    weighted = grads * gain
    centre = jnp.mean(scaled * weighted, axis=-1, keepdims=True)
    return inverse * (weighted - scaled * centre)


def add_rows(total_ref, row):
    row_id = lax.broadcasted_iota(jnp.int32, (8, D), 0)
    addend = jnp.where(row_id == 0, row, 0.0)

    @pl.when(pl.program_id(0) == 0)
    def _():
        total_ref[...] = addend

    @pl.when(pl.program_id(0) > 0)
    def _():
        total_ref[...] += addend


def keep_largest(total_ref, values):
    head = lax.broadcasted_iota(jnp.int32, (D, LANES), 0) // HEAD_DIM
    lane = lax.broadcasted_iota(jnp.int32, (D, LANES), 1)
    hot = jnp.where(head == lane, 1.0, 0.0).astype(BF)
    values = values.astype(F32)
    squares = nn((values * values).astype(BF), hot)
    row = jnp.broadcast_to(jnp.max(squares, axis=0, keepdims=True), (8, LANES))

    @pl.when(pl.program_id(0) == 0)
    def _():
        total_ref[...] = row

    @pl.when(pl.program_id(0) > 0)
    def _():
        total_ref[...] = jnp.maximum(total_ref[...], row)


def key_value_kernel(core_ref, own_ref, other_ref, rows_ref, kv_ref, size_ref, w_kv, sems):
    halves_loaded(core_ref, own_ref, other_ref, key_value_pieces(w_kv), sems)
    kv_ref[...] = nn(rows_ref[...], w_kv[...]).astype(BF)
    keep_largest(size_ref, kv_ref[:, :D])


def key_value(core, own, other, rows, steps, index, us):
    return pl.pallas_call(
        key_value_kernel,
        grid=(steps,),
        in_specs=[SMEM, ANY, ANY, pl.BlockSpec((BLOCK, D), index)],
        out_specs=[row_block(2 * D), fixed_block(8, LANES)],
        out_shape=[shape(steps * BLOCK, 2 * D), shape(8, LANES, F32)],
        scratch_shapes=[pltpu.VMEM((D, 2 * D), BF), pltpu.SemaphoreType.DMA((1,))],
        compiler_params=params(),
        cost_estimate=cost(us),
        name="key_value",
    )(core, own, other, rows)


def self_inputs_kernel(
    core_ref, own_ref, other_ref, x_ref, h_ref, qkv_ref, gains_ref, w_qkv, gain_columns, sems
):
    first_gain = 5 * D - HALF_COLUMNS
    pieces = query_pieces(w_qkv)
    pieces.append((1, slice(first_gain, first_gain + LANES), gain_columns))
    halves_loaded(core_ref, own_ref, other_ref, pieces, sems)

    @pl.when(pl.program_id(0) == 0)
    def _():
        gains_ref[...] = gain_columns[...].astype(F32).T[:8]

    h_ref[...] = normed(x_ref[...].astype(F32), gains_ref[:1, :])[2]
    qkv_ref[...] = nn(h_ref[...], w_qkv[...]).astype(BF)


def self_inputs(core, own, other, x):
    return pl.pallas_call(
        self_inputs_kernel,
        grid=(ROWS // BLOCK,),
        in_specs=[SMEM, ANY, ANY, row_block(D)],
        out_specs=[row_block(D), row_block(3 * D), fixed_block(8, D)],
        out_shape=[shape(ROWS, D), shape(ROWS, 3 * D), shape(8, D, F32)],
        scratch_shapes=[
            pltpu.VMEM((D, 3 * D), BF),
            pltpu.VMEM((D, LANES), BF),
            pltpu.SemaphoreType.DMA((3,)),
        ],
        compiler_params=params(),
        cost_estimate=cost(6),
        name="self_inputs",
    )(core, own, other, x)


def cross_inputs_kernel(
    core_ref, own_ref, other_ref, gain_ref, x_ref, o_ref,
    x1_ref, h_ref, q_ref, size_ref, weights, sems,
):
    halves_loaded(core_ref, own_ref, other_ref, out_query_pieces(weights), sems)
    x1 = x_ref[...].astype(F32) + nn(o_ref[...], weights[:, :D])
    x1_ref[...] = x1
    h_ref[...] = normed(x1, gain_ref[1:2, :])[2]
    q_ref[...] = nn(h_ref[...], weights[:, D:]).astype(BF)
    keep_largest(size_ref, q_ref[...])


def cross_inputs(core, own, other, gain, x, o1):
    return pl.pallas_call(
        cross_inputs_kernel,
        grid=(ROWS // BLOCK,),
        in_specs=[SMEM, ANY, ANY, fixed_block(8, D), row_block(D), row_block(D)],
        out_specs=[row_block(D)] * 3 + [fixed_block(8, LANES)],
        out_shape=[shape(ROWS, D, F32), shape(ROWS, D), shape(ROWS, D), shape(8, LANES, F32)],
        scratch_shapes=[pltpu.VMEM((D, 2 * D), BF), pltpu.SemaphoreType.DMA((2,))],
        compiler_params=params(),
        cost_estimate=cost(5),
        name="cross_inputs",
    )(core, own, other, gain, x, o1)


def ffn_kernel(
    core_ref, late_ref, own_ref, other_ref, gain_ref, x1_ref, o_ref, dy_ref,
    out_ref, h_ref, acts_ref, db_ref, dx_ref, do_ref, gain_grad_ref,
    w_out, w_gate, w_up, w_down, sems,
):
    width = w_gate.shape[1]
    first = pl.program_id(0) == 0
    copies = [
        pltpu.make_async_copy(late_ref.at[:, :D], w_out, sems.at[0]),
        pltpu.make_async_copy(late_ref.at[:, D : D + width], w_gate, sems.at[1]),
        pltpu.make_async_copy(late_ref.at[:, D + width :], w_up, sems.at[2]),
    ]

    def down_copies(side):
        halves = (own_ref, other_ref) if side == 0 else (other_ref, own_ref)
        columns = [slice(half * D // 2, (half + 1) * D // 2) for half in range(2)]
        return [
            pltpu.make_async_copy(halves[half], w_down.at[:, columns[half]], sems.at[3 + half])
            for half in range(2)
        ]

    @pl.when(first)
    def _():
        for copy in copies:
            copy.start()
        for side in range(2):

            @pl.when(core_ref[0] == side)
            def _():
                for copy in down_copies(side):
                    copy.start()

    def arrived(place):
        @pl.when(first)
        def _():
            copies[place].wait()

    arrived(0)
    x2 = x1_ref[...] + nn(o_ref[...], w_out[...])
    h_ref[...] = normed(x2, gain_ref[2:3, :])[2]
    dy_low = dy_ref[...]
    arrived(1)
    arrived(2)

    @pl.when(first)
    def _():
        for side in range(2):

            @pl.when(core_ref[0] == side)
            def _():
                for copy in down_copies(side):
                    copy.wait()

    scale = math.sqrt(2.0 / math.pi)
    out, dh = x2, 0.0
    h = h_ref[...]
    for start in range(0, width, FFN_CHUNK):
        part = slice(start, start + FFN_CHUNK)
        gate = nn(h, w_gate[:, part])
        up = nn(h, w_up[:, part])
        d_hidden = nt(dy_low, w_down[part, :])
        square = gate * gate
        turn = jnp.tanh(gate * (scale + (scale * 0.044715) * square))
        half = 0.5 + 0.5 * turn
        gelu = gate * half
        bend = gate * (0.5 * scale + (0.5 * scale * 3 * 0.044715) * square)
        slope = half + (1.0 - turn * turn) * bend
        hidden = (gelu * up).astype(BF)
        d_gate = (d_hidden * up * slope).astype(BF)
        d_up = (d_hidden * gelu).astype(BF)
        acts_ref[0, :, part] = d_gate
        acts_ref[1, :, part] = d_up
        acts_ref[2, :, part] = hidden
        out = out + nn(hidden, w_down[part, :])
        dh = dh + nt(d_gate, w_gate[:, part]) + nt(d_up, w_up[:, part])
    out_ref[...] = out.astype(BF)
    dx = dy_low.astype(F32) + norm_back(x2, gain_ref[2:3, :], dh, gain_grad_ref)
    dx_ref[...] = dx
    db_ref[...] = dx.astype(BF)
    do_ref[...] = nt(db_ref[...], w_out[...]).astype(BF)


def ffn(core, late, own, other, gain, x1, o2, dy):
    width = own.shape[0]
    return pl.pallas_call(
        ffn_kernel,
        grid=(ROWS // BLOCK,),
        in_specs=[SMEM, ANY, ANY, ANY, fixed_block(8, D), row_block(D), row_block(D), row_block(D)],
        out_specs=[
            row_block(D),
            row_block(D),
            pl.BlockSpec((3, BLOCK, width), lambda i: (0, i, 0)),
            row_block(D),
            row_block(D),
            row_block(D),
            fixed_block(8, D),
        ],
        out_shape=[
            shape(ROWS, D),
            shape(ROWS, D),
            jax.ShapeDtypeStruct((3, ROWS, width), BF),
            shape(ROWS, D),
            shape(ROWS, D, F32),
            shape(ROWS, D),
            shape(8, D, F32),
        ],
        scratch_shapes=[
            pltpu.VMEM((D, D), BF),
            pltpu.VMEM((D, width), BF),
            pltpu.VMEM((D, width), BF),
            pltpu.VMEM((width, D), BF),
            pltpu.SemaphoreType.DMA((5,)),
        ],
        compiler_params=params(),
        cost_estimate=cost(30),
        name="ffn",
    )(core, far(late), far(own), far(other), gain, far(x1), o2, far(dy))


def self_grads_kernel(
    core_ref, own_ref, other_ref, gain_ref, x1_ref, dx2_ref, dq0_ref, dq1_ref,
    dx1_ref, db_ref, do_ref, gain_grad_ref, weights, sems,
):
    halves_loaded(core_ref, own_ref, other_ref, out_query_pieces(weights), sems)
    low = pl.program_id(0) < TGT_LEN // BLOCK
    dh = nt(jnp.where(low, dq0_ref[...], dq1_ref[...]), weights[:, D:])
    dx1 = dx2_ref[...] + norm_back(x1_ref[...], gain_ref[1:2, :], dh, gain_grad_ref)
    dx1_ref[...] = dx1
    db_ref[...] = dx1.astype(BF)
    do_ref[...] = nt(db_ref[...], weights[:, :D]).astype(BF)


def self_grads(core, own, other, gain, x1, dx2, dq2):
    half = TGT_LEN // BLOCK
    return pl.pallas_call(
        self_grads_kernel,
        grid=(ROWS // BLOCK,),
        in_specs=[
            SMEM,
            ANY,
            ANY,
            fixed_block(8, D),
            row_block(D),
            row_block(D),
            pl.BlockSpec((BLOCK, D), lambda i: (jnp.minimum(i, half - 1), 0)),
            pl.BlockSpec((BLOCK, D), lambda i: (jnp.maximum(i - half, 0), 0)),
        ],
        out_specs=[row_block(D), row_block(D), row_block(D), fixed_block(8, D)],
        out_shape=[shape(ROWS, D, F32), shape(ROWS, D), shape(ROWS, D), shape(8, D, F32)],
        scratch_shapes=[pltpu.VMEM((D, 2 * D), BF), pltpu.SemaphoreType.DMA((2,))],
        compiler_params=params(),
        cost_estimate=cost(5),
        name="self_grads",
    )(core, far(own), far(other), gain, far(x1), far(dx2), *dq2)


def input_grads_kernel(
    core_ref, own_ref, other_ref, gain_ref, x_ref, dx1_ref, dqkv_ref,
    dx_ref, gain_grad_ref, w_qkv, sems,
):
    halves_loaded(core_ref, own_ref, other_ref, query_pieces(w_qkv), sems)
    dh = (
        nt(dqkv_ref[0], w_qkv[:, :D])
        + nt(dqkv_ref[1], w_qkv[:, D : 2 * D])
        + nt(dqkv_ref[2], w_qkv[:, 2 * D :])
    )
    x = x_ref[...].astype(F32)
    dx_ref[...] = (dx1_ref[...] + norm_back(x, gain_ref[:1, :], dh, gain_grad_ref)).astype(BF)


def input_grads(core, own, other, gain, x, dx1, dqkv):
    return pl.pallas_call(
        input_grads_kernel,
        grid=(ROWS // BLOCK,),
        in_specs=[
            SMEM, ANY, ANY, fixed_block(8, D), row_block(D), row_block(D),
            pl.BlockSpec((3, BLOCK, D), lambda i: (0, i, 0)),
        ],
        out_specs=[row_block(D), fixed_block(8, D)],
        out_shape=[shape(ROWS, D), shape(8, D, F32)],
        scratch_shapes=[pltpu.VMEM((D, 3 * D), BF), pltpu.SemaphoreType.DMA((2,))],
        compiler_params=params(),
        cost_estimate=cost(6),
        name="input_grads",
    )(core, far(own), far(other), gain, far(x), dx1, dqkv)


def memory_grads_kernel(core_ref, own_ref, other_ref, dkv_ref, dm_ref, w_kv, sems):
    halves_loaded(core_ref, own_ref, other_ref, key_value_pieces(w_kv), sems)
    dm_ref[...] = (nt(dkv_ref[0], w_kv[:, :D]) + nt(dkv_ref[1], w_kv[:, D:])).astype(BF)


def memory_grads(core, own, other, dkv):
    rows = dkv.shape[1]
    return pl.pallas_call(
        memory_grads_kernel,
        grid=(rows // BLOCK,),
        in_specs=[SMEM, ANY, ANY, pl.BlockSpec((2, BLOCK, D), lambda i: (0, i, 0))],
        out_specs=row_block(D),
        out_shape=shape(rows, D),
        scratch_shapes=[pltpu.VMEM((D, 2 * D), BF), pltpu.SemaphoreType.DMA((1,))],
        compiler_params=params(),
        cost_estimate=cost(rows / 400),
        name="memory_grads",
    )(core, own, other, dkv)


def stored_by_core(core_ref, grad, give_ref, keep_ref):
    across, _, count = give_ref.shape[0], 2, give_ref.shape[1]
    for side in range(2):

        @pl.when(core_ref[0] == side)
        def _():
            for place in range(across):
                first = place * 2 * count
                here, there = first + side * count, first + (1 - side) * count
                keep_ref[place] = grad[here : here + count].astype(BF)
                give_ref[place] = grad[there : there + count].astype(BF)


def row_grads_kernel(core_ref, rows_ref, grads_ref, give_ref, keep_ref, turned):
    @pl.when(pl.program_id(0) == 0)
    def _():
        turned[...] = rows_ref[...].T

    stored_by_core(core_ref, nn(turned[...], grads_ref[0]), give_ref, keep_ref)


def row_grads(core, rows, grads, across, us):
    units, length = grads.shape[0], grads.shape[1]
    count = D // (2 * across)
    block = pl.BlockSpec((across, count, D), lambda u: (0, 0, u))
    piece = jax.ShapeDtypeStruct((across, count, units * D), BF)
    return pl.pallas_call(
        row_grads_kernel,
        grid=(units,),
        in_specs=[SMEM, fixed_block(length, D), pl.BlockSpec((1, length, D), lambda u: (u, 0, 0))],
        out_specs=[block, block],
        out_shape=[piece, piece],
        scratch_shapes=[pltpu.VMEM((D, length), BF)],
        compiler_params=params(),
        cost_estimate=cost(us),
        name="row_grads",
    )(core, rows, grads)


def pair_grads_kernel(counts, core_ref, *refs):
    give_ref, keep_ref = refs[-2:]
    used = 0
    for place, count in enumerate(counts):
        turned = refs[used][...].T
        length = turned.shape[1] // count
        grad = sum(
            nn(turned[:, part * length : (part + 1) * length], refs[used + 1 + part][...])
            for part in range(count)
        )
        used += 1 + count
        columns = slice(place * D, (place + 1) * D)
        stored_by_core(core_ref, grad, give_ref.at[:, :, columns], keep_ref.at[:, :, columns])


def pair_grads(core, pairs, across):
    count = D // (2 * across)
    piece = jax.ShapeDtypeStruct((across, count, len(pairs) * D), BF)
    whole = pl.BlockSpec(memory_space=pltpu.VMEM)
    flat = [array for rows, grads in pairs for array in (rows,) + tuple(grads)]
    return pl.pallas_call(
        functools.partial(pair_grads_kernel, [len(grads) for _, grads in pairs]),
        in_specs=[SMEM] + [whole] * len(flat),
        out_specs=[whole, whole],
        out_shape=[piece, piece],
        compiler_params=params(),
        cost_estimate=cost(2.5 * len(pairs)),
        name="pair_grads",
    )(core, *flat)


def ffn_weight_grads_kernel(h_ref, acts_ref, dy_ref, out_ref):
    devices = out_ref.shape[0]
    width = acts_ref.shape[2]

    @pl.when(pl.program_id(0) < 2)
    def _():
        turned = h_ref[...].T
        share = D // devices
        for first in range(0, width, 2 * WIDE):
            both = [
                nn(turned, acts_ref[0, :, place : place + WIDE]).reshape(devices, share, WIDE)
                for place in (first, first + WIDE)
            ]
            row = first // WIDE * share
            out_ref[:, row : row + 2 * share, :] = jnp.concatenate(both, axis=1).astype(BF)

    @pl.when(pl.program_id(0) == 2)
    def _():
        turned = acts_ref[0].T
        share = width // devices
        for place in range(D // WIDE):
            grad = nn(turned, dy_ref[:, place * WIDE : (place + 1) * WIDE])
            out_ref[:, place * share : (place + 1) * share, :] = grad.reshape(
                devices, share, WIDE
            ).astype(BF)


def ffn_weight_grads(h3, acts, dy, devices):
    width = acts.shape[2]
    rows = D * width // WIDE // devices
    return pl.pallas_call(
        ffn_weight_grads_kernel,
        grid=(3,),
        in_specs=[
            fixed_block(ROWS, D),
            pl.BlockSpec((1, ROWS, width), lambda u: (u, 0, 0)),
            fixed_block(ROWS, D),
        ],
        out_specs=pl.BlockSpec((devices, rows, WIDE), lambda u: (0, u, 0)),
        out_shape=jax.ShapeDtypeStruct((devices, 3 * rows, WIDE), BF),
        compiler_params=params(),
        cost_estimate=cost(13),
        name="ffn_weight_grads",
    )(h3, far(acts), far(dy))


def memory_weight_grads_kernel(
    core_ref, mem_ref, next_ref, own0_ref, own1_ref, after0_ref, after1_ref,
    give_ref, keep_ref, turned,
):
    @pl.when(pl.program_id(0) == 0)
    def _():
        for m in range(MICRO):
            turned[:, m * OWN : (m + 1) * OWN] = mem_ref[m, 0, MEM_DEV - OWN :, :].T
        turned[:, MICRO * OWN :] = next_ref[...].T

    grad, used = 0.0, 0
    for part_ref in (own0_ref, own1_ref, after0_ref, after1_ref):
        length = part_ref.shape[1]
        grad = grad + nn(turned[:, used : used + length], part_ref[0])
        used += length
    stored_by_core(core_ref, grad, give_ref, keep_ref)


def memory_weight_grads(core, memory, next_rows, dkv_own, dkv_next, across):
    count = D // (2 * across)
    block = pl.BlockSpec((across, count, D), lambda u: (0, 0, u))
    piece = jax.ShapeDtypeStruct((across, count, 2 * D), BF)
    return pl.pallas_call(
        memory_weight_grads_kernel,
        grid=(2,),
        in_specs=[
            SMEM,
            pl.BlockSpec((MICRO, 1, MEM_DEV, D), lambda u: (0, 0, 0, 0)),
            fixed_block(MICRO * NEXT, D),
        ]
        + [pl.BlockSpec((1, OWN, D), lambda u: (u, 0, 0))] * MICRO
        + [pl.BlockSpec((1, NEXT, D), lambda u: (u, 0, 0))] * MICRO,
        out_specs=[block, block],
        out_shape=[piece, piece],
        scratch_shapes=[pltpu.VMEM((D, MICRO * (OWN + NEXT)), BF)],
        compiler_params=params(),
        cost_estimate=cost(8),
        name="memory_weight_grads",
    )(core, memory, next_rows, *dkv_own, *dkv_next)


def memory_total_kernel(core_ref, own_ref, other_ref, dkv_ref, prev_ref, dm_ref, w_kv, sems):
    halves_loaded(core_ref, own_ref, other_ref, key_value_pieces(w_kv), sems)
    block = pl.program_id(0)

    @pl.when(block == 0)
    def _():
        dm_ref[...] = prev_ref[...]

    @pl.when(block > 0)
    def _():
        grads = nt(dkv_ref[0], w_kv[:, :D]) + nt(dkv_ref[1], w_kv[:, D:])
        shared = jnp.where(block == 1, prev_ref[...].astype(F32), 0.0)
        dm_ref[...] = (grads + shared).astype(BF)


def memory_total(core, own, other, dkv, prev):
    return pl.pallas_call(
        memory_total_kernel,
        grid=(MEM_DEV // BLOCK,),
        in_specs=[
            SMEM,
            ANY,
            ANY,
            pl.BlockSpec((2, BLOCK, D), lambda i: (0, jnp.maximum(i - 1, 0), 0)),
            pl.BlockSpec((BLOCK, D), lambda i: (jnp.minimum(i, 1), 0)),
        ],
        out_specs=row_block(D),
        out_shape=shape(MEM_DEV, D),
        scratch_shapes=[pltpu.VMEM((D, 2 * D), BF), pltpu.SemaphoreType.DMA((1,))],
        compiler_params=params(),
        cost_estimate=cost(4),
        name="memory_total",
    )(core, own, other, dkv, prev)


def extras_kernel(share, core_ref, sums_ref, first_ref, second_ref, third_ref, give_ref, keep_ref):
    row_id = lax.broadcasted_iota(jnp.int32, (8, D), 0)
    norms = jnp.zeros((8, D), F32)
    for place, ref in enumerate((first_ref, second_ref, third_ref)):
        norms = jnp.where(row_id == place, ref[:1, :], norms)
    stacked = jnp.concatenate([norms, jnp.zeros((LANES - 8, D), F32)], axis=0).T
    distance = lax.broadcasted_iota(jnp.int32, (HALF, LANES), 0)
    bucket_id = lax.broadcasted_iota(jnp.int32, (HALF, LANES), 1)
    exact_count = BUCKETS // 2
    bucket = jnp.full((HALF, LANES), exact_count, jnp.int32)
    for threshold in bucket_limits(BUCKETS, REACH):
        bucket = bucket + (distance >= threshold).astype(jnp.int32)
    bucket = jnp.where(distance < exact_count, distance, bucket)
    sums = sums_ref[...]
    together = LANES // BUCKETS
    lines = [jnp.zeros((1, LANES), F32) for _ in range(HEADS // together)]
    for part in range(together):
        near_hot = (bucket == bucket_id - part * BUCKETS).astype(F32)
        far_hot = (bucket_id == (part + 1) * BUCKETS - 1).astype(F32)
        table = sum(
            lax.dot_general(
                sums[:, place, :], hot, (((1,), (0,)), ((), ())),
                precision=lax.Precision.HIGHEST, preferred_element_type=F32,
            )
            for place, hot in ((0, near_hot), (1, far_hot))
        )
        for line in range(len(lines)):
            head = line * together + part
            lines[line] = lines[line] + table[head : head + 1]
    row_in_share = lax.broadcasted_iota(jnp.int32, (D, LANES), 0) % share
    tall = jnp.zeros((D, LANES), F32)
    for line, row in enumerate(lines):
        tall = jnp.where(row_in_share == line, row, tall)
    both = jnp.concatenate([stacked, tall], axis=1)
    stored_by_core(core_ref, both, give_ref, keep_ref)


def extras(core, sums, norms, across, share):
    piece = jax.ShapeDtypeStruct((across, D // (2 * across), 2 * LANES), BF)
    whole = pl.BlockSpec(memory_space=pltpu.VMEM)
    return pl.pallas_call(
        functools.partial(extras_kernel, share),
        in_specs=[SMEM] + [whole] * 4,
        out_specs=[whole, whole],
        out_shape=[piece, piece],
        compiler_params=params(),
        cost_estimate=cost(2),
        name="extras",
    )(core, sums, *norms)


def packed_kernel(core_ref, *refs):
    here_ref, there_ref = refs[-2:]
    joined = jnp.concatenate([ref[...] for ref in refs[:-2]], axis=1)
    halves = joined[:, :HALF_COLUMNS], joined[:, HALF_COLUMNS:]
    for side in range(2):

        @pl.when(core_ref[0] == side)
        def _():
            here_ref[...] = halves[side]
            there_ref[...] = halves[1 - side]


def packed(core, parts):
    whole = pl.BlockSpec(memory_space=pltpu.VMEM)
    piece = shape(parts[0].shape[0], HALF_COLUMNS)
    return pl.pallas_call(
        packed_kernel,
        in_specs=[SMEM] + [whole] * len(parts),
        out_specs=[whole, whole],
        out_shape=[piece, piece],
        compiler_params=params(),
        cost_estimate=cost(1),
        name="packed",
    )(core, *parts)


def assembled_kernel(place_ref, *refs):
    out_ref = refs[-1]
    for step, piece_ref in enumerate(refs[:-1]):

        @pl.when(pl.program_id(0) == step)
        def _():
            out_ref[0, :, 0] = piece_ref[...]


def assembled(place, pieces):
    count, rows, columns = pieces[0].shape
    return pl.pallas_call(
        assembled_kernel,
        grid_spec=pltpu.PrefetchScalarGridSpec(
            num_scalar_prefetch=1,
            grid=(4,),
            in_specs=[pl.BlockSpec((count, rows, columns), lambda i, place: (0, 0, 0))] * 4,
            out_specs=pl.BlockSpec(
                (1, count, 1, rows, columns),
                lambda i, place: (place[0] ^ (i // 2), 0, place[1] ^ (i % 2), 0, 0),
            ),
        ),
        out_shape=jax.ShapeDtypeStruct((2, count, 2, rows, columns), BF),
        compiler_params=params(),
        cost_estimate=cost(3),
        name="assembled",
    )(place, *pieces)


def bias_tiles_kernel(table_ref, tiles_ref):
    head = pl.program_id(0)
    key_id = lax.broadcasted_iota(jnp.int32, (HALF, HALF), 0)
    query_id = lax.broadcasted_iota(jnp.int32, (HALF, HALF), 1)
    limits = bucket_limits(BUCKETS, REACH)
    exact_count = BUCKETS // 2
    for tile in range(2):
        distance = query_id - key_id + tile * HALF
        grid = jnp.full((HALF, HALF), table_ref[head, 0], F32)
        for bucket in range(1, BUCKETS):
            start = bucket if bucket <= exact_count else limits[bucket - exact_count - 1]
            grid = jnp.where(distance >= start, table_ref[head, bucket], grid)
        if tile == 0:
            grid = jnp.where(distance >= 0, grid, MASKED)
        tiles_ref[0, tile] = grid


def bias_tiles(table):
    return pl.pallas_call(
        bias_tiles_kernel,
        grid=(HEADS,),
        in_specs=[pl.BlockSpec(memory_space=pltpu.SMEM)],
        out_specs=pl.BlockSpec((1, 2, HALF, HALF), lambda h: (h, 0, 0, 0)),
        out_shape=jax.ShapeDtypeStruct((HEADS, 2, HALF, HALF), F32),
        cost_estimate=cost(8),
        name="bias_tiles",
    )(table)


def softmax_columns(scores):
    top = jnp.max(scores, axis=0, keepdims=True)
    weights = jnp.exp(scores - top)
    total = jnp.sum(weights, axis=0, keepdims=True)
    return weights.astype(BF), 1.0 / total, top + jnp.log(total)


def put_lse(lse_ref, rows):
    row_id = lax.broadcasted_iota(jnp.int32, (8, TGT_LEN), 0)
    lse_ref[0] = jnp.where(row_id == 0, rows[0], rows[1])


def attended(scores, value, small):
    top = 0.0 if small else jnp.max(scores, axis=0, keepdims=True)
    weights = jnp.exp(scores if small else scores - top).astype(BF)
    both = nn(value, weights)
    total = both[HEAD_DIM : HEAD_DIM + 1]
    return both[:HEAD_DIM] * (1.0 / total), top + jnp.log(total)


def cross_forward_kernel(
    small_ref, q_ref, ko_ref, kn_ref, vo_ref, vn_ref, mask_ref, o_ref, lse_ref, k_ext
):
    def run(small):
        k_ext[:OWN, :LANES] = ko_ref[...]
        k_ext[OWN:, :LANES] = kn_ref[...]
        k_ext[:, LANES:] = mask_ref[0]
        q_t = q_ref[...].T
        v_t = jnp.concatenate([vo_ref[...], vn_ref[...]], axis=0).T
        ones = extra_rows(TGT_LEN, 1.0, ())
        rows_of_ones = jnp.ones((16, KEYS), BF)
        scores = [
            nn(k_ext[...], jnp.concatenate([head_rows(q_t, head), ones], axis=0))
            for head in range(2)
        ]
        values = [
            jnp.concatenate([v_t[head * HEAD_DIM : (head + 1) * HEAD_DIM], rows_of_ones], axis=0)
            for head in range(2)
        ]
        mixed, lses = zip(*[attended(scores[head], values[head], small) for head in range(2)])
        o_ref[...] = jnp.concatenate(mixed, axis=0).T.astype(BF)
        put_lse(lse_ref, lses)

    @pl.when(small_ref[0] == 1)
    def _():
        run(True)

    @pl.when(small_ref[0] != 1)
    def _():
        run(False)


def cross_backward_kernel(
    q_ref, ko_ref, kn_ref, vo_ref, vn_ref, mask_ref, o_ref, do_ref, lse_ref,
    dq_ref, own_ref, next_ref, k_ext, v_ext,
):
    k_ext[:OWN, :LANES] = ko_ref[...]
    k_ext[OWN:, :LANES] = kn_ref[...]
    k_ext[:, LANES:] = mask_ref[0]
    v_ext[:OWN, :LANES] = vo_ref[...]
    v_ext[OWN:, :LANES] = vn_ref[...]
    v_ext[:, LANES:] = jnp.ones((KEYS, LANES), BF)
    k_t = k_ext[:, :LANES].T
    q = q_ref[...]
    d_o = do_ref[...]
    q_t = q.T
    do_t = d_o.T
    centre_t = (o_ref[...].astype(F32) * d_o.astype(F32)).T
    dq, dk, dv = [], [], []
    for head in range(2):
        rows = slice(head * HEAD_DIM, (head + 1) * HEAD_DIM)
        lse = lse_ref[0, head : head + 1, :]
        centre = jnp.sum(centre_t[rows], axis=0, keepdims=True)
        query = jnp.concatenate(
            [head_rows(q_t, head), extra_rows(TGT_LEN, 1.0, three_parts(-lse))], axis=0
        )
        grad = jnp.concatenate(
            [head_rows(do_t, head), extra_rows(TGT_LEN, 0.0, three_parts(-centre))], axis=0
        )
        probs = jnp.exp(nn(k_ext[...], query))
        grad_scores = (probs * nn(v_ext[...], grad)).astype(BF)
        dv.append(nn(probs.astype(BF), d_o))
        dk.append(nn(grad_scores, q))
        dq.append(nn(k_t[rows], grad_scores))
    dq_ref[...] = jnp.concatenate(dq, axis=0).T.astype(BF)
    lane = lax.broadcasted_iota(jnp.int32, (KEYS, LANES), 1)
    dk_pair = jnp.where(lane < HEAD_DIM, dk[0], dk[1]).astype(BF)
    dv_pair = jnp.where(lane < HEAD_DIM, dv[0], dv[1]).astype(BF)
    for place, pair in enumerate((dk_pair, dv_pair)):
        own_ref[place] = pair[:OWN]
        next_ref[place] = pair[OWN:]


def self_forward_kernel(q_ref, k_ref, v_ref, tiles_ref, o_ref, lse_ref):
    k = k_ref[...]
    q_t = q_ref[...].T
    v_t = v_ref[...].T
    mixed, lses = [], []
    for head in range(2):
        query = head_rows(q_t, head)
        value = v_t[head * HEAD_DIM : (head + 1) * HEAD_DIM]
        near, far = tiles_ref[head, 0], tiles_ref[head, 1]
        w0, i0, l0 = softmax_columns(nn(k[:HALF], query[:, :HALF]) + near)
        raw = nn(k, query[:, HALF:])
        w1, i1, l1 = softmax_columns(
            jnp.concatenate([raw[:HALF] + far, raw[HALF:] + near], axis=0)
        )
        out0 = nn(value[:, :HALF], w0) * i0
        out1 = nn(value, w1) * i1
        mixed.append(jnp.concatenate([out0, out1], axis=1))
        lses.append(jnp.concatenate([l0, l1], axis=1))
    o_ref[...] = jnp.concatenate(mixed, axis=0).T.astype(BF)
    put_lse(lse_ref, lses)


def distance_sums(near, far):
    key_id = lax.broadcasted_iota(jnp.int32, (HALF, HALF), 0)
    query_id = lax.broadcasted_iota(jnp.int32, (HALF, HALF), 1)
    close = (query_id - key_id + HALF) < REACH
    both = near + jnp.where(close, far, 0.0)
    group = both[:8]
    for first in range(8, HALF, 8):
        group = group + pltpu.roll(both[first : first + 8], HALF - first, 1)
    row_id = lax.broadcasted_iota(jnp.int32, (8, HALF), 0)
    turned = group
    for row in range(1, 8):
        turned = jnp.where(row_id == row, pltpu.roll(group, HALF - row, 1), turned)
    by_distance = jnp.sum(turned, axis=0, keepdims=True)
    rest = jnp.sum(jnp.where(close, 0.0, far), axis=0, keepdims=True)
    return jnp.where(row_id == 0, by_distance, jnp.where(row_id == 1, rest, 0.0))


def self_backward_kernel(
    q_ref, k_ref, v_ref, tiles_ref, o_ref, do_ref, lse_ref,
    dqkv_ref, sums_ref, k_ext, v_ext, near_ref, far_ref,
):
    row_ext = jnp.ones((TGT_LEN, LANES), BF)
    k_ext[:, :LANES] = k_ref[...]
    k_ext[:, LANES:] = row_ext
    v_ext[:, :LANES] = v_ref[...]
    v_ext[:, LANES:] = row_ext
    k_t = k_ref[...].T
    q = q_ref[...]
    d_o = do_ref[...]
    q_t = q.T
    do_t = d_o.T
    centre_t = (o_ref[...].astype(F32) * d_o.astype(F32)).T
    first = pl.program_id(1) == 0
    dq, dk, dv = [], [], []
    for head in range(2):
        rows = slice(head * HEAD_DIM, (head + 1) * HEAD_DIM)
        lse = lse_ref[0, head : head + 1, :]
        centre = jnp.sum(centre_t[rows], axis=0, keepdims=True)
        query = jnp.concatenate(
            [head_rows(q_t, head), extra_rows(TGT_LEN, 0.0, three_parts(-lse))], axis=0
        )
        grad = jnp.concatenate(
            [head_rows(do_t, head), extra_rows(TGT_LEN, 0.0, three_parts(-centre))], axis=0
        )
        near, far = tiles_ref[head, 0], tiles_ref[head, 1]
        raw0 = nn(k_ext[:HALF, :], query[:, :HALF])
        raw1 = nn(k_ext[...], query[:, HALF:])
        p00 = jnp.exp(raw0 + near)
        p10 = jnp.exp(raw1[:HALF] + far)
        p11 = jnp.exp(raw1[HALF:] + near)
        g0 = nn(v_ext[:HALF, :], grad[:, :HALF])
        g1 = nn(v_ext[...], grad[:, HALF:])
        s00 = p00 * g0
        s10 = p10 * g1[:HALF]
        s11 = p11 * g1[HALF:]
        near_sum, far_sum = s00 + s11, s10

        @pl.when(first)
        def _():
            near_ref[head] = near_sum
            far_ref[head] = far_sum

        @pl.when(jnp.logical_not(first))
        def _():
            sums_ref[head] = distance_sums(near_ref[head] + near_sum, far_ref[head] + far_sum)

        b00, b10, b11 = s00.astype(BF), s10.astype(BF), s11.astype(BF)
        w00, w10, w11 = p00.astype(BF), p10.astype(BF), p11.astype(BF)
        top = jnp.concatenate([w00, w10], axis=1)
        dv.append(jnp.concatenate([nn(top, d_o), nn(w11, d_o[HALF:])], axis=0))
        top = jnp.concatenate([b00, b10], axis=1)
        dk.append(jnp.concatenate([nn(top, q), nn(b11, q[HALF:])], axis=0))
        dq.append(
            jnp.concatenate(
                [
                    nn(k_t[rows, :HALF], b00),
                    nn(k_t[rows], jnp.concatenate([b10, b11], axis=0)),
                ],
                axis=1,
            )
        )
    dqkv_ref[0] = jnp.concatenate(dq, axis=0).T.astype(BF)
    lane = lax.broadcasted_iota(jnp.int32, (TGT_LEN, LANES), 1)
    dqkv_ref[1] = jnp.where(lane < HEAD_DIM, dk[0], dk[1]).astype(BF)
    dqkv_ref[2] = jnp.where(lane < HEAD_DIM, dv[0], dv[1]).astype(BF)


PAIR_GRID = (MICRO, PAIRS)


def pair_block(rows, offset=0):
    return pl.BlockSpec((rows, LANES), lambda m, p: (m, p + offset))


LSE_BLOCK = pl.BlockSpec((1, 8, TGT_LEN), lambda m, p: (m * PAIRS + p, 0, 0))
LSE_SHAPE = jax.ShapeDtypeStruct((MICRO * PAIRS, 8, TGT_LEN), F32)
MASK_BLOCK = pl.BlockSpec((1, KEYS, LANES), lambda m, p: (m, 0, 0))


def cross_forward(small, q, kv_own, kv_next, mask):
    return pl.pallas_call(
        cross_forward_kernel,
        grid=PAIR_GRID,
        in_specs=[
            SMEM,
            pair_block(TGT_LEN),
            pair_block(OWN),
            pair_block(NEXT),
            pair_block(OWN, PAIRS),
            pair_block(NEXT, PAIRS),
            MASK_BLOCK,
        ],
        out_specs=[pair_block(TGT_LEN), LSE_BLOCK],
        out_shape=[jax.ShapeDtypeStruct((ROWS, D), BF), LSE_SHAPE],
        scratch_shapes=[pltpu.VMEM((KEYS, 2 * LANES), BF)],
        compiler_params=params(),
        cost_estimate=cost(32),
        name="cross_forward",
    )(small, q, kv_own, kv_next, kv_own, kv_next, mask)


def cross_backward(m, q, kv_own, kv_next, mask, o, d_o, lse):
    def block(rows, offset=0):
        return pl.BlockSpec((rows, LANES), lambda p: (m, p + offset))

    return pl.pallas_call(
        cross_backward_kernel,
        grid=(PAIRS,),
        in_specs=[
            block(TGT_LEN),
            block(OWN),
            block(NEXT),
            block(OWN, PAIRS),
            block(NEXT, PAIRS),
            pl.BlockSpec((1, KEYS, LANES), lambda p: (m, 0, 0)),
            block(TGT_LEN),
            block(TGT_LEN),
            pl.BlockSpec((1, 8, TGT_LEN), lambda p: (m * PAIRS + p, 0, 0)),
        ],
        out_specs=[
            pl.BlockSpec((TGT_LEN, LANES), lambda p: (0, p)),
            pl.BlockSpec((2, OWN, LANES), lambda p: (0, 0, p)),
            pl.BlockSpec((2, NEXT, LANES), lambda p: (0, 0, p)),
        ],
        out_shape=[
            shape(TGT_LEN, D),
            jax.ShapeDtypeStruct((2, OWN, D), BF),
            jax.ShapeDtypeStruct((2, NEXT, D), BF),
        ],
        scratch_shapes=[pltpu.VMEM((KEYS, 2 * LANES), BF)] * 2,
        compiler_params=params(),
        cost_estimate=cost(22),
        name="cross_backward",
    )(*map(far, (q, kv_own, kv_next, kv_own, kv_next, mask, o, d_o, lse)))


def swapped(spec):
    index = spec.index_map
    return pl.BlockSpec(spec.block_shape, lambda p, m: index(m, p))


TILE_BLOCK = pl.BlockSpec((2, 2, HALF, HALF), lambda p, m: (p, 0, 0, 0))


def self_forward(qkv, tiles):
    return pl.pallas_call(
        self_forward_kernel,
        grid=(PAIRS, MICRO),
        in_specs=[
            swapped(pair_block(TGT_LEN)),
            swapped(pair_block(TGT_LEN, PAIRS)),
            swapped(pair_block(TGT_LEN, 2 * PAIRS)),
            TILE_BLOCK,
        ],
        out_specs=[swapped(pair_block(TGT_LEN)), swapped(LSE_BLOCK)],
        out_shape=[jax.ShapeDtypeStruct((ROWS, D), BF), LSE_SHAPE],
        compiler_params=params(),
        cost_estimate=cost(17),
        name="self_forward",
    )(qkv, qkv, qkv, tiles)


def self_backward(qkv, tiles, o, d_o, lse):
    sums = jax.ShapeDtypeStruct((HEADS, 8, HALF), F32)
    return pl.pallas_call(
        self_backward_kernel,
        grid=(PAIRS, MICRO),
        in_specs=[
            swapped(pair_block(TGT_LEN)),
            swapped(pair_block(TGT_LEN, PAIRS)),
            swapped(pair_block(TGT_LEN, 2 * PAIRS)),
            TILE_BLOCK,
            swapped(pair_block(TGT_LEN)),
            swapped(pair_block(TGT_LEN)),
            swapped(LSE_BLOCK),
        ],
        out_specs=[
            pl.BlockSpec((3, TGT_LEN, LANES), lambda p, m: (0, m, p)),
            pl.BlockSpec((2, 8, HALF), lambda p, m: (p, 0, 0)),
        ],
        out_shape=[jax.ShapeDtypeStruct((3, ROWS, D), BF), sums],
        scratch_shapes=[pltpu.VMEM((TGT_LEN, 2 * LANES), BF)] * 2
        + [pltpu.VMEM((2, HALF, HALF), F32)] * 2,
        compiler_params=params(),
        cost_estimate=cost(24),
        name="self_backward",
    )(qkv, qkv, qkv, tiles, o, d_o, lse)


def key_masks(offsets_row, position):
    shard_ids = jnp.arange(offsets_row.shape[0], dtype=jnp.int32)
    own_start = jnp.sum(jnp.where(shard_ids == position, offsets_row, 0))
    next_start = jnp.sum(jnp.where(shard_ids == position + 1, offsets_row, 0))
    own_valid = jnp.arange(MEM_DEV - OWN, MEM_DEV, dtype=jnp.int32) >= own_start
    next_valid = jnp.arange(NEXT, dtype=jnp.int32) < next_start
    valid = jnp.concatenate([own_valid, next_valid])[:, None]
    lane = jnp.arange(LANES, dtype=jnp.int32)[None, :]
    return jnp.where((lane == 0), jnp.where(valid, 0.0, MASKED), 1.0).astype(BF)


def passed_along(block, distance):
    devices = range(lax.axis_size("seq"))
    route = [(i - distance, i) for i in devices if i - distance in devices]
    return lax.ppermute(block, "seq", route)


def device_bits():
    bits = []
    for axis in AXES:
        count = lax.axis_size(axis).bit_length() - 1
        bits += [(axis, place) for place in reversed(range(count))]
    return bits


def bit_groups():
    bits = device_bits()
    core = ("dp", 0)
    low = (lax.axis_size("seq").bit_length() - 1) // 2
    plane = [b for b in bits if b != core and (b[0] == "dp" or b[1] < low)]
    column = [b for b in bits if b[0] == "seq" and b[1] >= low]
    return [core], plane, column


def mine(bit):
    axis, place = bit
    return (lax.axis_index(axis) >> place) & 1


def flips(group):
    for mask in range(1, 1 << len(group)):
        yield [(mask >> place) & 1 for place in range(len(group))]


def exchange(block, group, flip):
    mask = 0
    for (axis, place), turned in zip(group, flip):
        stride = lax.axis_size("seq") if axis == "dp" else 1
        mask ^= turned * stride << place
    count = lax.axis_size("dp") * lax.axis_size("seq")
    return lax.ppermute(block, AXES, [(i, i ^ mask) for i in range(count)])


def gather_stage(held, dims, group, fillers=()):
    order = device_bits()
    joined = sorted(dims + group, key=order.index)
    tail = held.shape[len(dims) :]
    spot = tuple(1 if bit in group else 2 for bit in joined) + tail
    turns = [[0] * len(group)] + list(flips(group))
    pieces = [held] + [exchange(held, group, flip) for flip in turns[1:]]
    pieces, fillers = tied(pieces, fillers)
    if len(group) == 2 and joined[0] == group[0] and joined[-1] == group[1] and tail[0] % 8 == 0:
        place = jnp.stack([mine(bit) for bit in group]).astype(jnp.int32)
        order = [turns.index([first, last]) for first in range(2) for last in range(2)]
        flat = [pieces[turn].reshape((-1,) + tail) for turn in order]
        return assembled(place, flat).reshape((2,) * len(joined) + tail), joined, fillers
    result = jnp.zeros((2,) * len(joined) + tail, held.dtype)
    for flip, piece in zip(turns, pieces):
        start = [mine(bit) ^ flip[group.index(bit)] if bit in group else 0 for bit in joined]
        result = lax.dynamic_update_slice(result, piece.reshape(spot), start + [0] * len(tail))
    return result, joined, fillers


def paired_halves(shard, core):
    halves = shard.reshape(shard.shape[0], 2, -1)
    here = lax.dynamic_index_in_dim(halves, core, 1, keepdims=False)
    there = lax.dynamic_index_in_dim(halves, 1 - core, 1, keepdims=False)
    return swapped_halves(here, there, core)


def swapped_halves(here, there, core):
    received = exchange(there, bit_groups()[0], [1])
    return jnp.stack([jnp.where(core == 0, here, received), jnp.where(core == 0, received, here)])


def both_halves(held):
    own = held.reshape(-1, held.shape[-1])
    return own, exchange(own, bit_groups()[0], [1])


def gather_bits(held, dims, group):
    for bit in reversed(group):
        held, dims, _ = gather_stage(held, dims, [bit])
    return held, dims, ()


def tree_sum(terms):
    terms = [term.astype(F32) for term in terms]
    while len(terms) > 1:
        terms = [
            terms[place] + terms[place + 1] if place + 1 < len(terms) else terms[place]
            for place in range(0, len(terms), 2)
        ]
    return terms[0]


def picked(array, dims, group, flip):
    left = list(dims)
    for bit, turned in zip(group, flip):
        place = left.index(bit)
        left.remove(bit)
        array = lax.dynamic_index_in_dim(array, mine(bit) ^ turned, place, keepdims=False)
    return array


def scatter_parts(bundles, dims, group):
    def part(flip):
        sums = [
            tree_sum([picked(term, dims, group, flip) for term in terms]).astype(BF)
            for terms in bundles
        ]
        return jnp.concatenate(sums, axis=-1) if len(sums) > 1 else sums[0]

    return [part([0] * len(group))] + [part(flip) for flip in flips(group)]


def scattered(parts, group):
    sent = [exchange(part, group, flip) for part, flip in zip(parts[1:], flips(group))]
    return parts[:1] + sent


def core_stage(give, keep):
    core, _, _ = bit_groups()
    dims = [bit for bit in device_bits() if bit not in core]
    received = exchange(give, core, [1])
    split = (2,) * len(dims) + (give.shape[0] * give.shape[1] >> len(dims), give.shape[2])
    return [keep.reshape(split), received.reshape(split)]


def without(dims, group):
    return [bit for bit in dims if bit not in group]


def passed_along(block, distance):
    devices = range(lax.axis_size("seq"))
    route = [(i - distance, i) for i in devices if i - distance in devices]
    return lax.ppermute(block, "seq", route)


def ffn_grads(h3, acts, dy, later):
    devices = lax.axis_size("dp") * lax.axis_size("seq")
    width = acts.shape[2]
    if D // devices % 8 or width // devices % 16:
        total = [
            lax.psum_scatter(
                lax.dot_general(
                    rows, grads, (((0,), (0,)), ((), ())), preferred_element_type=F32
                ),
                AXES,
                scatter_dimension=0,
                tiled=True,
            )
            for rows, grads in ((h3, acts[0]), (h3, acts[1]), (acts[2], dy))
        ]
        return total, later
    partial = ffn_weight_grads(h3, acts, dy, devices)
    later, partial = tied(later, partial)
    return lax.psum_scatter(partial, AXES, scatter_dimension=0, tiled=True), later


def ffn_columns(total, share, width):
    if isinstance(total, (list, tuple)):
        return total
    total = total[0].astype(F32)
    rows = share * width // WIDE

    def columns(first, height):
        block = total[first : first + rows].reshape(-1, height, WIDE)
        return block.transpose(1, 0, 2).reshape(height, -1)

    return columns(0, share), columns(rows, share), columns(2 * rows, rows * WIDE // D)


def tied(values, parts):
    values, parts = lax.optimization_barrier((values, parts))
    return values, parts


def local(
    decoder_in,
    memory,
    doc_offsets,
    self_query,
    self_key,
    self_value,
    self_out,
    cross_query,
    cross_key,
    cross_value,
    cross_out,
    ffn_gate,
    ffn_up,
    ffn_down,
    norm_self,
    norm_cross,
    norm_ffn,
    bias_table,
    cotangent,
):
    position = lax.axis_index("seq")
    core = lax.axis_index("dp") & 1
    core_id = core.reshape(1).astype(jnp.int32)
    across = lax.axis_size("dp") // 2
    share = self_query.shape[0]
    core_bits, plane, column = bit_groups()

    gains = jnp.stack([norm_self, norm_cross, norm_ffn], axis=1)
    gains = jnp.pad(gains, ((0, 0), (0, 2 * LANES - 3)))
    first = packed(
        core_id, [cross_key, cross_value, self_query, self_key, self_value, gains]
    )
    second = jnp.concatenate([self_out, cross_query], axis=1)
    late = jnp.concatenate([cross_out, ffn_gate, ffn_up], axis=1)
    first = swapped_halves(*first, core)
    first, dims, _ = gather_stage(first, core_bits, column)
    first, second, ffn_down, doc_offsets, memory, bias_table = lax.optimization_barrier(
        (first, second, ffn_down, doc_offsets, memory, bias_table)
    )
    second = paired_halves(second, core)
    third = paired_halves(ffn_down, core)
    tiles = bias_tiles(bias_table.astype(F32))
    mask = jnp.stack([key_masks(doc_offsets[m, 0], position) for m in range(MICRO)])
    next_rows = memory[:, 0, :NEXT]
    narrow = second.reshape(2, 2 * share, -1)
    second, _, _ = gather_bits(jnp.concatenate([narrow, third], axis=1), core_bits, column)
    first, _, (second, tiles, mask, next_rows, late) = gather_stage(
        first, dims, plane, (second, tiles, mask, next_rows, late)
    )
    third = second[..., 2 * share :, :]
    second = second[..., : 2 * share, :].reshape(third.shape[:-2] + (share, D))
    own, other = both_halves(first)
    late = lax.all_gather(late, AXES, axis=0, tiled=True)
    x = decoder_in.reshape(ROWS, D)
    dy = cotangent.reshape(ROWS, D)
    mem = memory.reshape(MICRO * MEM_DEV, D)
    next_rows = passed_along(next_rows, -1).reshape(MICRO * NEXT, D)

    x, second = tied(x, second)
    h1, qkv, gains = self_inputs(core_id, own, other, x)
    o1, lse1 = self_forward(qkv, tiles)
    mem, o1 = tied(mem, o1)
    kv_own, own_size = key_value(
        core_id, own, other, mem, MICRO * OWN // BLOCK, lambda i: (i + i // 3 + 1, 0), 6
    )
    second, _, (o1, kv_own, next_rows) = gather_stage(
        second, dims, plane, (o1, kv_own, next_rows)
    )
    own_b, other_b = both_halves(second)
    next_rows, third, own_b = lax.optimization_barrier((next_rows, third, own_b))
    kv_next, next_size = key_value(
        core_id, own, other, next_rows, MICRO * NEXT // BLOCK, lambda i: (i, 0), 4
    )
    o1, kv_next = tied(o1, kv_next)
    x1, h2, q2, query_size = cross_inputs(core_id, own_b, other_b, gains, x, o1)
    largest = jnp.max(query_size[:1] * jnp.maximum(own_size[:1], next_size[:1]))
    small = (largest <= SMALL_SCORE**2).astype(jnp.int32).reshape(1)
    o2, lse2 = cross_forward(small, q2, kv_own, kv_next, mask)
    third, _, o2 = gather_stage(third, dims, plane, o2)
    own_c, other_c = both_halves(third)
    out, h3, acts, db2, dx2, do2, g_norm_ffn = ffn(
        core_id, late, own_c, other_c, gains, x1, o2, dy
    )
    ffn_total, do2 = ffn_grads(h3, acts, dy, do2)
    dims = without(device_bits(), core_bits)
    arguments = (q2, kv_own, kv_next, mask, o2, do2, lse2)
    results, arrived = [], []
    for m in range(MICRO):
        dq_m, own_m, next_m = cross_backward(m, *arguments)
        dm_m = memory_grads(core_id, own, other, next_m)
        if m + 1 < MICRO:
            arguments, dm_m = tied(arguments, dm_m)
        results.append((dq_m, own_m, next_m))
        if arrived:
            dm_m, arrived[-1] = tied(dm_m, arrived[-1])
        arrived.append(passed_along(dm_m, 1))
    dq2, dkv_own, dkv_next = zip(*results)
    dkv_own, dkv_next, dm_m = lax.optimization_barrier((dkv_own, dkv_next, dm_m))
    pair_terms = core_stage(*pair_grads(core_id, [(o2, (db2,)), (h2, dq2)], across))
    give, keep = memory_weight_grads(core_id, memory, next_rows, dkv_own, dkv_next, across)
    dq2, give = tied(dq2, give)
    memory_terms = core_stage(give, keep)
    dx1, db1, do1, g_norm_cross = self_grads(core_id, own_b, other_b, gains, x1, dx2, dq2)
    (db1, do1), pair_terms, memory_terms = lax.optimization_barrier(
        ((db1, do1), pair_terms, memory_terms)
    )
    out_terms = core_stage(*pair_grads(core_id, [(o1, (db1,))], across))
    cross_parts = scatter_parts([pair_terms, memory_terms, out_terms], dims, plane)
    do1, cross_parts = tied(do1, cross_parts)
    cross_terms = scattered(cross_parts, plane)
    dqkv, sums = self_backward(qkv, tiles, o1, do1, lse1)
    dqkv, arrived[-1] = tied(dqkv, arrived[-1])
    give, keep = row_grads(core_id, h1, dqkv, across, 5)
    dqkv, give, cross_terms = lax.optimization_barrier((dqkv, give, cross_terms))
    self_terms = core_stage(give, keep)
    left = without(dims, plane)
    high, low = column[:1], column[1:]
    cross_parts = scatter_parts([cross_terms], left, high)
    dqkv, cross_parts = tied(dqkv, cross_parts)
    cross_terms = scattered(cross_parts, high)
    grad_decoder, g_norm_self = input_grads(core_id, own, other, gains, x, dx1, dqkv)
    g_norm_self, self_terms = tied(g_norm_self, self_terms)
    self_parts = scatter_parts([self_terms], dims, plane)
    give, keep = extras(core_id, sums, [g_norm_self, g_norm_cross, g_norm_ffn], across, share)
    dkv_own, self_parts, give = lax.optimization_barrier((dkv_own, self_parts, give))
    self_terms = scattered(self_parts, plane)
    extra_terms = core_stage(give, keep)
    totals = [memory_total(core_id, own, other, dkv_own[0], arrived[0])]
    totals[0], extra_terms, cross_terms = lax.optimization_barrier(
        (totals[0], extra_terms, cross_terms)
    )
    cross_parts = scatter_parts([cross_terms], low, low)
    dkv_own, cross_parts = tied(dkv_own, cross_parts)
    cross_terms = scattered(cross_parts, low)
    extra_left = list(dims)
    for bit in plane:
        extra_parts = scatter_parts([extra_terms], extra_left, [bit])
        extra_left.remove(bit)
        if len(totals) == 1:
            dkv_own, extra_parts = tied(dkv_own, extra_parts)
        extra_terms = scattered(extra_parts, [bit])
        if len(totals) == 1:
            totals.append(memory_total(core_id, own, other, dkv_own[1], arrived[1]))
            totals[1], extra_terms = tied(totals[1], extra_terms)
    totals, self_terms, extra_terms = lax.optimization_barrier((totals, self_terms, extra_terms))
    self_parts = scatter_parts([self_terms, extra_terms], left, column)
    self_parts, cross_terms, ffn_total = lax.optimization_barrier(
        (self_parts, cross_terms, ffn_total)
    )
    g_self = tree_sum(scattered(self_parts, column))
    g_cross = tree_sum(cross_terms)
    grad_memory = jnp.stack(totals)
    g_gate, g_up, g_down = ffn_columns(ffn_total, share, ffn_gate.shape[1])

    table = g_self[: HEADS * BUCKETS // LANES, 3 * D + LANES :].reshape(HEADS, BUCKETS)

    def cut(stack, index):
        return stack[:, index * D : (index + 1) * D]

    return (
        out.reshape(decoder_in.shape),
        grad_decoder.reshape(decoder_in.shape),
        grad_memory.reshape(memory.shape),
        cut(g_self, 0),
        cut(g_self, 1),
        cut(g_self, 2),
        cut(g_cross, 4),
        cut(g_cross, 1),
        cut(g_cross, 2),
        cut(g_cross, 3),
        cut(g_cross, 0),
        g_gate,
        g_up,
        g_down,
        g_self[:, 3 * D],
        g_self[:, 3 * D + 1],
        g_self[:, 3 * D + 2],
        table,
    )


def solution(mesh):
    in_specs = (
        P(None, ("dp", "seq"), None, None),
        P(None, ("dp", "seq"), None, None),
        P(None, "dp", None),
        P(("dp", "seq"), None),
        P(("dp", "seq"), None),
        P(("dp", "seq"), None),
        P(("dp", "seq"), None),
        P(("dp", "seq"), None),
        P(("dp", "seq"), None),
        P(("dp", "seq"), None),
        P(("dp", "seq"), None),
        P(("dp", "seq"), None),
        P(("dp", "seq"), None),
        P(("dp", "seq"), None),
        P(("dp", "seq")),
        P(("dp", "seq")),
        P(("dp", "seq")),
        P(),
        P(None, ("dp", "seq"), None, None),
    )
    out_specs = (
        P(None, ("dp", "seq"), None, None),
        P(None, ("dp", "seq"), None, None),
        P(None, ("dp", "seq"), None, None),
        P(("dp", "seq"), None),
        P(("dp", "seq"), None),
        P(("dp", "seq"), None),
        P(("dp", "seq"), None),
        P(("dp", "seq"), None),
        P(("dp", "seq"), None),
        P(("dp", "seq"), None),
        P(("dp", "seq"), None),
        P(("dp", "seq"), None),
        P(("dp", "seq"), None),
        P(("dp", "seq"), None),
        P(("dp", "seq")),
        P(("dp", "seq")),
        P(("dp", "seq")),
        P(),
    )
    return jax.shard_map(local, mesh=mesh, in_specs=in_specs, out_specs=out_specs, check_vma=False)
```

```python
import functools
import math

import jax
import jax.numpy as jnp
from jax import lax
from jax.experimental import pallas as pl
from jax.experimental.pallas import tpu as pltpu
from jax.sharding import PartitionSpec as P

D = 768
HEADS = 12
HEAD_DIM = 64
BUCKETS = 32
REACH = 128
TGT_LEN = 512
MEM_DEV = 1024
MICRO = 2
PAIRS = HEADS // 2
LANES = 2 * HEAD_DIM
OWN = MEM_DEV - MEM_DEV // 4
NEXT = MEM_DEV // 2
KEYS = OWN + NEXT
HALF = 256
MASKED = -1e30
NORM_EPS = 1e-06
AXES = ("dp", "seq")
ROWS = MICRO * TGT_LEN
BLOCK = 256
WIDE = 256
SMALL_SCORE = 59.0
FFN_CHUNK = 1024
HALF_COLUMNS = 2048
VMEM_LIMIT = 52 * 1024 * 1024
BF = jnp.bfloat16
F32 = jnp.float32


def nn(a, b):
    return lax.dot_general(a, b, (((1,), (0,)), ((), ())), preferred_element_type=F32)


def bucket_limits(buckets, reach):
    exact_count = buckets // 2
    limits = []
    for target in range(exact_count + 1, buckets):
        distance = exact_count
        while (
            exact_count
            + int(
                math.log(distance / exact_count)
                / math.log(reach / exact_count)
                * (buckets - exact_count)
            )
            < target
        ):
            distance += 1
        limits.append(distance)
    return limits


def three_parts(row):
    high = row.astype(BF).astype(F32)
    rest = row - high
    middle = rest.astype(BF).astype(F32)
    return high, middle, rest - middle


def extra_rows(columns, first, parts):
    row_id = lax.broadcasted_iota(jnp.int32, (LANES, columns), 0)
    grid = jnp.where(row_id == 0, first, 0.0)
    for place, part in enumerate(parts):
        grid = jnp.where(row_id == place + 1, part, grid)
    return grid.astype(BF)


def head_rows(stacked, head):
    row_id = lax.broadcasted_iota(jnp.int32, stacked.shape, 0)
    return jnp.where((row_id // HEAD_DIM) == head, stacked, jnp.zeros_like(stacked))


def far(array):
    return pltpu.with_memory_space_constraint(array, pltpu.HBM)


def nt(a, b):
    return lax.dot_general(a, b, (((1,), (1,)), ((), ())), preferred_element_type=F32)


def params(**options):
    return pltpu.CompilerParams(vmem_limit_bytes=VMEM_LIMIT, **options)


def cost(us):
    return pl.CostEstimate(flops=int(us), bytes_accessed=0, transcendentals=0)


def shape(rows, columns, kind=BF):
    return jax.ShapeDtypeStruct((rows, columns), kind)


def row_block(columns, rows=BLOCK):
    return pl.BlockSpec((rows, columns), lambda i: (i, 0))


def fixed_block(rows, columns):
    return pl.BlockSpec((rows, columns), lambda i: (0, 0))


ANY = pl.BlockSpec(memory_space=pl.ANY)
SMEM = pl.BlockSpec(memory_space=pltpu.SMEM)


def halves_loaded(core_ref, own_ref, other_ref, pieces, sems):
    @pl.when(pl.program_id(0) == 0)
    def _():
        for side in range(2):

            @pl.when(core_ref[0] == side)
            def _():
                halves = (own_ref, other_ref) if side == 0 else (other_ref, own_ref)
                copies = [
                    pltpu.make_async_copy(halves[half].at[:, source], target, sems.at[place])
                    for place, (half, source, target) in enumerate(pieces)
                ]
                for copy in copies:
                    copy.start()
                for copy in copies:
                    copy.wait()


def key_value_pieces(w_kv):
    return [(0, slice(0, 2 * D), w_kv)]


def out_query_pieces(weights):
    return [(side, slice(0, D), weights.at[:, side * D : (side + 1) * D]) for side in range(2)]


def query_pieces(w_qkv):
    cut = HALF_COLUMNS - 2 * D
    return [
        (0, slice(2 * D, HALF_COLUMNS), w_qkv.at[:, :cut]),
        (1, slice(0, 3 * D - cut), w_qkv.at[:, cut:]),
    ]


def normed(values, gain):
    inverse = lax.rsqrt(jnp.mean(values * values, axis=-1, keepdims=True) + NORM_EPS)
    scaled = values * inverse
    return scaled, inverse, (scaled * gain).astype(BF)


def norm_back(values, gain, grads, gain_grad_ref):
    inverse = lax.rsqrt(jnp.mean(values * values, axis=-1, keepdims=True) + NORM_EPS)
    scaled = values * inverse
    add_rows(gain_grad_ref, jnp.sum(scaled * grads, axis=0, keepdims=True))
    weighted = grads * gain
    centre = jnp.mean(scaled * weighted, axis=-1, keepdims=True)
    return inverse * (weighted - scaled * centre)


def add_rows(total_ref, row):
    row_id = lax.broadcasted_iota(jnp.int32, (8, D), 0)
    addend = jnp.where(row_id == 0, row, 0.0)

    @pl.when(pl.program_id(0) == 0)
    def _():
        total_ref[...] = addend

    @pl.when(pl.program_id(0) > 0)
    def _():
        total_ref[...] += addend


def keep_largest(total_ref, values):
    head = lax.broadcasted_iota(jnp.int32, (D, LANES), 0) // HEAD_DIM
    lane = lax.broadcasted_iota(jnp.int32, (D, LANES), 1)
    hot = jnp.where(head == lane, 1.0, 0.0).astype(BF)
    values = values.astype(F32)
    squares = nn((values * values).astype(BF), hot)
    row = jnp.broadcast_to(jnp.max(squares, axis=0, keepdims=True), (8, LANES))

    @pl.when(pl.program_id(0) == 0)
    def _():
        total_ref[...] = row

    @pl.when(pl.program_id(0) > 0)
    def _():
        total_ref[...] = jnp.maximum(total_ref[...], row)


def key_value_kernel(core_ref, own_ref, other_ref, rows_ref, kv_ref, size_ref, w_kv, sems):
    halves_loaded(core_ref, own_ref, other_ref, key_value_pieces(w_kv), sems)
    kv_ref[...] = nn(rows_ref[...], w_kv[...]).astype(BF)
    keep_largest(size_ref, kv_ref[:, :D])


def key_value(core, own, other, rows, steps, index, us):
    return pl.pallas_call(
        key_value_kernel,
        grid=(steps,),
        in_specs=[SMEM, ANY, ANY, pl.BlockSpec((BLOCK, D), index)],
        out_specs=[row_block(2 * D), fixed_block(8, LANES)],
        out_shape=[shape(steps * BLOCK, 2 * D), shape(8, LANES, F32)],
        scratch_shapes=[pltpu.VMEM((D, 2 * D), BF), pltpu.SemaphoreType.DMA((1,))],
        compiler_params=params(),
        cost_estimate=cost(us),
        name="key_value",
    )(core, own, other, rows)


def self_inputs_kernel(
    core_ref, own_ref, other_ref, x_ref, h_ref, qkv_ref, gains_ref, w_qkv, gain_columns, sems
):
    first_gain = 5 * D - HALF_COLUMNS
    pieces = query_pieces(w_qkv)
    pieces.append((1, slice(first_gain, first_gain + LANES), gain_columns))
    halves_loaded(core_ref, own_ref, other_ref, pieces, sems)

    @pl.when(pl.program_id(0) == 0)
    def _():
        gains_ref[...] = gain_columns[...].astype(F32).T[:8]

    h_ref[...] = normed(x_ref[...].astype(F32), gains_ref[:1, :])[2]
    qkv_ref[...] = nn(h_ref[...], w_qkv[...]).astype(BF)


def self_inputs(core, own, other, x):
    return pl.pallas_call(
        self_inputs_kernel,
        grid=(ROWS // BLOCK,),
        in_specs=[SMEM, ANY, ANY, row_block(D)],
        out_specs=[row_block(D), row_block(3 * D), fixed_block(8, D)],
        out_shape=[shape(ROWS, D), shape(ROWS, 3 * D), shape(8, D, F32)],
        scratch_shapes=[
            pltpu.VMEM((D, 3 * D), BF),
            pltpu.VMEM((D, LANES), BF),
            pltpu.SemaphoreType.DMA((3,)),
        ],
        compiler_params=params(),
        cost_estimate=cost(6),
        name="self_inputs",
    )(core, own, other, x)


def cross_inputs_kernel(
    core_ref, own_ref, other_ref, gain_ref, x_ref, o_ref,
    x1_ref, h_ref, q_ref, size_ref, weights, sems,
):
    halves_loaded(core_ref, own_ref, other_ref, out_query_pieces(weights), sems)
    x1 = x_ref[...].astype(F32) + nn(o_ref[...], weights[:, :D])
    x1_ref[...] = x1
    h_ref[...] = normed(x1, gain_ref[1:2, :])[2]
    q_ref[...] = nn(h_ref[...], weights[:, D:]).astype(BF)
    keep_largest(size_ref, q_ref[...])


def cross_inputs(core, own, other, gain, x, o1):
    return pl.pallas_call(
        cross_inputs_kernel,
        grid=(ROWS // BLOCK,),
        in_specs=[SMEM, ANY, ANY, fixed_block(8, D), row_block(D), row_block(D)],
        out_specs=[row_block(D)] * 3 + [fixed_block(8, LANES)],
        out_shape=[shape(ROWS, D, F32), shape(ROWS, D), shape(ROWS, D), shape(8, LANES, F32)],
        scratch_shapes=[pltpu.VMEM((D, 2 * D), BF), pltpu.SemaphoreType.DMA((2,))],
        compiler_params=params(),
        cost_estimate=cost(5),
        name="cross_inputs",
    )(core, own, other, gain, x, o1)


def ffn_kernel(
    core_ref, late_ref, own_ref, other_ref, gain_ref, x1_ref, o_ref, dy_ref,
    out_ref, h_ref, acts_ref, db_ref, dx_ref, do_ref, gain_grad_ref,
    w_out, w_gate, w_up, w_down, sems,
):
    width = w_gate.shape[1]
    first = pl.program_id(0) == 0
    copies = [
        pltpu.make_async_copy(late_ref.at[:, :D], w_out, sems.at[0]),
        pltpu.make_async_copy(late_ref.at[:, D : D + width], w_gate, sems.at[1]),
        pltpu.make_async_copy(late_ref.at[:, D + width :], w_up, sems.at[2]),
    ]

    def down_copies(side):
        halves = (own_ref, other_ref) if side == 0 else (other_ref, own_ref)
        columns = [slice(half * D // 2, (half + 1) * D // 2) for half in range(2)]
        return [
            pltpu.make_async_copy(halves[half], w_down.at[:, columns[half]], sems.at[3 + half])
            for half in range(2)
        ]

    @pl.when(first)
    def _():
        for copy in copies:
            copy.start()
        for side in range(2):

            @pl.when(core_ref[0] == side)
            def _():
                for copy in down_copies(side):
                    copy.start()

    def arrived(place):
        @pl.when(first)
        def _():
            copies[place].wait()

    arrived(0)
    x2 = x1_ref[...] + nn(o_ref[...], w_out[...])
    h_ref[...] = normed(x2, gain_ref[2:3, :])[2]
    dy_low = dy_ref[...]
    arrived(1)
    arrived(2)

    @pl.when(first)
    def _():
        for side in range(2):

            @pl.when(core_ref[0] == side)
            def _():
                for copy in down_copies(side):
                    copy.wait()

    scale = math.sqrt(2.0 / math.pi)
    out, dh = x2, 0.0
    h = h_ref[...]
    for start in range(0, width, FFN_CHUNK):
        part = slice(start, start + FFN_CHUNK)
        gate = nn(h, w_gate[:, part])
        up = nn(h, w_up[:, part])
        d_hidden = nt(dy_low, w_down[part, :])
        square = gate * gate
        turn = jnp.tanh(gate * (scale + (scale * 0.044715) * square))
        half = 0.5 + 0.5 * turn
        gelu = gate * half
        bend = gate * (0.5 * scale + (0.5 * scale * 3 * 0.044715) * square)
        slope = half + (1.0 - turn * turn) * bend
        hidden = (gelu * up).astype(BF)
        d_gate = (d_hidden * up * slope).astype(BF)
        d_up = (d_hidden * gelu).astype(BF)
        acts_ref[0, :, part] = d_gate
        acts_ref[1, :, part] = d_up
        acts_ref[2, :, part] = hidden
        out = out + nn(hidden, w_down[part, :])
        dh = dh + nt(d_gate, w_gate[:, part]) + nt(d_up, w_up[:, part])
    out_ref[...] = out.astype(BF)
    dx = dy_low.astype(F32) + norm_back(x2, gain_ref[2:3, :], dh, gain_grad_ref)
    dx_ref[...] = dx
    db_ref[...] = dx.astype(BF)
    do_ref[...] = nt(db_ref[...], w_out[...]).astype(BF)


def ffn(core, late, own, other, gain, x1, o2, dy):
    width = own.shape[0]
    return pl.pallas_call(
        ffn_kernel,
        grid=(ROWS // BLOCK,),
        in_specs=[SMEM, ANY, ANY, ANY, fixed_block(8, D), row_block(D), row_block(D), row_block(D)],
        out_specs=[
            row_block(D),
            row_block(D),
            pl.BlockSpec((3, BLOCK, width), lambda i: (0, i, 0)),
            row_block(D),
            row_block(D),
            row_block(D),
            fixed_block(8, D),
        ],
        out_shape=[
            shape(ROWS, D),
            shape(ROWS, D),
            jax.ShapeDtypeStruct((3, ROWS, width), BF),
            shape(ROWS, D),
            shape(ROWS, D, F32),
            shape(ROWS, D),
            shape(8, D, F32),
        ],
        scratch_shapes=[
            pltpu.VMEM((D, D), BF),
            pltpu.VMEM((D, width), BF),
            pltpu.VMEM((D, width), BF),
            pltpu.VMEM((width, D), BF),
            pltpu.SemaphoreType.DMA((5,)),
        ],
        compiler_params=params(),
        cost_estimate=cost(30),
        name="ffn",
    )(core, far(late), far(own), far(other), gain, far(x1), o2, far(dy))


def self_grads_kernel(
    core_ref, own_ref, other_ref, gain_ref, x1_ref, dx2_ref, dq0_ref, dq1_ref,
    dx1_ref, db_ref, do_ref, gain_grad_ref, weights, sems,
):
    halves_loaded(core_ref, own_ref, other_ref, out_query_pieces(weights), sems)
    low = pl.program_id(0) < TGT_LEN // BLOCK
    dh = nt(jnp.where(low, dq0_ref[...], dq1_ref[...]), weights[:, D:])
    dx1 = dx2_ref[...] + norm_back(x1_ref[...], gain_ref[1:2, :], dh, gain_grad_ref)
    dx1_ref[...] = dx1
    db_ref[...] = dx1.astype(BF)
    do_ref[...] = nt(db_ref[...], weights[:, :D]).astype(BF)


def self_grads(core, own, other, gain, x1, dx2, dq2):
    half = TGT_LEN // BLOCK
    return pl.pallas_call(
        self_grads_kernel,
        grid=(ROWS // BLOCK,),
        in_specs=[
            SMEM,
            ANY,
            ANY,
            fixed_block(8, D),
            row_block(D),
            row_block(D),
            pl.BlockSpec((BLOCK, D), lambda i: (jnp.minimum(i, half - 1), 0)),
            pl.BlockSpec((BLOCK, D), lambda i: (jnp.maximum(i - half, 0), 0)),
        ],
        out_specs=[row_block(D), row_block(D), row_block(D), fixed_block(8, D)],
        out_shape=[shape(ROWS, D, F32), shape(ROWS, D), shape(ROWS, D), shape(8, D, F32)],
        scratch_shapes=[pltpu.VMEM((D, 2 * D), BF), pltpu.SemaphoreType.DMA((2,))],
        compiler_params=params(),
        cost_estimate=cost(5),
        name="self_grads",
    )(core, far(own), far(other), gain, far(x1), far(dx2), *dq2)


def input_grads_kernel(
    core_ref, own_ref, other_ref, gain_ref, x_ref, dx1_ref, dqkv_ref,
    dx_ref, gain_grad_ref, w_qkv, sems,
):
    halves_loaded(core_ref, own_ref, other_ref, query_pieces(w_qkv), sems)
    dh = (
        nt(dqkv_ref[0], w_qkv[:, :D])
        + nt(dqkv_ref[1], w_qkv[:, D : 2 * D])
        + nt(dqkv_ref[2], w_qkv[:, 2 * D :])
    )
    x = x_ref[...].astype(F32)
    dx_ref[...] = (dx1_ref[...] + norm_back(x, gain_ref[:1, :], dh, gain_grad_ref)).astype(BF)


def input_grads(core, own, other, gain, x, dx1, dqkv):
    return pl.pallas_call(
        input_grads_kernel,
        grid=(ROWS // BLOCK,),
        in_specs=[
            SMEM, ANY, ANY, fixed_block(8, D), row_block(D), row_block(D),
            pl.BlockSpec((3, BLOCK, D), lambda i: (0, i, 0)),
        ],
        out_specs=[row_block(D), fixed_block(8, D)],
        out_shape=[shape(ROWS, D), shape(8, D, F32)],
        scratch_shapes=[pltpu.VMEM((D, 3 * D), BF), pltpu.SemaphoreType.DMA((2,))],
        compiler_params=params(),
        cost_estimate=cost(6),
        name="input_grads",
    )(core, far(own), far(other), gain, far(x), dx1, dqkv)


def memory_grads_kernel(core_ref, own_ref, other_ref, dkv_ref, dm_ref, w_kv, sems):
    halves_loaded(core_ref, own_ref, other_ref, key_value_pieces(w_kv), sems)
    dm_ref[...] = (nt(dkv_ref[0], w_kv[:, :D]) + nt(dkv_ref[1], w_kv[:, D:])).astype(BF)


def memory_grads(core, own, other, dkv):
    rows = dkv.shape[1]
    return pl.pallas_call(
        memory_grads_kernel,
        grid=(rows // BLOCK,),
        in_specs=[SMEM, ANY, ANY, pl.BlockSpec((2, BLOCK, D), lambda i: (0, i, 0))],
        out_specs=row_block(D),
        out_shape=shape(rows, D),
        scratch_shapes=[pltpu.VMEM((D, 2 * D), BF), pltpu.SemaphoreType.DMA((1,))],
        compiler_params=params(),
        cost_estimate=cost(rows / 400),
        name="memory_grads",
    )(core, own, other, dkv)


def stored_by_core(core_ref, grad, give_ref, keep_ref):
    across, _, count = give_ref.shape[0], 2, give_ref.shape[1]
    for side in range(2):

        @pl.when(core_ref[0] == side)
        def _():
            for place in range(across):
                first = place * 2 * count
                here, there = first + side * count, first + (1 - side) * count
                keep_ref[place] = grad[here : here + count].astype(BF)
                give_ref[place] = grad[there : there + count].astype(BF)


def row_grads_kernel(core_ref, rows_ref, grads_ref, give_ref, keep_ref, turned):
    @pl.when(pl.program_id(0) == 0)
    def _():
        turned[...] = rows_ref[...].T

    stored_by_core(core_ref, nn(turned[...], grads_ref[0]), give_ref, keep_ref)


def row_grads(core, rows, grads, across, us):
    units, length = grads.shape[0], grads.shape[1]
    count = D // (2 * across)
    block = pl.BlockSpec((across, count, D), lambda u: (0, 0, u))
    piece = jax.ShapeDtypeStruct((across, count, units * D), BF)
    return pl.pallas_call(
        row_grads_kernel,
        grid=(units,),
        in_specs=[SMEM, fixed_block(length, D), pl.BlockSpec((1, length, D), lambda u: (u, 0, 0))],
        out_specs=[block, block],
        out_shape=[piece, piece],
        scratch_shapes=[pltpu.VMEM((D, length), BF)],
        compiler_params=params(),
        cost_estimate=cost(us),
        name="row_grads",
    )(core, rows, grads)


def pair_grads_kernel(counts, core_ref, *refs):
    give_ref, keep_ref = refs[-2:]
    used = 0
    for place, count in enumerate(counts):
        turned = refs[used][...].T
        length = turned.shape[1] // count
        grad = sum(
            nn(turned[:, part * length : (part + 1) * length], refs[used + 1 + part][...])
            for part in range(count)
        )
        used += 1 + count
        columns = slice(place * D, (place + 1) * D)
        stored_by_core(core_ref, grad, give_ref.at[:, :, columns], keep_ref.at[:, :, columns])


def pair_grads(core, pairs, across):
    count = D // (2 * across)
    piece = jax.ShapeDtypeStruct((across, count, len(pairs) * D), BF)
    whole = pl.BlockSpec(memory_space=pltpu.VMEM)
    flat = [array for rows, grads in pairs for array in (rows,) + tuple(grads)]
    return pl.pallas_call(
        functools.partial(pair_grads_kernel, [len(grads) for _, grads in pairs]),
        in_specs=[SMEM] + [whole] * len(flat),
        out_specs=[whole, whole],
        out_shape=[piece, piece],
        compiler_params=params(),
        cost_estimate=cost(2.5 * len(pairs)),
        name="pair_grads",
    )(core, *flat)


def ffn_weight_grads_kernel(h_ref, acts_ref, dy_ref, out_ref):
    devices = out_ref.shape[0]
    width = acts_ref.shape[2]

    @pl.when(pl.program_id(0) < 2)
    def _():
        turned = h_ref[...].T
        share = D // devices
        for first in range(0, width, 2 * WIDE):
            both = [
                nn(turned, acts_ref[0, :, place : place + WIDE]).reshape(devices, share, WIDE)
                for place in (first, first + WIDE)
            ]
            row = first // WIDE * share
            out_ref[:, row : row + 2 * share, :] = jnp.concatenate(both, axis=1).astype(BF)

    @pl.when(pl.program_id(0) == 2)
    def _():
        turned = acts_ref[0].T
        share = width // devices
        for place in range(D // WIDE):
            grad = nn(turned, dy_ref[:, place * WIDE : (place + 1) * WIDE])
            out_ref[:, place * share : (place + 1) * share, :] = grad.reshape(
                devices, share, WIDE
            ).astype(BF)


def ffn_weight_grads(h3, acts, dy, devices):
    width = acts.shape[2]
    rows = D * width // WIDE // devices
    return pl.pallas_call(
        ffn_weight_grads_kernel,
        grid=(3,),
        in_specs=[
            fixed_block(ROWS, D),
            pl.BlockSpec((1, ROWS, width), lambda u: (u, 0, 0)),
            fixed_block(ROWS, D),
        ],
        out_specs=pl.BlockSpec((devices, rows, WIDE), lambda u: (0, u, 0)),
        out_shape=jax.ShapeDtypeStruct((devices, 3 * rows, WIDE), BF),
        compiler_params=params(),
        cost_estimate=cost(13),
        name="ffn_weight_grads",
    )(h3, far(acts), far(dy))


def memory_weight_grads_kernel(
    core_ref, mem_ref, next_ref, own0_ref, own1_ref, after0_ref, after1_ref,
    give_ref, keep_ref, turned,
):
    @pl.when(pl.program_id(0) == 0)
    def _():
        for m in range(MICRO):
            turned[:, m * OWN : (m + 1) * OWN] = mem_ref[m, 0, MEM_DEV - OWN :, :].T
        turned[:, MICRO * OWN :] = next_ref[...].T

    grad, used = 0.0, 0
    for part_ref in (own0_ref, own1_ref, after0_ref, after1_ref):
        length = part_ref.shape[1]
        grad = grad + nn(turned[:, used : used + length], part_ref[0])
        used += length
    stored_by_core(core_ref, grad, give_ref, keep_ref)


def memory_weight_grads(core, memory, next_rows, dkv_own, dkv_next, across):
    count = D // (2 * across)
    block = pl.BlockSpec((across, count, D), lambda u: (0, 0, u))
    piece = jax.ShapeDtypeStruct((across, count, 2 * D), BF)
    return pl.pallas_call(
        memory_weight_grads_kernel,
        grid=(2,),
        in_specs=[
            SMEM,
            pl.BlockSpec((MICRO, 1, MEM_DEV, D), lambda u: (0, 0, 0, 0)),
            fixed_block(MICRO * NEXT, D),
        ]
        + [pl.BlockSpec((1, OWN, D), lambda u: (u, 0, 0))] * MICRO
        + [pl.BlockSpec((1, NEXT, D), lambda u: (u, 0, 0))] * MICRO,
        out_specs=[block, block],
        out_shape=[piece, piece],
        scratch_shapes=[pltpu.VMEM((D, MICRO * (OWN + NEXT)), BF)],
        compiler_params=params(),
        cost_estimate=cost(8),
        name="memory_weight_grads",
    )(core, memory, next_rows, *dkv_own, *dkv_next)


def memory_total_kernel(core_ref, own_ref, other_ref, dkv_ref, prev_ref, dm_ref, w_kv, sems):
    halves_loaded(core_ref, own_ref, other_ref, key_value_pieces(w_kv), sems)
    block = pl.program_id(0)

    @pl.when(block == 0)
    def _():
        dm_ref[...] = prev_ref[...]

    @pl.when(block > 0)
    def _():
        grads = nt(dkv_ref[0], w_kv[:, :D]) + nt(dkv_ref[1], w_kv[:, D:])
        shared = jnp.where(block == 1, prev_ref[...].astype(F32), 0.0)
        dm_ref[...] = (grads + shared).astype(BF)


def memory_total(core, own, other, dkv, prev):
    return pl.pallas_call(
        memory_total_kernel,
        grid=(MEM_DEV // BLOCK,),
        in_specs=[
            SMEM,
            ANY,
            ANY,
            pl.BlockSpec((2, BLOCK, D), lambda i: (0, jnp.maximum(i - 1, 0), 0)),
            pl.BlockSpec((BLOCK, D), lambda i: (jnp.minimum(i, 1), 0)),
        ],
        out_specs=row_block(D),
        out_shape=shape(MEM_DEV, D),
        scratch_shapes=[pltpu.VMEM((D, 2 * D), BF), pltpu.SemaphoreType.DMA((1,))],
        compiler_params=params(),
        cost_estimate=cost(4),
        name="memory_total",
    )(core, own, other, dkv, prev)


def extras_kernel(share, core_ref, sums_ref, first_ref, second_ref, third_ref, give_ref, keep_ref):
    row_id = lax.broadcasted_iota(jnp.int32, (8, D), 0)
    norms = jnp.zeros((8, D), F32)
    for place, ref in enumerate((first_ref, second_ref, third_ref)):
        norms = jnp.where(row_id == place, ref[:1, :], norms)
    stacked = jnp.concatenate([norms, jnp.zeros((LANES - 8, D), F32)], axis=0).T
    distance = lax.broadcasted_iota(jnp.int32, (HALF, LANES), 0)
    bucket_id = lax.broadcasted_iota(jnp.int32, (HALF, LANES), 1)
    exact_count = BUCKETS // 2
    bucket = jnp.full((HALF, LANES), exact_count, jnp.int32)
    for threshold in bucket_limits(BUCKETS, REACH):
        bucket = bucket + (distance >= threshold).astype(jnp.int32)
    bucket = jnp.where(distance < exact_count, distance, bucket)
    sums = sums_ref[...]
    together = LANES // BUCKETS
    lines = [jnp.zeros((1, LANES), F32) for _ in range(HEADS // together)]
    for part in range(together):
        near_hot = (bucket == bucket_id - part * BUCKETS).astype(F32)
        far_hot = (bucket_id == (part + 1) * BUCKETS - 1).astype(F32)
        table = sum(
            lax.dot_general(
                sums[:, place, :], hot, (((1,), (0,)), ((), ())),
                precision=lax.Precision.HIGHEST, preferred_element_type=F32,
            )
            for place, hot in ((0, near_hot), (1, far_hot))
        )
        for line in range(len(lines)):
            head = line * together + part
            lines[line] = lines[line] + table[head : head + 1]
    row_in_share = lax.broadcasted_iota(jnp.int32, (D, LANES), 0) % share
    tall = jnp.zeros((D, LANES), F32)
    for line, row in enumerate(lines):
        tall = jnp.where(row_in_share == line, row, tall)
    both = jnp.concatenate([stacked, tall], axis=1)
    stored_by_core(core_ref, both, give_ref, keep_ref)


def extras(core, sums, norms, across, share):
    piece = jax.ShapeDtypeStruct((across, D // (2 * across), 2 * LANES), BF)
    whole = pl.BlockSpec(memory_space=pltpu.VMEM)
    return pl.pallas_call(
        functools.partial(extras_kernel, share),
        in_specs=[SMEM] + [whole] * 4,
        out_specs=[whole, whole],
        out_shape=[piece, piece],
        compiler_params=params(),
        cost_estimate=cost(2),
        name="extras",
    )(core, sums, *norms)


def packed_kernel(core_ref, *refs):
    here_ref, there_ref = refs[-2:]
    joined = jnp.concatenate([ref[...] for ref in refs[:-2]], axis=1)
    halves = joined[:, :HALF_COLUMNS], joined[:, HALF_COLUMNS:]
    for side in range(2):

        @pl.when(core_ref[0] == side)
        def _():
            here_ref[...] = halves[side]
            there_ref[...] = halves[1 - side]


def packed(core, parts):
    whole = pl.BlockSpec(memory_space=pltpu.VMEM)
    piece = shape(parts[0].shape[0], HALF_COLUMNS)
    return pl.pallas_call(
        packed_kernel,
        in_specs=[SMEM] + [whole] * len(parts),
        out_specs=[whole, whole],
        out_shape=[piece, piece],
        compiler_params=params(),
        cost_estimate=cost(1),
        name="packed",
    )(core, *parts)


def assembled_kernel(place_ref, *refs):
    out_ref = refs[-1]
    for step, piece_ref in enumerate(refs[:-1]):

        @pl.when(pl.program_id(0) == step)
        def _():
            out_ref[0, :, 0] = piece_ref[...]


def assembled(place, pieces):
    count, rows, columns = pieces[0].shape
    return pl.pallas_call(
        assembled_kernel,
        grid_spec=pltpu.PrefetchScalarGridSpec(
            num_scalar_prefetch=1,
            grid=(4,),
            in_specs=[pl.BlockSpec((count, rows, columns), lambda i, place: (0, 0, 0))] * 4,
            out_specs=pl.BlockSpec(
                (1, count, 1, rows, columns),
                lambda i, place: (place[0] ^ (i // 2), 0, place[1] ^ (i % 2), 0, 0),
            ),
        ),
        out_shape=jax.ShapeDtypeStruct((2, count, 2, rows, columns), BF),
        compiler_params=params(),
        cost_estimate=cost(3),
        name="assembled",
    )(place, *pieces)


def bias_tiles_kernel(table_ref, tiles_ref):
    head = pl.program_id(0)
    key_id = lax.broadcasted_iota(jnp.int32, (HALF, HALF), 0)
    query_id = lax.broadcasted_iota(jnp.int32, (HALF, HALF), 1)
    limits = bucket_limits(BUCKETS, REACH)
    exact_count = BUCKETS // 2
    for tile in range(2):
        distance = query_id - key_id + tile * HALF
        grid = jnp.full((HALF, HALF), table_ref[head, 0], F32)
        for bucket in range(1, BUCKETS):
            start = bucket if bucket <= exact_count else limits[bucket - exact_count - 1]
            grid = jnp.where(distance >= start, table_ref[head, bucket], grid)
        if tile == 0:
            grid = jnp.where(distance >= 0, grid, MASKED)
        tiles_ref[0, tile] = grid


def bias_tiles(table):
    return pl.pallas_call(
        bias_tiles_kernel,
        grid=(HEADS,),
        in_specs=[pl.BlockSpec(memory_space=pltpu.SMEM)],
        out_specs=pl.BlockSpec((1, 2, HALF, HALF), lambda h: (h, 0, 0, 0)),
        out_shape=jax.ShapeDtypeStruct((HEADS, 2, HALF, HALF), F32),
        cost_estimate=cost(8),
        name="bias_tiles",
    )(table)


def put_lse(lse_ref, rows):
    row_id = lax.broadcasted_iota(jnp.int32, (8, TGT_LEN), 0)
    lse_ref[0] = jnp.where(row_id == 0, rows[0], rows[1])


def attended(scores, value, small):
    top = 0.0 if small else jnp.max(scores, axis=0, keepdims=True)
    weights = jnp.exp(scores if small else scores - top).astype(BF)
    both = nn(value, weights)
    total = both[HEAD_DIM : HEAD_DIM + 1]
    return both[:HEAD_DIM] * (1.0 / total), top + jnp.log(total)


def cross_forward_kernel(
    small_ref, q_ref, ko_ref, kn_ref, vo_ref, vn_ref, mask_ref, o_ref, lse_ref, k_ext
):
    def run(small):
        k_ext[:OWN, :LANES] = ko_ref[...]
        k_ext[OWN:, :LANES] = kn_ref[...]
        k_ext[:, LANES:] = mask_ref[0]
        q_t = q_ref[...].T
        v_t = jnp.concatenate([vo_ref[...], vn_ref[...]], axis=0).T
        ones = extra_rows(TGT_LEN, 1.0, ())
        rows_of_ones = jnp.ones((16, KEYS), BF)
        scores = [
            nn(k_ext[...], jnp.concatenate([head_rows(q_t, head), ones], axis=0))
            for head in range(2)
        ]
        values = [
            jnp.concatenate([v_t[head * HEAD_DIM : (head + 1) * HEAD_DIM], rows_of_ones], axis=0)
            for head in range(2)
        ]
        mixed, lses = zip(*[attended(scores[head], values[head], small) for head in range(2)])
        o_ref[...] = jnp.concatenate(mixed, axis=0).T.astype(BF)
        put_lse(lse_ref, lses)

    @pl.when(small_ref[0] == 1)
    def _():
        run(True)

    @pl.when(small_ref[0] != 1)
    def _():
        run(False)


def cross_backward_kernel(
    q_ref, ko_ref, kn_ref, vo_ref, vn_ref, mask_ref, o_ref, do_ref, lse_ref,
    dq_ref, own_ref, next_ref, k_ext, v_ext,
):
    k_ext[:OWN, :LANES] = ko_ref[...]
    k_ext[OWN:, :LANES] = kn_ref[...]
    k_ext[:, LANES:] = mask_ref[0]
    v_ext[:OWN, :LANES] = vo_ref[...]
    v_ext[OWN:, :LANES] = vn_ref[...]
    v_ext[:, LANES:] = jnp.ones((KEYS, LANES), BF)
    k_t = k_ext[:, :LANES].T
    q = q_ref[...]
    d_o = do_ref[...]
    q_t = q.T
    do_t = d_o.T
    centre_t = (o_ref[...].astype(F32) * d_o.astype(F32)).T
    dq, dk, dv = [], [], []
    for head in range(2):
        rows = slice(head * HEAD_DIM, (head + 1) * HEAD_DIM)
        lse = lse_ref[0, head : head + 1, :]
        centre = jnp.sum(centre_t[rows], axis=0, keepdims=True)
        query = jnp.concatenate(
            [head_rows(q_t, head), extra_rows(TGT_LEN, 1.0, three_parts(-lse))], axis=0
        )
        grad = jnp.concatenate(
            [head_rows(do_t, head), extra_rows(TGT_LEN, 0.0, three_parts(-centre))], axis=0
        )
        probs = jnp.exp(nn(k_ext[...], query))
        grad_scores = (probs * nn(v_ext[...], grad)).astype(BF)
        dv.append(nn(probs.astype(BF), d_o))
        dk.append(nn(grad_scores, q))
        dq.append(nn(k_t[rows], grad_scores))
    dq_ref[...] = jnp.concatenate(dq, axis=0).T.astype(BF)
    lane = lax.broadcasted_iota(jnp.int32, (KEYS, LANES), 1)
    dk_pair = jnp.where(lane < HEAD_DIM, dk[0], dk[1]).astype(BF)
    dv_pair = jnp.where(lane < HEAD_DIM, dv[0], dv[1]).astype(BF)
    for place, pair in enumerate((dk_pair, dv_pair)):
        own_ref[place] = pair[:OWN]
        next_ref[place] = pair[OWN:]


def self_forward_kernel(q_ref, k_ref, v_ref, tiles_ref, o_ref, lse_ref):
    k = k_ref[...]
    q_t = q_ref[...].T
    v_t = v_ref[...].T
    rows_of_ones = jnp.ones((16, TGT_LEN), BF)
    queries = [head_rows(q_t, head) for head in range(2)]
    raws = [(nn(k[:HALF], query[:, :HALF]), nn(k, query[:, HALF:])) for query in queries]
    mixed, lses = [], []
    for head in range(2):
        rows = slice(head * HEAD_DIM, (head + 1) * HEAD_DIM)
        value = jnp.concatenate([v_t[rows], rows_of_ones], axis=0)
        near, far = tiles_ref[head, 0], tiles_ref[head, 1]
        first, raw = raws[head]
        out0, l0 = attended(first + near, value[:, :HALF], False)
        scores = jnp.concatenate([raw[:HALF] + far, raw[HALF:] + near], axis=0)
        out1, l1 = attended(scores, value, False)
        mixed.append(jnp.concatenate([out0, out1], axis=1))
        lses.append(jnp.concatenate([l0, l1], axis=1))
    o_ref[...] = jnp.concatenate(mixed, axis=0).T.astype(BF)
    put_lse(lse_ref, lses)


def distance_sums(near, far):
    key_id = lax.broadcasted_iota(jnp.int32, (HALF, HALF), 0)
    query_id = lax.broadcasted_iota(jnp.int32, (HALF, HALF), 1)
    close = (query_id - key_id + HALF) < REACH
    both = near + jnp.where(close, far, 0.0)
    group = both[:8]
    for first in range(8, HALF, 8):
        group = group + pltpu.roll(both[first : first + 8], HALF - first, 1)
    row_id = lax.broadcasted_iota(jnp.int32, (8, HALF), 0)
    turned = group
    for row in range(1, 8):
        turned = jnp.where(row_id == row, pltpu.roll(group, HALF - row, 1), turned)
    by_distance = jnp.sum(turned, axis=0, keepdims=True)
    rest = jnp.sum(jnp.where(close, 0.0, far), axis=0, keepdims=True)
    return jnp.where(row_id == 0, by_distance, jnp.where(row_id == 1, rest, 0.0))


def self_backward_kernel(
    q_ref, k_ref, v_ref, tiles_ref, o_ref, do_ref, lse_ref,
    dqkv_ref, sums_ref, k_ext, v_ext, near_ref, far_ref,
):
    row_ext = jnp.ones((TGT_LEN, LANES), BF)
    k_ext[:, :LANES] = k_ref[...]
    k_ext[:, LANES:] = row_ext
    v_ext[:, :LANES] = v_ref[...]
    v_ext[:, LANES:] = row_ext
    k_t = k_ref[...].T
    q = q_ref[...]
    d_o = do_ref[...]
    q_t = q.T
    do_t = d_o.T
    centre_t = (o_ref[...].astype(F32) * d_o.astype(F32)).T
    first = pl.program_id(1) == 0
    dq, dk, dv = [], [], []
    for head in range(2):
        rows = slice(head * HEAD_DIM, (head + 1) * HEAD_DIM)
        lse = lse_ref[0, head : head + 1, :]
        centre = jnp.sum(centre_t[rows], axis=0, keepdims=True)
        query = jnp.concatenate(
            [head_rows(q_t, head), extra_rows(TGT_LEN, 0.0, three_parts(-lse))], axis=0
        )
        grad = jnp.concatenate(
            [head_rows(do_t, head), extra_rows(TGT_LEN, 0.0, three_parts(-centre))], axis=0
        )
        near, far = tiles_ref[head, 0], tiles_ref[head, 1]
        raw0 = nn(k_ext[:HALF, :], query[:, :HALF])
        raw1 = nn(k_ext[...], query[:, HALF:])
        p00 = jnp.exp(raw0 + near)
        p10 = jnp.exp(raw1[:HALF] + far)
        p11 = jnp.exp(raw1[HALF:] + near)
        g0 = nn(v_ext[:HALF, :], grad[:, :HALF])
        g1 = nn(v_ext[...], grad[:, HALF:])
        s00 = p00 * g0
        s10 = p10 * g1[:HALF]
        s11 = p11 * g1[HALF:]
        near_sum, far_sum = s00 + s11, s10

        @pl.when(first)
        def _():
            near_ref[head] = near_sum
            far_ref[head] = far_sum

        @pl.when(jnp.logical_not(first))
        def _():
            sums_ref[head] = distance_sums(near_ref[head] + near_sum, far_ref[head] + far_sum)

        b00, b10, b11 = s00.astype(BF), s10.astype(BF), s11.astype(BF)
        w00, w10, w11 = p00.astype(BF), p10.astype(BF), p11.astype(BF)
        top = jnp.concatenate([w00, w10], axis=1)
        dv.append(jnp.concatenate([nn(top, d_o), nn(w11, d_o[HALF:])], axis=0))
        top = jnp.concatenate([b00, b10], axis=1)
        dk.append(jnp.concatenate([nn(top, q), nn(b11, q[HALF:])], axis=0))
        dq.append(
            jnp.concatenate(
                [
                    nn(k_t[rows, :HALF], b00),
                    nn(k_t[rows], jnp.concatenate([b10, b11], axis=0)),
                ],
                axis=1,
            )
        )
    dqkv_ref[0] = jnp.concatenate(dq, axis=0).T.astype(BF)
    lane = lax.broadcasted_iota(jnp.int32, (TGT_LEN, LANES), 1)
    dqkv_ref[1] = jnp.where(lane < HEAD_DIM, dk[0], dk[1]).astype(BF)
    dqkv_ref[2] = jnp.where(lane < HEAD_DIM, dv[0], dv[1]).astype(BF)


PAIR_GRID = (MICRO, PAIRS)


def pair_block(rows, offset=0):
    return pl.BlockSpec((rows, LANES), lambda m, p: (m, p + offset))


LSE_BLOCK = pl.BlockSpec((1, 8, TGT_LEN), lambda m, p: (m * PAIRS + p, 0, 0))
LSE_SHAPE = jax.ShapeDtypeStruct((MICRO * PAIRS, 8, TGT_LEN), F32)
MASK_BLOCK = pl.BlockSpec((1, KEYS, LANES), lambda m, p: (m, 0, 0))


def cross_forward(small, q, kv_own, kv_next, mask):
    return pl.pallas_call(
        cross_forward_kernel,
        grid=PAIR_GRID,
        in_specs=[
            SMEM,
            pair_block(TGT_LEN),
            pair_block(OWN),
            pair_block(NEXT),
            pair_block(OWN, PAIRS),
            pair_block(NEXT, PAIRS),
            MASK_BLOCK,
        ],
        out_specs=[pair_block(TGT_LEN), LSE_BLOCK],
        out_shape=[jax.ShapeDtypeStruct((ROWS, D), BF), LSE_SHAPE],
        scratch_shapes=[pltpu.VMEM((KEYS, 2 * LANES), BF)],
        compiler_params=params(),
        cost_estimate=cost(32),
        name="cross_forward",
    )(small, q, kv_own, kv_next, kv_own, kv_next, mask)


def cross_backward(m, q, kv_own, kv_next, mask, o, d_o, lse):
    def block(rows, offset=0):
        return pl.BlockSpec((rows, LANES), lambda p: (m, p + offset))

    return pl.pallas_call(
        cross_backward_kernel,
        grid=(PAIRS,),
        in_specs=[
            block(TGT_LEN),
            block(OWN),
            block(NEXT),
            block(OWN, PAIRS),
            block(NEXT, PAIRS),
            pl.BlockSpec((1, KEYS, LANES), lambda p: (m, 0, 0)),
            block(TGT_LEN),
            block(TGT_LEN),
            pl.BlockSpec((1, 8, TGT_LEN), lambda p: (m * PAIRS + p, 0, 0)),
        ],
        out_specs=[
            pl.BlockSpec((TGT_LEN, LANES), lambda p: (0, p)),
            pl.BlockSpec((2, OWN, LANES), lambda p: (0, 0, p)),
            pl.BlockSpec((2, NEXT, LANES), lambda p: (0, 0, p)),
        ],
        out_shape=[
            shape(TGT_LEN, D),
            jax.ShapeDtypeStruct((2, OWN, D), BF),
            jax.ShapeDtypeStruct((2, NEXT, D), BF),
        ],
        scratch_shapes=[pltpu.VMEM((KEYS, 2 * LANES), BF)] * 2,
        compiler_params=params(),
        cost_estimate=cost(22),
        name="cross_backward",
    )(*map(far, (q, kv_own, kv_next, kv_own, kv_next, mask, o, d_o, lse)))


def swapped(spec):
    index = spec.index_map
    return pl.BlockSpec(spec.block_shape, lambda p, m: index(m, p))


TILE_BLOCK = pl.BlockSpec((2, 2, HALF, HALF), lambda p, m: (p, 0, 0, 0))


def self_forward(qkv, tiles):
    return pl.pallas_call(
        self_forward_kernel,
        grid=(PAIRS, MICRO),
        in_specs=[
            swapped(pair_block(TGT_LEN)),
            swapped(pair_block(TGT_LEN, PAIRS)),
            swapped(pair_block(TGT_LEN, 2 * PAIRS)),
            TILE_BLOCK,
        ],
        out_specs=[swapped(pair_block(TGT_LEN)), swapped(LSE_BLOCK)],
        out_shape=[jax.ShapeDtypeStruct((ROWS, D), BF), LSE_SHAPE],
        compiler_params=params(),
        cost_estimate=cost(17),
        name="self_forward",
    )(qkv, qkv, qkv, tiles)


def self_backward(qkv, tiles, o, d_o, lse):
    sums = jax.ShapeDtypeStruct((HEADS, 8, HALF), F32)
    return pl.pallas_call(
        self_backward_kernel,
        grid=(PAIRS, MICRO),
        in_specs=[
            swapped(pair_block(TGT_LEN)),
            swapped(pair_block(TGT_LEN, PAIRS)),
            swapped(pair_block(TGT_LEN, 2 * PAIRS)),
            TILE_BLOCK,
            swapped(pair_block(TGT_LEN)),
            swapped(pair_block(TGT_LEN)),
            swapped(LSE_BLOCK),
        ],
        out_specs=[
            pl.BlockSpec((3, TGT_LEN, LANES), lambda p, m: (0, m, p)),
            pl.BlockSpec((2, 8, HALF), lambda p, m: (p, 0, 0)),
        ],
        out_shape=[jax.ShapeDtypeStruct((3, ROWS, D), BF), sums],
        scratch_shapes=[pltpu.VMEM((TGT_LEN, 2 * LANES), BF)] * 2
        + [pltpu.VMEM((2, HALF, HALF), F32)] * 2,
        compiler_params=params(),
        cost_estimate=cost(24),
        name="self_backward",
    )(qkv, qkv, qkv, tiles, o, d_o, lse)


def key_masks(offsets_row, position):
    shard_ids = jnp.arange(offsets_row.shape[0], dtype=jnp.int32)
    own_start = jnp.sum(jnp.where(shard_ids == position, offsets_row, 0))
    next_start = jnp.sum(jnp.where(shard_ids == position + 1, offsets_row, 0))
    own_valid = jnp.arange(MEM_DEV - OWN, MEM_DEV, dtype=jnp.int32) >= own_start
    next_valid = jnp.arange(NEXT, dtype=jnp.int32) < next_start
    valid = jnp.concatenate([own_valid, next_valid])[:, None]
    lane = jnp.arange(LANES, dtype=jnp.int32)[None, :]
    return jnp.where((lane == 0), jnp.where(valid, 0.0, MASKED), 1.0).astype(BF)


def passed_along(block, distance):
    devices = range(lax.axis_size("seq"))
    route = [(i - distance, i) for i in devices if i - distance in devices]
    return lax.ppermute(block, "seq", route)


def device_bits():
    bits = []
    for axis in AXES:
        count = lax.axis_size(axis).bit_length() - 1
        bits += [(axis, place) for place in reversed(range(count))]
    return bits


def bit_groups():
    bits = device_bits()
    core = ("dp", 0)
    low = (lax.axis_size("seq").bit_length() - 1) // 2
    plane = [b for b in bits if b != core and (b[0] == "dp" or b[1] < low)]
    column = [b for b in bits if b[0] == "seq" and b[1] >= low]
    return [core], plane, column


def mine(bit):
    axis, place = bit
    return (lax.axis_index(axis) >> place) & 1


def flips(group):
    for mask in range(1, 1 << len(group)):
        yield [(mask >> place) & 1 for place in range(len(group))]


def exchange(block, group, flip):
    mask = 0
    for (axis, place), turned in zip(group, flip):
        stride = lax.axis_size("seq") if axis == "dp" else 1
        mask ^= turned * stride << place
    count = lax.axis_size("dp") * lax.axis_size("seq")
    return lax.ppermute(block, AXES, [(i, i ^ mask) for i in range(count)])


def gather_stage(held, dims, group, fillers=()):
    order = device_bits()
    joined = sorted(dims + group, key=order.index)
    tail = held.shape[len(dims) :]
    spot = tuple(1 if bit in group else 2 for bit in joined) + tail
    turns = [[0] * len(group)] + list(flips(group))
    pieces = [held] + [exchange(held, group, flip) for flip in turns[1:]]
    pieces, fillers = tied(pieces, fillers)
    if len(group) == 2 and joined[0] == group[0] and joined[-1] == group[1] and tail[0] % 8 == 0:
        place = jnp.stack([mine(bit) for bit in group]).astype(jnp.int32)
        order = [turns.index([first, last]) for first in range(2) for last in range(2)]
        flat = [pieces[turn].reshape((-1,) + tail) for turn in order]
        return assembled(place, flat).reshape((2,) * len(joined) + tail), joined, fillers
    result = jnp.zeros((2,) * len(joined) + tail, held.dtype)
    for flip, piece in zip(turns, pieces):
        start = [mine(bit) ^ flip[group.index(bit)] if bit in group else 0 for bit in joined]
        result = lax.dynamic_update_slice(result, piece.reshape(spot), start + [0] * len(tail))
    return result, joined, fillers


def paired_halves(shard, core):
    halves = shard.reshape(shard.shape[0], 2, -1)
    here = lax.dynamic_index_in_dim(halves, core, 1, keepdims=False)
    there = lax.dynamic_index_in_dim(halves, 1 - core, 1, keepdims=False)
    return swapped_halves(here, there, core)


def swapped_halves(here, there, core):
    received = exchange(there, bit_groups()[0], [1])
    return jnp.stack([jnp.where(core == 0, here, received), jnp.where(core == 0, received, here)])


def both_halves(held):
    own = held.reshape(-1, held.shape[-1])
    return own, exchange(own, bit_groups()[0], [1])


def gather_bits(held, dims, group):
    for bit in reversed(group):
        held, dims, _ = gather_stage(held, dims, [bit])
    return held, dims, ()


def tree_sum(terms):
    terms = [term.astype(F32) for term in terms]
    while len(terms) > 1:
        terms = [
            terms[place] + terms[place + 1] if place + 1 < len(terms) else terms[place]
            for place in range(0, len(terms), 2)
        ]
    return terms[0]


def picked(array, dims, group, flip):
    left = list(dims)
    for bit, turned in zip(group, flip):
        place = left.index(bit)
        left.remove(bit)
        array = lax.dynamic_index_in_dim(array, mine(bit) ^ turned, place, keepdims=False)
    return array


def scatter_parts(bundles, dims, group):
    def part(flip):
        sums = [
            tree_sum([picked(term, dims, group, flip) for term in terms]).astype(BF)
            for terms in bundles
        ]
        return jnp.concatenate(sums, axis=-1) if len(sums) > 1 else sums[0]

    return [part([0] * len(group))] + [part(flip) for flip in flips(group)]


def scattered(parts, group):
    sent = [exchange(part, group, flip) for part, flip in zip(parts[1:], flips(group))]
    return parts[:1] + sent


def core_stage(give, keep):
    core, _, _ = bit_groups()
    dims = [bit for bit in device_bits() if bit not in core]
    received = exchange(give, core, [1])
    split = (2,) * len(dims) + (give.shape[0] * give.shape[1] >> len(dims), give.shape[2])
    return [keep.reshape(split), received.reshape(split)]


def without(dims, group):
    return [bit for bit in dims if bit not in group]


def passed_along(block, distance):
    devices = range(lax.axis_size("seq"))
    route = [(i - distance, i) for i in devices if i - distance in devices]
    return lax.ppermute(block, "seq", route)


def ffn_grads(h3, acts, dy, later):
    devices = lax.axis_size("dp") * lax.axis_size("seq")
    width = acts.shape[2]
    if D // devices % 8 or width // devices % 16:
        total = [
            lax.psum_scatter(
                lax.dot_general(
                    rows, grads, (((0,), (0,)), ((), ())), preferred_element_type=F32
                ),
                AXES,
                scatter_dimension=0,
                tiled=True,
            )
            for rows, grads in ((h3, acts[0]), (h3, acts[1]), (acts[2], dy))
        ]
        return total, later
    partial = ffn_weight_grads(h3, acts, dy, devices)
    later, partial = tied(later, partial)
    return lax.psum_scatter(partial, AXES, scatter_dimension=0, tiled=True), later


def ffn_columns(total, share, width):
    if isinstance(total, (list, tuple)):
        return total
    total = total[0].astype(F32)
    rows = share * width // WIDE

    def columns(first, height):
        block = total[first : first + rows].reshape(-1, height, WIDE)
        return block.transpose(1, 0, 2).reshape(height, -1)

    return columns(0, share), columns(rows, share), columns(2 * rows, rows * WIDE // D)


def tied(values, parts):
    values, parts = lax.optimization_barrier((values, parts))
    return values, parts


def local(
    decoder_in,
    memory,
    doc_offsets,
    self_query,
    self_key,
    self_value,
    self_out,
    cross_query,
    cross_key,
    cross_value,
    cross_out,
    ffn_gate,
    ffn_up,
    ffn_down,
    norm_self,
    norm_cross,
    norm_ffn,
    bias_table,
    cotangent,
):
    position = lax.axis_index("seq")
    core = lax.axis_index("dp") & 1
    core_id = core.reshape(1).astype(jnp.int32)
    across = lax.axis_size("dp") // 2
    share = self_query.shape[0]
    core_bits, plane, column = bit_groups()

    gains = jnp.stack([norm_self, norm_cross, norm_ffn], axis=1)
    gains = jnp.pad(gains, ((0, 0), (0, 2 * LANES - 3)))
    first = packed(
        core_id, [cross_key, cross_value, self_query, self_key, self_value, gains]
    )
    second = jnp.concatenate([self_out, cross_query], axis=1)
    late = jnp.concatenate([cross_out, ffn_gate, ffn_up], axis=1)
    first = swapped_halves(*first, core)
    first, dims, _ = gather_stage(first, core_bits, column)
    first, second, ffn_down, doc_offsets, memory, bias_table = lax.optimization_barrier(
        (first, second, ffn_down, doc_offsets, memory, bias_table)
    )
    second = paired_halves(second, core)
    third = paired_halves(ffn_down, core)
    tiles = bias_tiles(bias_table.astype(F32))
    mask = jnp.stack([key_masks(doc_offsets[m, 0], position) for m in range(MICRO)])
    next_rows = memory[:, 0, :NEXT]
    narrow = second.reshape(2, 2 * share, -1)
    second, _, _ = gather_bits(jnp.concatenate([narrow, third], axis=1), core_bits, column)
    first, _, (second, tiles, mask, next_rows, late) = gather_stage(
        first, dims, plane, (second, tiles, mask, next_rows, late)
    )
    third = second[..., 2 * share :, :]
    second = second[..., : 2 * share, :].reshape(third.shape[:-2] + (share, D))
    own, other = both_halves(first)
    late = lax.all_gather(late, AXES, axis=0, tiled=True)
    x = decoder_in.reshape(ROWS, D)
    dy = cotangent.reshape(ROWS, D)
    mem = memory.reshape(MICRO * MEM_DEV, D)
    next_rows = passed_along(next_rows, -1).reshape(MICRO * NEXT, D)

    x, second = tied(x, second)
    h1, qkv, gains = self_inputs(core_id, own, other, x)
    o1, lse1 = self_forward(qkv, tiles)
    mem, o1 = tied(mem, o1)
    kv_own, own_size = key_value(
        core_id, own, other, mem, MICRO * OWN // BLOCK, lambda i: (i + i // 3 + 1, 0), 6
    )
    second, _, (o1, kv_own, next_rows) = gather_stage(
        second, dims, plane, (o1, kv_own, next_rows)
    )
    own_b, other_b = both_halves(second)
    next_rows, third, own_b = lax.optimization_barrier((next_rows, third, own_b))
    kv_next, next_size = key_value(
        core_id, own, other, next_rows, MICRO * NEXT // BLOCK, lambda i: (i, 0), 4
    )
    o1, kv_next = tied(o1, kv_next)
    x1, h2, q2, query_size = cross_inputs(core_id, own_b, other_b, gains, x, o1)
    largest = jnp.max(query_size[:1] * jnp.maximum(own_size[:1], next_size[:1]))
    small = (largest <= SMALL_SCORE**2).astype(jnp.int32).reshape(1)
    o2, lse2 = cross_forward(small, q2, kv_own, kv_next, mask)
    third, _, o2 = gather_stage(third, dims, plane, o2)
    own_c, other_c = both_halves(third)
    out, h3, acts, db2, dx2, do2, g_norm_ffn = ffn(
        core_id, late, own_c, other_c, gains, x1, o2, dy
    )
    ffn_total, do2 = ffn_grads(h3, acts, dy, do2)
    dims = without(device_bits(), core_bits)
    arguments = (q2, kv_own, kv_next, mask, o2, do2, lse2)
    results, arrived = [], []
    for m in range(MICRO):
        dq_m, own_m, next_m = cross_backward(m, *arguments)
        dm_m = memory_grads(core_id, own, other, next_m)
        if m + 1 < MICRO:
            arguments, dm_m = tied(arguments, dm_m)
        results.append((dq_m, own_m, next_m))
        if arrived:
            dm_m, arrived[-1] = tied(dm_m, arrived[-1])
        arrived.append(passed_along(dm_m, 1))
    dq2, dkv_own, dkv_next = zip(*results)
    dkv_own, dkv_next, dm_m = lax.optimization_barrier((dkv_own, dkv_next, dm_m))
    pair_terms = core_stage(*pair_grads(core_id, [(o2, (db2,)), (h2, dq2)], across))
    give, keep = memory_weight_grads(core_id, memory, next_rows, dkv_own, dkv_next, across)
    dq2, give = tied(dq2, give)
    memory_terms = core_stage(give, keep)
    dx1, db1, do1, g_norm_cross = self_grads(core_id, own_b, other_b, gains, x1, dx2, dq2)
    (db1, do1), pair_terms, memory_terms = lax.optimization_barrier(
        ((db1, do1), pair_terms, memory_terms)
    )
    out_terms = core_stage(*pair_grads(core_id, [(o1, (db1,))], across))
    cross_parts = scatter_parts([pair_terms, memory_terms, out_terms], dims, plane)
    do1, cross_parts = tied(do1, cross_parts)
    cross_terms = scattered(cross_parts, plane)
    dqkv, sums = self_backward(qkv, tiles, o1, do1, lse1)
    dqkv, arrived[-1] = tied(dqkv, arrived[-1])
    give, keep = row_grads(core_id, h1, dqkv, across, 5)
    dqkv, give, cross_terms = lax.optimization_barrier((dqkv, give, cross_terms))
    self_terms = core_stage(give, keep)
    left = without(dims, plane)
    high, low = column[:1], column[1:]
    cross_parts = scatter_parts([cross_terms], left, high)
    dqkv, cross_parts = tied(dqkv, cross_parts)
    cross_terms = scattered(cross_parts, high)
    grad_decoder, g_norm_self = input_grads(core_id, own, other, gains, x, dx1, dqkv)
    g_norm_self, self_terms = tied(g_norm_self, self_terms)
    self_parts = scatter_parts([self_terms], dims, plane)
    give, keep = extras(core_id, sums, [g_norm_self, g_norm_cross, g_norm_ffn], across, share)
    dkv_own, self_parts, give = lax.optimization_barrier((dkv_own, self_parts, give))
    self_terms = scattered(self_parts, plane)
    extra_terms = core_stage(give, keep)
    totals = [memory_total(core_id, own, other, dkv_own[0], arrived[0])]
    totals[0], extra_terms, cross_terms = lax.optimization_barrier(
        (totals[0], extra_terms, cross_terms)
    )
    cross_parts = scatter_parts([cross_terms], low, low)
    dkv_own, cross_parts = tied(dkv_own, cross_parts)
    cross_terms = scattered(cross_parts, low)
    extra_left = list(dims)
    for bit in plane:
        extra_parts = scatter_parts([extra_terms], extra_left, [bit])
        extra_left.remove(bit)
        if len(totals) == 1:
            dkv_own, extra_parts = tied(dkv_own, extra_parts)
        extra_terms = scattered(extra_parts, [bit])
        if len(totals) == 1:
            totals.append(memory_total(core_id, own, other, dkv_own[1], arrived[1]))
            totals[1], extra_terms = tied(totals[1], extra_terms)
    totals, self_terms, extra_terms = lax.optimization_barrier((totals, self_terms, extra_terms))
    self_parts = scatter_parts([self_terms, extra_terms], left, column)
    self_parts, cross_terms, ffn_total = lax.optimization_barrier(
        (self_parts, cross_terms, ffn_total)
    )
    g_self = tree_sum(scattered(self_parts, column))
    g_cross = tree_sum(cross_terms)
    grad_memory = jnp.stack(totals)
    g_gate, g_up, g_down = ffn_columns(ffn_total, share, ffn_gate.shape[1])

    table = g_self[: HEADS * BUCKETS // LANES, 3 * D + LANES :].reshape(HEADS, BUCKETS)

    def cut(stack, index):
        return stack[:, index * D : (index + 1) * D]

    return (
        out.reshape(decoder_in.shape),
        grad_decoder.reshape(decoder_in.shape),
        grad_memory.reshape(memory.shape),
        cut(g_self, 0),
        cut(g_self, 1),
        cut(g_self, 2),
        cut(g_cross, 4),
        cut(g_cross, 1),
        cut(g_cross, 2),
        cut(g_cross, 3),
        cut(g_cross, 0),
        g_gate,
        g_up,
        g_down,
        g_self[:, 3 * D],
        g_self[:, 3 * D + 1],
        g_self[:, 3 * D + 2],
        table,
    )


def solution(mesh):
    in_specs = (
        P(None, ("dp", "seq"), None, None),
        P(None, ("dp", "seq"), None, None),
        P(None, "dp", None),
        P(("dp", "seq"), None),
        P(("dp", "seq"), None),
        P(("dp", "seq"), None),
        P(("dp", "seq"), None),
        P(("dp", "seq"), None),
        P(("dp", "seq"), None),
        P(("dp", "seq"), None),
        P(("dp", "seq"), None),
        P(("dp", "seq"), None),
        P(("dp", "seq"), None),
        P(("dp", "seq"), None),
        P(("dp", "seq")),
        P(("dp", "seq")),
        P(("dp", "seq")),
        P(),
        P(None, ("dp", "seq"), None, None),
    )
    out_specs = (
        P(None, ("dp", "seq"), None, None),
        P(None, ("dp", "seq"), None, None),
        P(None, ("dp", "seq"), None, None),
        P(("dp", "seq"), None),
        P(("dp", "seq"), None),
        P(("dp", "seq"), None),
        P(("dp", "seq"), None),
        P(("dp", "seq"), None),
        P(("dp", "seq"), None),
        P(("dp", "seq"), None),
        P(("dp", "seq"), None),
        P(("dp", "seq"), None),
        P(("dp", "seq"), None),
        P(("dp", "seq"), None),
        P(("dp", "seq")),
        P(("dp", "seq")),
        P(("dp", "seq")),
        P(),
    )
    return jax.shard_map(local, mesh=mesh, in_specs=in_specs, out_specs=out_specs, check_vma=False)
```
